32 devices in a mesh: groups: 2 (over y), lat: 16 (over z, x, core).
Axes of the slice: x: 2, y: 2, z: 4, core: 2. Of those that a mesh axis runs over, the one named last changes fastest.
Arguments:
- grad_recon: bfloat16 [4096, 3584], P(('groups', 'lat')), parts along dimension 0, may hold values from -6 to 6
- inputs: bfloat16 [4096, 3584], P(('groups', 'lat')), parts along dimension 0, may hold values from -6 to 6
- decoder: bfloat16 [4096, 3584], P('lat'), may hold values from -0.09375 to 0.09375
- owners: int32 [4096, 4], P(('groups', 'lat')), parts along dimension 0, may hold values from 0 to 15, all different within a row; in each aligned block of 128 rows (0 to 127, 128 to 255, ...) at most 48 rows name the same one
- local_blocks: int32 [4096, 4], P(('groups', 'lat')), parts along dimension 0, may hold values from 0 to 1
- offsets: int32 [4096, 4, 16], P(('groups', 'lat')), parts along dimension 0, may hold values from 0 to 127, as said below
- act_values: bfloat16 [4096, 4, 16], P(('groups', 'lat')), parts along dimension 0, may hold values from 0.049804688 to 3
Outputs:
- decoder_grad: bfloat16 [8192, 3584], P(('groups', 'lat')), parts along dimension 0
- encoder_grad: bfloat16 [3584, 8192], P(None, ('groups', 'lat')), parts along dimension 1
- bias_grad: float32 [8192], P(('groups', 'lat')), parts along dimension 0
- latent_grads: float32 [4096, 64], P(('groups', 'lat')), parts along dimension 0
The draws below stay inside these ranges and needn't reach their ends.
There are 2 independent parts, one for each index of `groups`. The reference program is written for one: setup_inputs(seed, part) draws one part's arguments, and reference() takes and returns one part's arrays. A program takes and returns all parts, laid end to end along the dimension named above; an argument that names none is the same for every part. Nothing has to cross between parts.
Inputs may be any that keep to these rules, and one draw needn't show every extreme that they name: The 4 owners of one row are different; in the rows of one device no owner is named by more than 48 rows, a bound that some block reaches. The 16 offsets of one row and block are different.
All inputs are finite; a program needn't handle non-finite values.
Results may differ from the reference program's by a relative error of at most 0.005.
Values may be sent and summed in bfloat16 or wider, within the bound.
No kernel may reach another device: no remote copies, remote signals or barrier semaphores. Data moves between devices by JAX's collectives and lax.ppermute only.
A program may use at most 128 MiB of HBM per device.

```python
import math
import jax
import jax.numpy as jnp
import numpy as np
from jax import lax

D = 3584
BLOCK = 128
K = 64
NB = 4
TOK_DEV = 128
BLK_DEV = 2
KB = 16
ROWS = 2048
LATENTS = 4096
CAP = 48
N_LAT = 16


def draw_offsets(key, part):
    key = jax.random.fold_in(key, 7)
    keys = jax.random.split(key, ROWS * NB)
    chosen = jax.vmap(lambda single: jax.random.permutation(single, BLOCK)[:KB])(keys)
    return chosen.reshape(ROWS, NB, KB).astype(jnp.int32)


def plant(entries, key, low, top_value):
    longest = entries.shape.index(max(entries.shape))
    spots = []
    for shift in (0, 1):
        where = [jax.random.randint(jax.random.fold_in(key, axis), (), 0, length) for axis, length in enumerate(entries.shape)]
        where[longest] = (where[longest] + shift) % entries.shape[longest]
        spots.append(tuple(where))
    return entries.at[spots[0]].set(low).at[spots[1]].set(top_value)


def level_of(stream_key, shape, cuts, low, top_value):
    level = 1.0
    for dim, parts in cuts:
        heights = jax.random.uniform(jax.random.fold_in(jax.random.fold_in(stream_key, 6), dim), (parts,), jnp.float32, low / len(cuts), top_value / len(cuts))
        level = level * jnp.repeat(jnp.exp(heights), shape[dim] // parts).reshape((-1,) + (1,) * (len(shape) - 1 - dim))
    return level


def shared_out(rng, own, number, rows, amount, top, bound, slope):
    order = jax.random.permutation(rng, amount)
    crowded, ordinary = load_shares(amount, rows * top, bound, slope, True), load_shares(amount, rows * top, bound, slope, False)
    places = jnp.arange(amount)

    def named(sizes, turn):
        used = int((sizes > 0).sum())
        fixed = max(1, used // 4)
        passed = fixed + (places - fixed + turn * (used - fixed)) % max(1, amount - fixed)
        return jnp.zeros((amount,), jnp.int32).at[order[jnp.where(places < fixed, places, passed)]].set(jnp.asarray(sizes, jnp.int32))

    sizes = jnp.where(number % 4 == 0, named(crowded, number // 4), named(ordinary, number - number // 4 - 1))
    mixed = jax.random.permutation(jax.random.fold_in(own, 3), amount)
    giver, taker = mixed[0:amount // 2 * 2:2], mixed[1:amount // 2 * 2:2]
    slack = jnp.minimum(sizes[giver] - 1, bound - sizes[taker]) // 2
    slack = jnp.where((giver == order[0]) | (taker == order[0]) | (sizes[taker] == 0), 0, jnp.maximum(slack, 0))
    passed = jax.random.randint(jax.random.fold_in(own, 4), (amount // 2,), 0, 1 << 20) % (slack + 1)
    sizes = sizes.at[giver].add(-passed).at[taker].add(passed)
    items = jnp.searchsorted(jnp.cumsum(sizes), jnp.arange(rows * top), side="right").astype(jnp.int32)
    table = items.reshape(top, rows).T
    table = table[jax.random.permutation(jax.random.fold_in(own, 1), rows)]
    turn = jax.random.randint(jax.random.fold_in(own, 2), (rows, 1), 0, top)
    return jnp.take_along_axis(table, (jnp.arange(top)[None, :] + turn) % top, axis=1)


def load_shares(amount, total, bound, lean, full):
    weights = [(1 << 20) // math.isqrt(rank ** lean) + 1 for rank in range(1, amount + 1)]
    largest = bound if full else min(bound, max(-(-total // amount), total * weights[0] // sum(weights)))
    least = 1 if total - largest >= amount - 1 else 0
    counts, surplus = [largest] + [least] * (amount - 1), total - largest - least * (amount - 1)
    while surplus > 0:
        candidates = [i for i in range(1, amount) if counts[i] < largest] or [i for i in range(1, amount) if counts[i] < bound]
        mass, budget = sum([weights[i] for i in candidates]), surplus
        for i in candidates:
            addition = min(bound - counts[i], max(1, budget * weights[i] // mass), surplus)
            counts[i] = counts[i] + addition
            surplus = surplus - addition
    return np.array(counts)


def centred(rng, shape, deviation, bound, cuts=(), dtype=jnp.bfloat16):
    factor_of = level_of(rng, shape, cuts, -0.22, 0.18) if cuts else 1.0
    entries = jax.random.normal(rng, shape, jnp.float32) * deviation * factor_of
    return jnp.minimum(jnp.maximum(entries, -bound), bound).astype(dtype)


def setup_inputs(seed: int = 0, part: int = 0) -> dict:
    key_list = jax.random.split(jax.random.key(seed), 8)
    own_keys = jax.random.split(jax.random.fold_in(key_list[7], part), 8)
    grad_recon = centred(own_keys[0], (ROWS, D), 1.0, 6.0, ((0, 16),))
    inputs = centred(own_keys[1], (ROWS, D), 1.0, 6.0, ((0, 16),))
    decoder = centred(key_list[2], (LATENTS, D), D ** -0.5, 0.09375, ((0, 16),))
    owners_keys = jax.random.split(jax.random.fold_in(own_keys[3], 1), ROWS // TOK_DEV)
    owners_turns = jax.random.permutation(jax.random.fold_in(own_keys[3], 3), ROWS // TOK_DEV)
    owners = jax.vmap(lambda own, number: shared_out(jax.random.fold_in(own_keys[3], 2), own, number, TOK_DEV, N_LAT, NB, CAP, 2))(owners_keys, owners_turns).reshape((ROWS, NB))
    local_blocks = plant(jax.random.randint(own_keys[4], (ROWS, NB), 0, BLK_DEV), jax.random.fold_in(own_keys[4], 1), 0, BLK_DEV - 1).astype(jnp.int32)
    offsets = draw_offsets(jax.random.fold_in(jax.random.fold_in(key_list[7], part), 71), part)
    act_values = jnp.clip(jnp.exp(math.log(3.0) - 4.0982585 * jax.random.uniform(own_keys[6], (ROWS, NB, KB), jnp.float32) ** level_of(own_keys[6], (ROWS, NB, KB), ((0, 16),), -0.2, 0.2)), 0.049804688, 3.0).astype(jnp.bfloat16)
    return dict(grad_recon=grad_recon, inputs=inputs, decoder=decoder, owners=owners, local_blocks=local_blocks, offsets=offsets, act_values=act_values)


def reference(grad_recon, inputs, decoder, owners, local_blocks, offsets, act_values):
    latent_ids = ((owners * BLK_DEV + local_blocks)[:, :, None] * BLOCK + offsets).astype(jnp.int32)
    block_rows = min(ROWS, 256)
    steps_count = ROWS // block_rows
    ids_blocks = latent_ids.reshape(steps_count, block_rows, K)
    act_blocks = act_values.reshape(steps_count, block_rows, K)
    grad_blocks = grad_recon.reshape(steps_count, block_rows, D)
    input_blocks = inputs.reshape(steps_count, block_rows, D)

    def one_block(carry, pieces):
        dec_acc, enc_acc, bias_acc = carry
        ids_piece, act_piece, grad_piece, input_piece = pieces
        flat_ids = ids_piece.reshape(-1)
        rows_taken = decoder[flat_ids].reshape(block_rows, K, D)
        grads_here = jnp.einsum("td,tkd->tk", grad_piece.astype(jnp.float32), rows_taken.astype(jnp.float32))
        dec_terms = act_piece.astype(jnp.float32)[:, :, None] * grad_piece.astype(jnp.float32)[:, None, :]
        dec_acc = dec_acc.at[flat_ids].add(dec_terms.reshape(-1, D))
        rounded = grads_here.astype(jnp.bfloat16).astype(jnp.float32)
        enc_terms = rounded[:, :, None] * input_piece.astype(jnp.float32)[:, None, :]
        enc_acc = enc_acc.at[flat_ids].add(enc_terms.reshape(-1, D))
        bias_acc = bias_acc.at[flat_ids].add(grads_here.reshape(-1))
        return (dec_acc, enc_acc, bias_acc), grads_here

    start = (jnp.zeros((LATENTS, D), jnp.float32), jnp.zeros((LATENTS, D), jnp.float32), jnp.zeros((LATENTS,), jnp.float32))
    (dec_acc, enc_acc, bias_acc), grads_all = lax.scan(one_block, start, (ids_blocks, act_blocks, grad_blocks, input_blocks))
    decoder_grad = dec_acc.astype(jnp.bfloat16)
    encoder_grad = enc_acc.T.astype(jnp.bfloat16)
    latent_grads = grads_all.reshape(ROWS, K)
    return decoder_grad, encoder_grad, bias_acc, latent_grads
```

```python
import functools

import jax
import jax.numpy as jnp
from jax import lax
from jax.experimental import pallas as pl
from jax.experimental.pallas import tpu as pltpu
from jax.sharding import PartitionSpec as P

BLOCK = 128
PART_BYTES = 9 << 20
HELD_BYTES = 1 << 25


def build_kernel(block_count, per_block, me_ref, meta_ref, acts_ref, cols_ref):
    pairs = block_count * per_block
    meta = meta_ref[0].astype(jnp.float32)
    me = me_ref[0].astype(jnp.float32)
    tokens = meta.shape[1]
    values = jnp.zeros((per_block, tokens), jnp.float32)
    columns = jnp.full((per_block, tokens), -1.0, jnp.float32)
    for i in range(block_count):
        mine = meta[2 * pairs + i : 2 * pairs + i + 1] == me
        values = jnp.where(mine, meta[i * per_block : (i + 1) * per_block], values)
        columns = jnp.where(mine, meta[pairs + i * per_block : pairs + (i + 1) * per_block], columns)
    columns = columns.astype(jnp.int32)
    cols_ref[0] = columns
    row = lax.broadcasted_iota(jnp.int32, (acts_ref.shape[0], tokens), 0)
    dense = jnp.zeros(row.shape, jnp.float32)
    for k in range(per_block):
        dense = jnp.where(row == columns[k : k + 1], values[k : k + 1], dense)
    acts_ref[...] = dense.astype(jnp.bfloat16)


def mask_kernel(per_block, products_ref, cols_ref, pre_ref, lat_ref, bias_ref):
    products = products_ref[...]
    columns = cols_ref[0]
    row = lax.broadcasted_iota(jnp.int32, products.shape, 0)
    kept = jnp.zeros(products.shape, jnp.float32)
    for k in range(per_block):
        hit = row == columns[k : k + 1]
        picked = jnp.where(hit, products, 0.0)
        lat_ref[0, k : k + 1, :] = jnp.sum(picked, axis=0, keepdims=True)
        kept = kept + picked
    pre_ref[...] = kept.astype(jnp.bfloat16)

    @pl.when(pl.program_id(0) == 0)
    def _():
        bias_ref[...] = jnp.zeros_like(bias_ref)

    bias_ref[...] += kept


def column_parts(width, least, row_count):
    lanes = width // BLOCK
    for parts in range(least, lanes + 1):
        if lanes % parts == 0 and row_count * (width // parts) * 2 <= PART_BYTES:
            return parts
    return lanes


def per_device(grad_recon, inputs, decoder, owners, local_blocks, offsets, act_values):
    token_count, width = grad_recon.shape
    block_count = owners.shape[1]
    per_block = offsets.shape[2]
    latent_count = decoder.shape[0]
    peer_count = lax.axis_size("lat")
    pairs = block_count * per_block
    row_count = peer_count * token_count
    me = lax.axis_index("lat").astype(jnp.int32).reshape(1)

    own_t = owners.T
    columns_t = (local_blocks.T[:, None, :] * BLOCK + offsets.transpose(1, 2, 0)).reshape(pairs, token_count)
    acts_t = act_values.transpose(1, 2, 0).reshape(pairs, token_count)
    filler = jnp.zeros((-block_count % 16, token_count), jnp.bfloat16)
    meta = jnp.concatenate([acts_t, columns_t.astype(jnp.bfloat16), own_t.astype(jnp.bfloat16), filler], axis=0)
    meta_all = lax.all_gather(meta, "lat", axis=0)

    parts = column_parts(width, 2, row_count)
    span = width // parts
    depth = max(1, HELD_BYTES // (row_count * span * 2))

    def gathered(rows, p, done):
        piece = rows[:, p * span : (p + 1) * span]
        if len(done) >= depth:
            piece, _ = lax.optimization_barrier((piece, done[-depth]))
        return lax.all_gather(piece, "lat", axis=0, tiled=True)

    acts_dense, cols = pl.pallas_call(
        functools.partial(build_kernel, block_count, per_block),
        grid=(peer_count,),
        in_specs=[
            pl.BlockSpec(memory_space=pltpu.SMEM),
            pl.BlockSpec((1, meta.shape[0], token_count), lambda s: (s, 0, 0)),
        ],
        out_specs=[
            pl.BlockSpec((latent_count, token_count), lambda s: (0, s)),
            pl.BlockSpec((1, per_block, token_count), lambda s: (s, 0, 0)),
        ],
        out_shape=[
            jax.ShapeDtypeStruct((latent_count, row_count), jnp.bfloat16),
            jax.ShapeDtypeStruct((peer_count, per_block, token_count), jnp.int32),
        ],
        cost_estimate=pl.CostEstimate(flops=latent_count * row_count * 48, bytes_accessed=row_count * latent_count * 2, transcendentals=0),
    )(me, meta_all)

    products = None
    decoder_parts = []
    for p in range(parts):
        rows = gathered(grad_recon, p, decoder_parts)
        part = lax.dot_general(acts_dense, rows, (((1,), (0,)), ((), ())), preferred_element_type=jnp.float32).astype(jnp.bfloat16)
        term = lax.dot_general(
            decoder[:, p * span : (p + 1) * span], rows, (((1,), (1,)), ((), ())), preferred_element_type=jnp.float32
        )
        products = term if products is None else products + term
        if depth < 2 * parts:
            part, products = lax.optimization_barrier((part, products))
        decoder_parts.append(part)
    decoder_grad = jnp.concatenate(decoder_parts, axis=1)

    pre_grads, lat, bias_lanes = pl.pallas_call(
        functools.partial(mask_kernel, per_block),
        grid=(peer_count,),
        in_specs=[
            pl.BlockSpec((latent_count, token_count), lambda s: (0, s)),
            pl.BlockSpec((1, per_block, token_count), lambda s: (s, 0, 0)),
        ],
        out_specs=[
            pl.BlockSpec((latent_count, token_count), lambda s: (0, s)),
            pl.BlockSpec((1, per_block, token_count), lambda s: (s, 0, 0)),
            pl.BlockSpec((latent_count, token_count), lambda s: (0, 0)),
        ],
        out_shape=[
            jax.ShapeDtypeStruct((latent_count, row_count), jnp.bfloat16),
            jax.ShapeDtypeStruct((peer_count, per_block, token_count), jnp.float32),
            jax.ShapeDtypeStruct((latent_count, token_count), jnp.float32),
        ],
        cost_estimate=pl.CostEstimate(flops=latent_count * row_count * 64, bytes_accessed=row_count * latent_count * 6, transcendentals=0),
    )(products, cols)
    bias_grad = jnp.sum(bias_lanes, axis=1)

    returned = lax.all_to_all(lat, "lat", split_axis=0, concat_axis=0, tiled=True)
    owner_id = jnp.arange(peer_count, dtype=jnp.int32)[:, None, None, None]
    picked = jnp.where(own_t[None, :, None, :] == owner_id, returned[:, None, :, :], 0.0)
    latent_grads = jnp.sum(picked, axis=0).reshape(pairs, token_count).T

    encoder_parts = []
    for p in range(parts):
        rows = gathered(inputs, p, decoder_parts + encoder_parts)
        encoder_parts.append(
            lax.dot_general(rows, pre_grads, (((0,), (1,)), ((), ())), preferred_element_type=jnp.float32).astype(jnp.bfloat16)
        )
    encoder_grad = jnp.concatenate(encoder_parts, axis=0)
    return (decoder_grad, encoder_grad, bias_grad, latent_grads)


def solution(mesh):
    placed = (
        P(("groups", "lat"), None),
        P(("groups", "lat"), None),
        P("lat", None),
        P(("groups", "lat"), None),
        P(("groups", "lat"), None),
        P(("groups", "lat"), None, None),
        P(("groups", "lat"), None, None),
    )
    return jax.shard_map(
        per_device,
        mesh=mesh,
        in_specs=placed,
        out_specs=(
            P(("groups", "lat"), None),
            P(None, ("groups", "lat")),
            P(("groups", "lat")),
            P(("groups", "lat"), None),
        ),
        check_vma=False,
    )
```

```python
import functools

import jax
import jax.numpy as jnp
import numpy as np
from jax import lax
from jax.experimental import pallas as pl
from jax.experimental.pallas import tpu as pltpu
from jax.sharding import PartitionSpec as P

BLOCK = 128
PART_BYTES = 9 << 20
HELD_BYTES = 1 << 25
RING_BYTES = 1 << 26
VMEM_BYTES = 48 << 20


def ring_tables(peer_count):
    chips = peer_count // 2
    ring = [chip for chip in range(chips) if chip % 2 == 0] + [chip for chip in reversed(range(chips)) if chip % 2]
    place = {chip: spot for spot, chip in enumerate(ring)}
    sources = np.zeros((peer_count, chips, 4), np.int32)
    first_step = np.zeros((peer_count, 2, chips), np.int32)
    for device in range(peer_count):
        chip, core = divmod(device, 2)
        sign = 1 - 2 * core
        for step in range(chips):
            ahead, behind = ring[(place[chip] - sign * step) % chips], ring[(place[chip] + sign * step) % chips]
            sources[device, step] = (2 * ahead + core, 2 * ahead + 1 - core, 2 * behind + 1 - core, 2 * behind + core)
            first_step[device, 0, ahead] = step
            first_step[device, 1, behind] = step
    up = [(2 * ring[i], 2 * ring[(i + 1) % chips]) for i in range(chips)]
    down = [(2 * ring[i], 2 * ring[(i - 1) % chips]) for i in range(chips)]
    up_1, down_1 = [(a + 1, b + 1) for a, b in up], [(a + 1, b + 1) for a, b in down]
    swap = [(i, i ^ 1) for i in range(peer_count)]
    return sources, first_step, up + down_1, down + up_1, swap


def join_rows(parts, rows_ref):
    half = parts[0].shape[0]
    for i, part in enumerate(parts):
        rows_ref[i * half : (i + 1) * half, :] = part[...]


def grad_kernel(has_total, last, per_block, *refs):
    order_ref, meta_ref, decoder_ref = refs[:3]
    parts = refs[3:7]
    refs = refs[7:]
    total_ref = None
    if has_total:
        total_ref, refs = refs[0], refs[1:]
    out_ref, pre_ref, lat_ref, bias_ref, rows_ref, acts_ref = refs
    join_rows(parts, rows_ref)
    latents, width = decoder_ref.shape
    tokens = rows_ref.shape[0] // 2
    products = lax.dot_general(decoder_ref[...], rows_ref[...], (((1,), (1,)), ((), ())), preferred_element_type=jnp.float32)
    low = lax.broadcasted_iota(jnp.int32, (2 * per_block, tokens), 1) < tokens // 2
    row = lax.broadcasted_iota(jnp.int32, (latents, tokens), 0)
    bias = jnp.zeros((latents, tokens), jnp.float32)
    for tile in range(2):
        meta = jnp.where(
            low,
            meta_ref[order_ref[2 * tile]].astype(jnp.float32),
            meta_ref[order_ref[2 * tile + 1]].astype(jnp.float32),
        )
        columns = meta[:per_block].astype(jnp.int32)
        values = meta[per_block:]
        here = products[:, tile * tokens : (tile + 1) * tokens]
        kept = jnp.zeros((latents, tokens), jnp.float32)
        dense = jnp.zeros((latents, tokens), jnp.float32)
        for k in range(per_block):
            hit = row == columns[k : k + 1]
            picked = jnp.where(hit, here, 0.0)
            lat_ref[tile, k : k + 1, :] = jnp.sum(picked, axis=0, keepdims=True)
            kept = kept + picked
            dense = jnp.where(hit, values[k : k + 1], dense)
        bias = bias + kept
        pre_ref[:, tile * tokens : (tile + 1) * tokens] = kept.astype(jnp.bfloat16)
        acts_ref[:, tile * tokens : (tile + 1) * tokens] = dense.astype(jnp.bfloat16)
    bias_ref[...] = bias
    acts = acts_ref[...]
    span = 512 if width % 512 == 0 else BLOCK

    def column(i, _):
        at = pl.ds(pl.multiple_of(i * span, span), span)
        term = lax.dot_general(acts, rows_ref[:, at], (((1,), (0,)), ((), ())), preferred_element_type=jnp.float32)
        if has_total:
            term = term + total_ref[:, at]
        out_ref[:, at] = term.astype(out_ref.dtype)
        return 0

    lax.fori_loop(0, width // span, column, 0)


def input_kernel(has_total, last, *refs):
    pre_ref = refs[0]
    parts = refs[1:5]
    refs = refs[5:]
    total_ref = None
    if has_total:
        total_ref, refs = refs[0], refs[1:]
    out_ref, rows_ref = refs
    join_rows(parts, rows_ref)
    width = rows_ref.shape[1]
    pre = pre_ref[...]
    span = 512 if width % 512 == 0 else BLOCK

    def column(i, _):
        at = pl.ds(pl.multiple_of(i * span, span), span)
        term = lax.dot_general(rows_ref[:, at], pre, (((0,), (1,)), ((), ())), preferred_element_type=jnp.float32)
        if has_total:
            term = term + total_ref[at, :]
        out_ref[at, :] = term.astype(out_ref.dtype)
        return 0

    lax.fori_loop(0, width // span, column, 0)


def ring_rows(rows, down_up):
    up, down, swap, chips = down_up
    half = rows.shape[0] // 2
    low, high = rows[:half], rows[half:]
    steps = []
    for step in range(chips):
        if step:
            low = lax.ppermute(low, "lat", up)
            high = lax.ppermute(high, "lat", down)
        other_low = lax.ppermute(low, "lat", swap)
        other_high = lax.ppermute(high, "lat", swap)
        steps.append((low, other_high, other_low, high))
    return steps


def by_ring(grad_recon, inputs, decoder, owners, local_blocks, offsets, act_values):
    token_count, width = grad_recon.shape
    block_count = owners.shape[1]
    per_block = offsets.shape[2]
    latent_count = decoder.shape[0]
    peer_count = lax.axis_size("lat")
    chips = peer_count // 2
    me = lax.axis_index("lat")
    sources, first_step, up, down, swap = ring_tables(peer_count)
    order = jnp.asarray(sources)[me]
    step_of = jnp.asarray(first_step)[me]

    own_t = owners.T
    columns_t = (local_blocks.T[:, None, :] * BLOCK + offsets.transpose(1, 2, 0)).astype(jnp.float32)
    values_t = act_values.transpose(1, 2, 0).astype(jnp.float32)
    peers = jnp.arange(peer_count, dtype=jnp.int32)
    sent_columns = jnp.full((peer_count, per_block, token_count), -1.0, jnp.float32)
    sent_values = jnp.zeros((peer_count, per_block, token_count), jnp.float32)
    for i in range(block_count):
        named = own_t[i][None, None, :] == peers[:, None, None]
        sent_columns = jnp.where(named, columns_t[i][None], sent_columns)
        sent_values = jnp.where(named, values_t[i][None], sent_values)
    meta = jnp.concatenate([sent_columns, sent_values], axis=1).astype(jnp.bfloat16)
    meta = lax.all_to_all(meta, "lat", split_axis=0, concat_axis=0, tiled=True)

    grad_steps = ring_rows(grad_recon, (up, down, swap, chips))
    input_steps = ring_rows(inputs, (up, down, swap, chips))
    params = pltpu.CompilerParams(vmem_limit_bytes=VMEM_BYTES)
    whole = pl.BlockSpec(memory_space=pltpu.VMEM)
    scalars = pl.BlockSpec(memory_space=pltpu.SMEM)
    step_tokens = 2 * token_count
    work = 2 * latent_count * width * step_tokens

    total, pres, lats, biases = None, [], [], []
    for step, parts in enumerate(grad_steps):
        last = step == chips - 1
        operands = [order[step], meta, decoder, *parts] + ([] if total is None else [total])
        total, pre, lat, bias = pl.pallas_call(
            functools.partial(grad_kernel, total is not None, last, per_block),
            in_specs=[scalars] + [whole] * (len(operands) - 1),
            out_specs=[whole] * 4,
            out_shape=[
                jax.ShapeDtypeStruct((latent_count, width), jnp.bfloat16 if last else jnp.float32),
                jax.ShapeDtypeStruct((latent_count, step_tokens), jnp.bfloat16),
                jax.ShapeDtypeStruct((2, per_block, token_count), jnp.float32),
                jax.ShapeDtypeStruct((latent_count, token_count), jnp.float32),
            ],
            scratch_shapes=[
                pltpu.VMEM((step_tokens, width), jnp.bfloat16),
                pltpu.VMEM((latent_count, step_tokens), jnp.bfloat16),
            ],
            compiler_params=params,
            cost_estimate=pl.CostEstimate(flops=2 * work, bytes_accessed=12 * latent_count * width, transcendentals=0),
            name="grad_step",
        )(*operands)
        pres.append(pre)
        lats.append(lat)
        biases.append(bias)
    decoder_grad = total
    bias_grad = jnp.sum(functools.reduce(jnp.add, biases), axis=1)

    lat = jnp.stack(lats)
    ahead, behind = lat[:, 0][step_of[0]], lat[:, 1][step_of[1]]
    low = (jnp.arange(token_count) < token_count // 2)[None, None, :]
    same, other = jnp.where(low, ahead, behind), jnp.where(low, behind, ahead)
    even = me % 2 == 0
    lat = jnp.stack([jnp.where(even, same, other), jnp.where(even, other, same)], axis=1)
    returned = lax.all_to_all(
        lat.reshape(peer_count, per_block, token_count), "lat", split_axis=0, concat_axis=0, tiled=True
    )
    latent_grads = pick_returned(returned, own_t)

    total = None
    for step, parts in enumerate(input_steps):
        last = step == chips - 1
        operands = [pres[step], *parts] + ([] if total is None else [total])
        total = pl.pallas_call(
            functools.partial(input_kernel, total is not None, last),
            in_specs=[whole] * len(operands),
            out_specs=whole,
            out_shape=jax.ShapeDtypeStruct((width, latent_count), jnp.bfloat16 if last else jnp.float32),
            scratch_shapes=[pltpu.VMEM((step_tokens, width), jnp.bfloat16)],
            compiler_params=params,
            cost_estimate=pl.CostEstimate(flops=work, bytes_accessed=10 * latent_count * width, transcendentals=0),
            name="input_step",
        )(*operands)
    return (decoder_grad, total, bias_grad, latent_grads)


def pick_returned(returned, own_t):
    owner_id = jnp.arange(returned.shape[0], dtype=jnp.int32)[:, None, None, None]
    picked = jnp.where(own_t[None, :, None, :] == owner_id, returned[:, None, :, :], 0.0)
    return jnp.sum(picked, axis=0).reshape(-1, own_t.shape[1]).T


def build_kernel(block_count, per_block, me_ref, meta_ref, acts_ref, cols_ref):
    pairs = block_count * per_block
    meta = meta_ref[0].astype(jnp.float32)
    me = me_ref[0].astype(jnp.float32)
    tokens = meta.shape[1]
    values = jnp.zeros((per_block, tokens), jnp.float32)
    columns = jnp.full((per_block, tokens), -1.0, jnp.float32)
    for i in range(block_count):
        mine = meta[2 * pairs + i : 2 * pairs + i + 1] == me
        values = jnp.where(mine, meta[i * per_block : (i + 1) * per_block], values)
        columns = jnp.where(mine, meta[pairs + i * per_block : pairs + (i + 1) * per_block], columns)
    columns = columns.astype(jnp.int32)
    cols_ref[0] = columns
    row = lax.broadcasted_iota(jnp.int32, (acts_ref.shape[0], tokens), 0)
    dense = jnp.zeros(row.shape, jnp.float32)
    for k in range(per_block):
        dense = jnp.where(row == columns[k : k + 1], values[k : k + 1], dense)
    acts_ref[...] = dense.astype(jnp.bfloat16)


def mask_kernel(per_block, products_ref, cols_ref, pre_ref, lat_ref, bias_ref):
    products = products_ref[...]
    columns = cols_ref[0]
    row = lax.broadcasted_iota(jnp.int32, products.shape, 0)
    kept = jnp.zeros(products.shape, jnp.float32)
    for k in range(per_block):
        picked = jnp.where(row == columns[k : k + 1], products, 0.0)
        lat_ref[0, k : k + 1, :] = jnp.sum(picked, axis=0, keepdims=True)
        kept = kept + picked
    pre_ref[...] = kept.astype(jnp.bfloat16)

    @pl.when(pl.program_id(0) == 0)
    def _():
        bias_ref[...] = jnp.zeros_like(bias_ref)

    bias_ref[...] += kept


def column_parts(width, row_count):
    lanes = width // BLOCK
    for parts in range(2, lanes + 1):
        if lanes % parts == 0 and row_count * (width // parts) * 2 <= PART_BYTES:
            return parts
    return lanes


def by_gather(grad_recon, inputs, decoder, owners, local_blocks, offsets, act_values):
    token_count, width = grad_recon.shape
    block_count = owners.shape[1]
    per_block = offsets.shape[2]
    latent_count = decoder.shape[0]
    peer_count = lax.axis_size("lat")
    pairs = block_count * per_block
    row_count = peer_count * token_count
    me = lax.axis_index("lat").astype(jnp.int32).reshape(1)

    own_t = owners.T
    columns_t = (local_blocks.T[:, None, :] * BLOCK + offsets.transpose(1, 2, 0)).reshape(pairs, token_count)
    acts_t = act_values.transpose(1, 2, 0).reshape(pairs, token_count)
    filler = jnp.zeros((-block_count % 16, token_count), jnp.bfloat16)
    meta = jnp.concatenate([acts_t, columns_t.astype(jnp.bfloat16), own_t.astype(jnp.bfloat16), filler], axis=0)
    meta_all = lax.all_gather(meta, "lat", axis=0)

    parts = column_parts(width, row_count)
    span = width // parts
    depth = max(1, HELD_BYTES // (row_count * span * 2))

    def gathered(rows, p, done):
        piece = rows[:, p * span : (p + 1) * span]
        if len(done) >= depth:
            piece, _ = lax.optimization_barrier((piece, done[-depth]))
        return lax.all_gather(piece, "lat", axis=0, tiled=True)

    tile = pl.BlockSpec((latent_count, token_count), lambda s: (0, s))
    picks = pl.BlockSpec((1, per_block, token_count), lambda s: (s, 0, 0))
    acts_dense, cols = pl.pallas_call(
        functools.partial(build_kernel, block_count, per_block),
        grid=(peer_count,),
        in_specs=[
            pl.BlockSpec(memory_space=pltpu.SMEM),
            pl.BlockSpec((1, meta.shape[0], token_count), lambda s: (s, 0, 0)),
        ],
        out_specs=[tile, picks],
        out_shape=[
            jax.ShapeDtypeStruct((latent_count, row_count), jnp.bfloat16),
            jax.ShapeDtypeStruct((peer_count, per_block, token_count), jnp.int32),
        ],
        name="build",
    )(me, meta_all)

    products = None
    decoder_parts = []
    for p in range(parts):
        rows = gathered(grad_recon, p, decoder_parts)
        part = lax.dot_general(
            acts_dense, rows, (((1,), (0,)), ((), ())), preferred_element_type=jnp.float32
        ).astype(jnp.bfloat16)
        term = lax.dot_general(
            decoder[:, p * span : (p + 1) * span], rows, (((1,), (1,)), ((), ())), preferred_element_type=jnp.float32
        )
        products = term if products is None else products + term
        if depth < 2 * parts:
            part, products = lax.optimization_barrier((part, products))
        decoder_parts.append(part)
    decoder_grad = jnp.concatenate(decoder_parts, axis=1)

    pre_grads, lat, bias_lanes = pl.pallas_call(
        functools.partial(mask_kernel, per_block),
        grid=(peer_count,),
        in_specs=[tile, picks],
        out_specs=[tile, picks, pl.BlockSpec((latent_count, token_count), lambda s: (0, 0))],
        out_shape=[
            jax.ShapeDtypeStruct((latent_count, row_count), jnp.bfloat16),
            jax.ShapeDtypeStruct((peer_count, per_block, token_count), jnp.float32),
            jax.ShapeDtypeStruct((latent_count, token_count), jnp.float32),
        ],
        name="mask",
    )(products, cols)
    bias_grad = jnp.sum(bias_lanes, axis=1)
    returned = lax.all_to_all(lat, "lat", split_axis=0, concat_axis=0, tiled=True)
    latent_grads = pick_returned(returned, own_t)

    encoder_parts = []
    for p in range(parts):
        rows = gathered(inputs, p, decoder_parts + encoder_parts)
        encoder_parts.append(
            lax.dot_general(rows, pre_grads, (((0,), (1,)), ((), ())), preferred_element_type=jnp.float32).astype(
                jnp.bfloat16
            )
        )
    return (decoder_grad, jnp.concatenate(encoder_parts, axis=0), bias_grad, latent_grads)


def per_device(grad_recon, *others):
    row_bytes = lax.axis_size("lat") * grad_recon.size * grad_recon.dtype.itemsize
    way = by_ring if 2 * row_bytes <= RING_BYTES and lax.axis_size("lat") % 2 == 0 else by_gather
    return way(grad_recon, *others)


def solution(mesh):
    rows = P(("groups", "lat"), None)
    entries = P(("groups", "lat"), None, None)
    return jax.shard_map(
        per_device,
        mesh=mesh,
        in_specs=(rows, rows, P("lat", None), rows, rows, entries, entries),
        out_specs=(rows, P(None, ("groups", "lat")), P(("groups", "lat")), rows),
        check_vma=False,
    )
```

```python
import functools

import jax
import jax.numpy as jnp
import numpy as np
from jax import lax
from jax.experimental import pallas as pl
from jax.experimental.pallas import tpu as pltpu
from jax.sharding import PartitionSpec as P

BLOCK = 128
PART_BYTES = 9 << 20
HELD_BYTES = 1 << 25
RING_BYTES = 1 << 26
VMEM_BYTES = 20 << 20


def ring_tables(peer_count):
    chips = peer_count // 2
    ring = [chip for chip in range(chips) if chip % 2 == 0] + [chip for chip in reversed(range(chips)) if chip % 2]
    place = {chip: spot for spot, chip in enumerate(ring)}
    sources = np.zeros((peer_count, chips, 2), np.int32)
    spot_of = np.zeros((peer_count, peer_count), np.int32)
    for device in range(peer_count):
        chip, core = divmod(device, 2)
        for step in range(chips):
            hop = (step + 1) // 2
            other = ring[(place[chip] + (-hop if step % 2 else hop)) % chips]
            sources[device, step] = (2 * other + core, 2 * other + 1 - core)
            spot_of[device, 2 * other + core] = 2 * step
            spot_of[device, 2 * other + 1 - core] = 2 * step + 1
    up = [(2 * ring[i] + c, 2 * ring[(i + 1) % chips] + c) for i in range(chips) for c in range(2)]
    down = [(b, a) for a, b in up]
    swap = [(i, i ^ 1) for i in range(peer_count)]
    return sources, spot_of, up, down, swap


def product_kernel(per_block, order_ref, meta_ref, decoder_ref, mine_ref, theirs_ref, acts_ref, pre_ref, lat_ref, bias_ref):
    latents, width = decoder_ref.shape
    tokens = mine_ref.shape[0]
    span = 512 if width % 512 == 0 else BLOCK
    products = jnp.zeros((latents, 2 * tokens), jnp.float32)
    for at in range(0, width, span):
        rows = jnp.concatenate([mine_ref[:, at : at + span], theirs_ref[:, at : at + span]], axis=0)
        products += lax.dot_general(
            decoder_ref[:, at : at + span], rows, (((1,), (1,)), ((), ())), preferred_element_type=jnp.float32
        )
    row = lax.broadcasted_iota(jnp.int32, (8, tokens), 0)
    for tile in range(2):
        meta = meta_ref[order_ref[tile]].astype(jnp.float32)
        columns = [jnp.broadcast_to(meta[k : k + 1], (8, tokens)).astype(jnp.int32) for k in range(per_block)]
        values = [jnp.broadcast_to(meta[per_block + k : per_block + k + 1], (8, tokens)) for k in range(per_block)]
        sums = [jnp.zeros((8, tokens), jnp.float32) for _ in range(per_block)]
        at = slice(tile * tokens, (tile + 1) * tokens)
        for block in range(0, latents, 16):
            kept_both, dense_both = [], []
            for base in (block, block + 8):
                here = products[base : base + 8, at]
                kept = jnp.zeros((8, tokens), jnp.float32)
                dense = jnp.zeros((8, tokens), jnp.float32)
                for k in range(per_block):
                    hit = columns[k] == row + base
                    picked = jnp.where(hit, here, 0.0)
                    sums[k] = sums[k] + picked
                    kept = kept + picked
                    dense = jnp.where(hit, values[k], dense)
                if tile == 0:
                    bias_ref[base : base + 8, :] = kept
                else:
                    bias_ref[base : base + 8, :] += kept
                kept_both.append(kept)
                dense_both.append(dense)
            pre_ref[block : block + 16, at] = jnp.concatenate(kept_both, axis=0).astype(jnp.bfloat16)
            acts_ref[block : block + 16, at] = jnp.concatenate(dense_both, axis=0).astype(jnp.bfloat16)
        for k in range(per_block):
            lat_ref[tile, k : k + 1, :] = jnp.sum(sums[k], axis=0, keepdims=True)


def decoder_kernel(steps, *refs):
    acts, rows, out_ref = refs[:steps], refs[steps : 3 * steps], refs[3 * steps]
    total = jnp.zeros(out_ref.shape, jnp.float32)
    for s in range(steps):
        both = jnp.concatenate([rows[2 * s][...], rows[2 * s + 1][...]], axis=0)
        total += jnp.dot(acts[s][...], both, preferred_element_type=jnp.float32)
    out_ref[...] = total.astype(out_ref.dtype)


def encoder_kernel(steps, *refs):
    pres, rows, refs = refs[:steps], refs[steps : 3 * steps], refs[3 * steps :]
    out_ref = refs[-1]
    total = refs[0][...] if len(refs) == 2 else jnp.zeros(out_ref.shape, jnp.float32)
    for s in range(steps):
        both = jnp.concatenate([rows[2 * s][...], rows[2 * s + 1][...]], axis=0)
        total += lax.dot_general(both, pres[s][...], (((0,), (1,)), ((), ())), preferred_element_type=jnp.float32)
    out_ref[...] = total.astype(out_ref.dtype)


def after(value, *others):
    return lax.optimization_barrier((value, *others))[0]


def by_ring(grad_recon, inputs, decoder, owners, local_blocks, offsets, act_values):
    token_count, width = grad_recon.shape
    block_count = owners.shape[1]
    per_block = offsets.shape[2]
    latent_count = decoder.shape[0]
    peer_count = lax.axis_size("lat")
    chips = peer_count // 2
    me = lax.axis_index("lat")
    sources, spot_of, up, down, swap = ring_tables(peer_count)
    order = jnp.asarray(sources)[me]
    spots = jnp.asarray(spot_of)[me]

    own_t = owners.T
    columns_t = (local_blocks.T[:, None, :] * BLOCK + offsets.transpose(1, 2, 0)).astype(jnp.float32)
    values_t = act_values.transpose(1, 2, 0).astype(jnp.float32)
    peers = jnp.arange(peer_count, dtype=jnp.int32)
    sent_columns = jnp.full((peer_count, per_block, token_count), -1.0, jnp.float32)
    sent_values = jnp.zeros((peer_count, per_block, token_count), jnp.float32)
    for i in range(block_count):
        named = own_t[i][None, None, :] == peers[:, None, None]
        sent_columns = jnp.where(named, columns_t[i][None], sent_columns)
        sent_values = jnp.where(named, values_t[i][None], sent_values)
    meta = jnp.concatenate([sent_columns, sent_values], axis=1).astype(jnp.bfloat16)
    meta = lax.all_to_all(meta, "lat", split_axis=0, concat_axis=0, tiled=True)

    whole = pl.BlockSpec(memory_space=pltpu.VMEM)
    scalars = pl.BlockSpec(memory_space=pltpu.SMEM)
    step_tokens = 2 * token_count
    work = 2 * latent_count * width * step_tokens
    params = pltpu.CompilerParams(vmem_limit_bytes=VMEM_BYTES)

    def products(step, rows):
        return pl.pallas_call(
            functools.partial(product_kernel, per_block),
            in_specs=[scalars] + [whole] * 4,
            out_specs=[whole] * 4,
            out_shape=[
                jax.ShapeDtypeStruct((latent_count, step_tokens), jnp.bfloat16),
                jax.ShapeDtypeStruct((latent_count, step_tokens), jnp.bfloat16),
                jax.ShapeDtypeStruct((2, per_block, token_count), jnp.float32),
                jax.ShapeDtypeStruct((latent_count, token_count), jnp.float32),
            ],
            compiler_params=params,
            cost_estimate=pl.CostEstimate(flops=work, bytes_accessed=2 * step_tokens * width, transcendentals=0),
            name="products",
        )(order[step], meta, decoder, *rows)

    span = 512 if width % 512 == 0 else BLOCK
    rows_block = pl.BlockSpec((token_count, span), lambda i: (0, i))

    def decoder_sum(acts, rows):
        return pl.pallas_call(
            functools.partial(decoder_kernel, len(acts)),
            grid=(width // span,),
            in_specs=[whole] * len(acts) + [rows_block] * (2 * len(acts)),
            out_specs=pl.BlockSpec((latent_count, span), lambda i: (0, i)),
            out_shape=jax.ShapeDtypeStruct((latent_count, width), jnp.bfloat16),
            compiler_params=params,
            cost_estimate=pl.CostEstimate(
                flops=work * len(acts), bytes_accessed=2 * len(acts) * step_tokens * width, transcendentals=0
            ),
            name="decoder_sum",
        )(*acts, *[part for pair in rows for part in pair])

    def encoder_sum(pres, rows, total, dtype):
        block = pl.BlockSpec((span, latent_count), lambda i: (i, 0))
        totals = [] if total is None else [total]
        return pl.pallas_call(
            functools.partial(encoder_kernel, len(pres)),
            grid=(width // span,),
            in_specs=[whole] * len(pres) + [rows_block] * (2 * len(pres)) + [block] * len(totals),
            out_specs=block,
            out_shape=jax.ShapeDtypeStruct((width, latent_count), dtype),
            compiler_params=params,
            cost_estimate=pl.CostEstimate(
                flops=work * len(pres), bytes_accessed=2 * len(pres) * step_tokens * width, transcendentals=0
            ),
            name="encoder_sum",
        )(*pres, *[part for pair in rows for part in pair], *totals)

    def other(rows):
        return lax.ppermute(rows, "lat", swap)

    grads, ins, done = [None] * chips, [None] * chips, [None] * chips
    held = {("g", True): grad_recon, ("g", False): grad_recon, ("i", True): inputs, ("i", False): inputs}

    def hop(kind, number, *first):
        for upward in (True, False):
            step = 2 * number - 1 if upward else 2 * number
            antipode = 2 * number == chips
            if antipode and upward != (kind == "g"):
                continue
            rows = held[kind, upward]
            if first:
                rows = after(rows, *first)
            rows = lax.ppermute(rows, "lat", up if upward else down)
            held[kind, upward] = rows
            (grads if kind == "g" else ins)[chips - 1 if antipode else step] = (rows, other(rows))

    def compute(*steps):
        for step in steps:
            done[step] = products(step, grads[step])

    hops = chips // 2
    grads[0] = (grad_recon, other(grad_recon))
    ins[0] = (inputs, other(inputs))
    hop("g", 1)
    hop("i", 1)
    compute(0)
    for number in range(2, hops + 1):
        earlier = [done[step][3] for step in range(max(0, 2 * number - 5), 2 * number - 3)]
        hop("g", number, *earlier)
        compute(2 * number - 3, 2 * number - 2)
        if number < hops:
            hop("i", number, *earlier)
    compute(chips - 1)
    hop("i", hops, done[chips - 2][3])
    acts, pres, lats, biases = zip(*done)

    lat = jnp.concatenate(lats, axis=0)[spots]
    returned = lax.all_to_all(lat, "lat", split_axis=0, concat_axis=0, tiled=True)
    latent_grads = pick_returned(returned, own_t)
    decoder_grad = decoder_sum(acts, grads)
    bias_grad = jnp.sum(functools.reduce(jnp.add, biases), axis=1)

    early = [0] + list(range(1, chips - 3)) + [chips - 2]
    late = [chips - 3, chips - 1]
    total = encoder_sum([pres[s] for s in early], [ins[s] for s in early], None, jnp.float32)
    encoder_grad = encoder_sum([pres[s] for s in late], [ins[s] for s in late], total, jnp.bfloat16)
    return (decoder_grad, encoder_grad, bias_grad, latent_grads)


def pick_returned(returned, own_t):
    owner_id = jnp.arange(returned.shape[0], dtype=jnp.int32)[:, None, None, None]
    picked = jnp.where(own_t[None, :, None, :] == owner_id, returned[:, None, :, :], 0.0)
    return jnp.sum(picked, axis=0).reshape(-1, own_t.shape[1]).T


def build_kernel(block_count, per_block, me_ref, meta_ref, acts_ref, cols_ref):
    pairs = block_count * per_block
    meta = meta_ref[0].astype(jnp.float32)
    me = me_ref[0].astype(jnp.float32)
    tokens = meta.shape[1]
    values = jnp.zeros((per_block, tokens), jnp.float32)
    columns = jnp.full((per_block, tokens), -1.0, jnp.float32)
    for i in range(block_count):
        mine = meta[2 * pairs + i : 2 * pairs + i + 1] == me
        values = jnp.where(mine, meta[i * per_block : (i + 1) * per_block], values)
        columns = jnp.where(mine, meta[pairs + i * per_block : pairs + (i + 1) * per_block], columns)
    columns = columns.astype(jnp.int32)
    cols_ref[0] = columns
    row = lax.broadcasted_iota(jnp.int32, (acts_ref.shape[0], tokens), 0)
    dense = jnp.zeros(row.shape, jnp.float32)
    for k in range(per_block):
        dense = jnp.where(row == columns[k : k + 1], values[k : k + 1], dense)
    acts_ref[...] = dense.astype(jnp.bfloat16)


def mask_kernel(per_block, products_ref, cols_ref, pre_ref, lat_ref, bias_ref):
    products = products_ref[...]
    columns = cols_ref[0]
    row = lax.broadcasted_iota(jnp.int32, products.shape, 0)
    kept = jnp.zeros(products.shape, jnp.float32)
    for k in range(per_block):
        picked = jnp.where(row == columns[k : k + 1], products, 0.0)
        lat_ref[0, k : k + 1, :] = jnp.sum(picked, axis=0, keepdims=True)
        kept = kept + picked
    pre_ref[...] = kept.astype(jnp.bfloat16)

    @pl.when(pl.program_id(0) == 0)
    def _():
        bias_ref[...] = jnp.zeros_like(bias_ref)

    bias_ref[...] += kept


def column_parts(width, row_count):
    lanes = width // BLOCK
    for parts in range(2, lanes + 1):
        if lanes % parts == 0 and row_count * (width // parts) * 2 <= PART_BYTES:
            return parts
    return lanes


def by_gather(grad_recon, inputs, decoder, owners, local_blocks, offsets, act_values):
    token_count, width = grad_recon.shape
    block_count = owners.shape[1]
    per_block = offsets.shape[2]
    latent_count = decoder.shape[0]
    peer_count = lax.axis_size("lat")
    pairs = block_count * per_block
    row_count = peer_count * token_count
    me = lax.axis_index("lat").astype(jnp.int32).reshape(1)

    own_t = owners.T
    columns_t = (local_blocks.T[:, None, :] * BLOCK + offsets.transpose(1, 2, 0)).reshape(pairs, token_count)
    acts_t = act_values.transpose(1, 2, 0).reshape(pairs, token_count)
    filler = jnp.zeros((-block_count % 16, token_count), jnp.bfloat16)
    meta = jnp.concatenate([acts_t, columns_t.astype(jnp.bfloat16), own_t.astype(jnp.bfloat16), filler], axis=0)
    meta_all = lax.all_gather(meta, "lat", axis=0)

    parts = column_parts(width, row_count)
    span = width // parts
    depth = max(1, HELD_BYTES // (row_count * span * 2))

    def gathered(rows, p, done):
        piece = rows[:, p * span : (p + 1) * span]
        if len(done) >= depth:
            piece, _ = lax.optimization_barrier((piece, done[-depth]))
        return lax.all_gather(piece, "lat", axis=0, tiled=True)

    tile = pl.BlockSpec((latent_count, token_count), lambda s: (0, s))
    picks = pl.BlockSpec((1, per_block, token_count), lambda s: (s, 0, 0))
    acts_dense, cols = pl.pallas_call(
        functools.partial(build_kernel, block_count, per_block),
        grid=(peer_count,),
        in_specs=[
            pl.BlockSpec(memory_space=pltpu.SMEM),
            pl.BlockSpec((1, meta.shape[0], token_count), lambda s: (s, 0, 0)),
        ],
        out_specs=[tile, picks],
        out_shape=[
            jax.ShapeDtypeStruct((latent_count, row_count), jnp.bfloat16),
            jax.ShapeDtypeStruct((peer_count, per_block, token_count), jnp.int32),
        ],
        name="build",
    )(me, meta_all)

    products = None
    decoder_parts = []
    for p in range(parts):
        rows = gathered(grad_recon, p, decoder_parts)
        part = lax.dot_general(
            acts_dense, rows, (((1,), (0,)), ((), ())), preferred_element_type=jnp.float32
        ).astype(jnp.bfloat16)
        term = lax.dot_general(
            decoder[:, p * span : (p + 1) * span], rows, (((1,), (1,)), ((), ())), preferred_element_type=jnp.float32
        )
        products = term if products is None else products + term
        if depth < 2 * parts:
            part, products = lax.optimization_barrier((part, products))
        decoder_parts.append(part)
    decoder_grad = jnp.concatenate(decoder_parts, axis=1)

    pre_grads, lat, bias_lanes = pl.pallas_call(
        functools.partial(mask_kernel, per_block),
        grid=(peer_count,),
        in_specs=[tile, picks],
        out_specs=[tile, picks, pl.BlockSpec((latent_count, token_count), lambda s: (0, 0))],
        out_shape=[
            jax.ShapeDtypeStruct((latent_count, row_count), jnp.bfloat16),
            jax.ShapeDtypeStruct((peer_count, per_block, token_count), jnp.float32),
            jax.ShapeDtypeStruct((latent_count, token_count), jnp.float32),
        ],
        name="mask",
    )(products, cols)
    bias_grad = jnp.sum(bias_lanes, axis=1)
    returned = lax.all_to_all(lat, "lat", split_axis=0, concat_axis=0, tiled=True)
    latent_grads = pick_returned(returned, own_t)

    encoder_parts = []
    for p in range(parts):
        rows = gathered(inputs, p, decoder_parts + encoder_parts)
        encoder_parts.append(
            lax.dot_general(rows, pre_grads, (((0,), (1,)), ((), ())), preferred_element_type=jnp.float32).astype(
                jnp.bfloat16
            )
        )
    return (decoder_grad, jnp.concatenate(encoder_parts, axis=0), bias_grad, latent_grads)


def per_device(grad_recon, *others):
    row_bytes = lax.axis_size("lat") * grad_recon.size * grad_recon.dtype.itemsize
    way = by_ring if 2 * row_bytes <= RING_BYTES and lax.axis_size("lat") % 4 == 0 else by_gather
    return way(grad_recon, *others)


def solution(mesh):
    rows = P(("groups", "lat"), None)
    entries = P(("groups", "lat"), None, None)
    return jax.shard_map(
        per_device,
        mesh=mesh,
        in_specs=(rows, rows, P("lat", None), rows, rows, entries, entries),
        out_specs=(rows, P(None, ("groups", "lat")), P(("groups", "lat")), rows),
        check_vma=False,
    )
```

```python
import functools

import jax
import jax.numpy as jnp
import numpy as np
from jax import lax
from jax.experimental import pallas as pl
from jax.experimental.pallas import tpu as pltpu
from jax.sharding import PartitionSpec as P

BLOCK = 128
PART_BYTES = 9 << 20
HELD_BYTES = 1 << 25
RING_BYTES = 1 << 26
VMEM_BYTES = 24 << 20


def ring_tables(peer_count):
    chips = peer_count // 2
    ring = [chip for chip in range(chips) if chip % 2 == 0] + [chip for chip in reversed(range(chips)) if chip % 2]
    place = {chip: spot for spot, chip in enumerate(ring)}
    sources = np.zeros((peer_count, chips, 2), np.int32)
    for device in range(peer_count):
        chip, core = divmod(device, 2)
        sign = 1 - 2 * core
        for hop in range(chips):
            behind, ahead = ring[(place[chip] - sign * hop) % chips], ring[(place[chip] + sign * hop) % chips]
            sources[device, hop] = (2 * behind + core, 2 * ahead + 1 - core)
    onward = [(2 * ring[i], 2 * ring[(i + 1) % chips]) for i in range(chips)]
    onward += [(2 * ring[i] + 1, 2 * ring[(i - 1) % chips] + 1) for i in range(chips)]
    swap = [(i, i ^ 1) for i in range(peer_count)]
    return sources, onward, swap


def product_kernel(per_block, order_ref, meta_ref, decoder_ref, mine_ref, theirs_ref, *refs):
    acts_ref, pre_ref, lat_ref, bias_ref, rows_ref, sems = refs[-6:]
    tokens = mine_ref.shape[0]
    copies = [
        pltpu.make_async_copy(source, rows_ref.at[pl.ds(i * tokens, tokens)], sems.at[i])
        for i, source in enumerate((mine_ref, theirs_ref))
    ]
    for copy in copies:
        copy.start()
    if len(refs) == 8:
        lat_ref[...] = refs[0][...]
        bias_ref[...] = refs[1][...]
    else:
        lat_ref[...] = jnp.zeros_like(lat_ref)
        bias_ref[...] = jnp.zeros_like(bias_ref)
    latents = decoder_ref.shape[0]
    for copy in copies:
        copy.wait()
    products = lax.dot_general(
        decoder_ref[...], rows_ref[...], (((1,), (1,)), ((), ())), preferred_element_type=jnp.float32
    )
    row = lax.broadcasted_iota(jnp.int32, (8, tokens), 0)
    for tile in range(2):
        meta = meta_ref[order_ref[tile]].astype(jnp.float32)
        columns = [jnp.broadcast_to(meta[k : k + 1], (8, tokens)).astype(jnp.int32) for k in range(per_block)]
        values = [jnp.broadcast_to(meta[per_block + k : per_block + k + 1], (8, tokens)) for k in range(per_block)]
        sums = [jnp.zeros((8, tokens), jnp.float32) for _ in range(per_block)]
        at = slice(tile * tokens, (tile + 1) * tokens)
        for block in range(0, latents, 16):
            kept_both, dense_both = [], []
            for base in (block, block + 8):
                here = products[base : base + 8, at]
                kept = jnp.zeros((8, tokens), jnp.float32)
                dense = jnp.zeros((8, tokens), jnp.float32)
                for k in range(per_block):
                    hit = columns[k] == row + base
                    picked = jnp.where(hit, here, 0.0)
                    sums[k] = sums[k] + picked
                    kept = kept + picked
                    dense = jnp.where(hit, values[k], dense)
                bias_ref[base : base + 8, :] += kept
                kept_both.append(kept)
                dense_both.append(dense)
            pre_ref[block : block + 16, at] = jnp.concatenate(kept_both, axis=0).astype(jnp.bfloat16)
            acts_ref[block : block + 16, at] = jnp.concatenate(dense_both, axis=0).astype(jnp.bfloat16)
        source = order_ref[tile]
        for k in range(per_block):
            lat_ref[source, k : k + 1, :] = jnp.sum(sums[k], axis=0, keepdims=True)


def decoder_kernel(steps, span, *refs):
    acts, rows, out_ref = refs[:steps], refs[steps : 3 * steps], refs[-1]

    def body(*blocks):
        total = jnp.zeros(blocks[-1].shape, jnp.float32)
        for s in range(steps):
            both = jnp.concatenate([blocks[2 * s][...], blocks[2 * s + 1][...]], axis=0)
            total += jnp.dot(acts[s][...], both, preferred_element_type=jnp.float32)
        blocks[-1][...] = total.astype(out_ref.dtype)

    tokens, width = rows[0].shape
    pltpu.emit_pipeline(
        body,
        grid=(width // span,),
        in_specs=[pl.BlockSpec((tokens, span), lambda i: (0, i))] * (2 * steps),
        out_specs=[pl.BlockSpec((out_ref.shape[0], span), lambda i: (0, i))],
    )(*rows, out_ref)


def encoder_kernel(steps, span, *refs):
    pres, rows, refs = refs[:steps], refs[steps : 3 * steps], refs[3 * steps :]
    out_ref = refs[-1]

    def body(*blocks):
        total = blocks[2 * steps][...] if len(refs) == 2 else jnp.zeros(blocks[-1].shape, jnp.float32)
        for s in range(steps):
            both = jnp.concatenate([blocks[2 * s][...], blocks[2 * s + 1][...]], axis=0)
            total += lax.dot_general(both, pres[s][...], (((0,), (1,)), ((), ())), preferred_element_type=jnp.float32)
        blocks[-1][...] = total.astype(out_ref.dtype)

    tokens, width = rows[0].shape
    sums = pl.BlockSpec((span, out_ref.shape[1]), lambda i: (i, 0))
    pltpu.emit_pipeline(
        body,
        grid=(width // span,),
        in_specs=[pl.BlockSpec((tokens, span), lambda i: (0, i))] * (2 * steps) + [sums] * (len(refs) - 1),
        out_specs=[sums],
    )(*rows, *refs)


def after(value, *others):
    return lax.optimization_barrier((value, *others))[0]


def by_ring(grad_recon, inputs, decoder, owners, local_blocks, offsets, act_values):
    token_count, width = grad_recon.shape
    block_count = owners.shape[1]
    per_block = offsets.shape[2]
    latent_count = decoder.shape[0]
    peer_count = lax.axis_size("lat")
    chips = peer_count // 2
    me = lax.axis_index("lat")
    sources, onward, swap = ring_tables(peer_count)
    order = jnp.asarray(sources)[me]

    own_t = owners.T
    columns_t = (local_blocks.T[:, None, :] * BLOCK + offsets.transpose(1, 2, 0)).astype(jnp.float32)
    values_t = act_values.transpose(1, 2, 0).astype(jnp.float32)
    peers = jnp.arange(peer_count, dtype=jnp.int32)
    sent_columns = jnp.full((peer_count, per_block, token_count), -1.0, jnp.float32)
    sent_values = jnp.zeros((peer_count, per_block, token_count), jnp.float32)
    for i in range(block_count):
        named = own_t[i][None, None, :] == peers[:, None, None]
        sent_columns = jnp.where(named, columns_t[i][None], sent_columns)
        sent_values = jnp.where(named, values_t[i][None], sent_values)
    meta = jnp.concatenate([sent_columns, sent_values], axis=1).astype(jnp.bfloat16)
    meta = lax.all_to_all(meta, "lat", split_axis=0, concat_axis=0, tiled=True)

    whole = pl.BlockSpec(memory_space=pltpu.VMEM)
    scalars = pl.BlockSpec(memory_space=pltpu.SMEM)
    far = pl.BlockSpec(memory_space=pltpu.HBM)
    step_tokens = 2 * token_count
    light = pl.CostEstimate(flops=1, bytes_accessed=1, transcendentals=0)
    params = pltpu.CompilerParams(vmem_limit_bytes=VMEM_BYTES)

    def products(step, rows, totals):
        return pl.pallas_call(
            functools.partial(product_kernel, per_block),
            in_specs=[scalars, whole, whole, far, far] + [whole] * len(totals),
            out_specs=[whole] * 4,
            out_shape=[
                jax.ShapeDtypeStruct((latent_count, step_tokens), jnp.bfloat16),
                jax.ShapeDtypeStruct((latent_count, step_tokens), jnp.bfloat16),
                jax.ShapeDtypeStruct((peer_count, per_block, token_count), jnp.float32),
                jax.ShapeDtypeStruct((latent_count, token_count), jnp.float32),
            ],
            scratch_shapes=[pltpu.VMEM((step_tokens, width), jnp.bfloat16), pltpu.SemaphoreType.DMA((2,))],
            compiler_params=params,
            cost_estimate=light,
            name="products",
        )(order[step], meta, decoder, *rows, *totals)

    span = 512 if width % 512 == 0 else BLOCK

    def decoder_sum(acts, rows):
        steps = len(acts)
        return pl.pallas_call(
            functools.partial(decoder_kernel, steps, span),
            in_specs=[whole] * steps + [far] * (2 * steps),
            out_specs=far,
            out_shape=jax.ShapeDtypeStruct((latent_count, width), jnp.bfloat16),
            compiler_params=params,
            cost_estimate=light,
            name="decoder_sum",
        )(*acts, *[part for pair in rows for part in pair])

    def encoder_sum(pres, rows, partial, dtype):
        steps = len(pres)
        partials = [] if partial is None else [partial]
        return pl.pallas_call(
            functools.partial(encoder_kernel, steps, span),
            in_specs=[whole] * steps + [far] * (2 * steps + len(partials)),
            out_specs=far,
            out_shape=jax.ShapeDtypeStruct((width, latent_count), dtype),
            compiler_params=params,
            cost_estimate=light,
            name="encoder_sum",
        )(*pres, *[part for pair in rows for part in pair], *partials)

    acts, pres, totals = [], [], ()
    grads, ins = [], [inputs]

    def send(rows, way, *first):
        return lax.ppermute(after(rows, *first) if first else rows, "lat", way)

    def compute(rows):
        nonlocal totals
        grads.append(rows)
        acts_here, pre_here, *totals = products(len(acts), rows, totals)
        acts.append(acts_here)
        pres.append(pre_here)

    arriving = send(grad_recon, onward)
    compute((grad_recon, send(grad_recon, swap)))
    partial = None
    for hop in range(1, chips):
        grad = arriving
        if hop < chips - 1:
            arriving = send(grad, onward, *((meta,) if hop == 1 else (totals[1],)))
        theirs = send(grad, swap, *(() if partial is None else (partial,)))
        moved = send(ins[hop - 1], onward, *((theirs,) if hop == 1 else (ins[hop - 2][1],)), *(totals if hop == chips - 1 else ()))
        compute((grad, theirs))
        ins[hop - 1] = (ins[hop - 1], send(ins[hop - 1], swap))
        ins.append(moved)
        if hop == chips - 2:
            partial = encoder_sum(pres[: hop - 1], ins[: hop - 1], None, jnp.float32)
    returned = lax.all_to_all(totals[0], "lat", split_axis=0, concat_axis=0, tiled=True)
    latent_grads = pick_returned(returned, own_t)
    decoder_grad = decoder_sum(acts, grads)
    ins[-1] = (ins[-1], send(ins[-1], swap, decoder_grad))
    bias_grad = jnp.sum(totals[1], axis=1)
    encoder_grad = encoder_sum(pres[chips - 3 :], ins[chips - 3 :], partial, jnp.bfloat16)
    return (decoder_grad, encoder_grad, bias_grad, latent_grads)


def pick_returned(returned, own_t):
    owner_id = jnp.arange(returned.shape[0], dtype=jnp.int32)[:, None, None, None]
    picked = jnp.where(own_t[None, :, None, :] == owner_id, returned[:, None, :, :], 0.0)
    return jnp.sum(picked, axis=0).reshape(-1, own_t.shape[1]).T


def build_kernel(block_count, per_block, me_ref, meta_ref, acts_ref, cols_ref):
    pairs = block_count * per_block
    meta = meta_ref[0].astype(jnp.float32)
    me = me_ref[0].astype(jnp.float32)
    tokens = meta.shape[1]
    values = jnp.zeros((per_block, tokens), jnp.float32)
    columns = jnp.full((per_block, tokens), -1.0, jnp.float32)
    for i in range(block_count):
        mine = meta[2 * pairs + i : 2 * pairs + i + 1] == me
        values = jnp.where(mine, meta[i * per_block : (i + 1) * per_block], values)
        columns = jnp.where(mine, meta[pairs + i * per_block : pairs + (i + 1) * per_block], columns)
    columns = columns.astype(jnp.int32)
    cols_ref[0] = columns
    row = lax.broadcasted_iota(jnp.int32, (acts_ref.shape[0], tokens), 0)
    dense = jnp.zeros(row.shape, jnp.float32)
    for k in range(per_block):
        dense = jnp.where(row == columns[k : k + 1], values[k : k + 1], dense)
    acts_ref[...] = dense.astype(jnp.bfloat16)


def mask_kernel(per_block, products_ref, cols_ref, pre_ref, lat_ref, bias_ref):
    products = products_ref[...]
    columns = cols_ref[0]
    row = lax.broadcasted_iota(jnp.int32, products.shape, 0)
    kept = jnp.zeros(products.shape, jnp.float32)
    for k in range(per_block):
        picked = jnp.where(row == columns[k : k + 1], products, 0.0)
        lat_ref[0, k : k + 1, :] = jnp.sum(picked, axis=0, keepdims=True)
        kept = kept + picked
    pre_ref[...] = kept.astype(jnp.bfloat16)

    @pl.when(pl.program_id(0) == 0)
    def _():
        bias_ref[...] = jnp.zeros_like(bias_ref)

    bias_ref[...] += kept


def column_parts(width, row_count):
    lanes = width // BLOCK
    for parts in range(2, lanes + 1):
        if lanes % parts == 0 and row_count * (width // parts) * 2 <= PART_BYTES:
            return parts
    return lanes


def by_gather(grad_recon, inputs, decoder, owners, local_blocks, offsets, act_values):
    token_count, width = grad_recon.shape
    block_count = owners.shape[1]
    per_block = offsets.shape[2]
    latent_count = decoder.shape[0]
    peer_count = lax.axis_size("lat")
    pairs = block_count * per_block
    row_count = peer_count * token_count
    me = lax.axis_index("lat").astype(jnp.int32).reshape(1)

    own_t = owners.T
    columns_t = (local_blocks.T[:, None, :] * BLOCK + offsets.transpose(1, 2, 0)).reshape(pairs, token_count)
    acts_t = act_values.transpose(1, 2, 0).reshape(pairs, token_count)
    filler = jnp.zeros((-block_count % 16, token_count), jnp.bfloat16)
    meta = jnp.concatenate([acts_t, columns_t.astype(jnp.bfloat16), own_t.astype(jnp.bfloat16), filler], axis=0)
    meta_all = lax.all_gather(meta, "lat", axis=0)

    parts = column_parts(width, row_count)
    span = width // parts
    depth = max(1, HELD_BYTES // (row_count * span * 2))

    def gathered(rows, p, done):
        piece = rows[:, p * span : (p + 1) * span]
        if len(done) >= depth:
            piece, _ = lax.optimization_barrier((piece, done[-depth]))
        return lax.all_gather(piece, "lat", axis=0, tiled=True)

    tile = pl.BlockSpec((latent_count, token_count), lambda s: (0, s))
    picks = pl.BlockSpec((1, per_block, token_count), lambda s: (s, 0, 0))
    acts_dense, cols = pl.pallas_call(
        functools.partial(build_kernel, block_count, per_block),
        grid=(peer_count,),
        in_specs=[
            pl.BlockSpec(memory_space=pltpu.SMEM),
            pl.BlockSpec((1, meta.shape[0], token_count), lambda s: (s, 0, 0)),
        ],
        out_specs=[tile, picks],
        out_shape=[
            jax.ShapeDtypeStruct((latent_count, row_count), jnp.bfloat16),
            jax.ShapeDtypeStruct((peer_count, per_block, token_count), jnp.int32),
        ],
        name="build",
    )(me, meta_all)

    products = None
    decoder_parts = []
    for p in range(parts):
        rows = gathered(grad_recon, p, decoder_parts)
        part = lax.dot_general(
            acts_dense, rows, (((1,), (0,)), ((), ())), preferred_element_type=jnp.float32
        ).astype(jnp.bfloat16)
        term = lax.dot_general(
            decoder[:, p * span : (p + 1) * span], rows, (((1,), (1,)), ((), ())), preferred_element_type=jnp.float32
        )
        products = term if products is None else products + term
        if depth < 2 * parts:
            part, products = lax.optimization_barrier((part, products))
        decoder_parts.append(part)
    decoder_grad = jnp.concatenate(decoder_parts, axis=1)

    pre_grads, lat, bias_lanes = pl.pallas_call(
        functools.partial(mask_kernel, per_block),
        grid=(peer_count,),
        in_specs=[tile, picks],
        out_specs=[tile, picks, pl.BlockSpec((latent_count, token_count), lambda s: (0, 0))],
        out_shape=[
            jax.ShapeDtypeStruct((latent_count, row_count), jnp.bfloat16),
            jax.ShapeDtypeStruct((peer_count, per_block, token_count), jnp.float32),
            jax.ShapeDtypeStruct((latent_count, token_count), jnp.float32),
        ],
        name="mask",
    )(products, cols)
    bias_grad = jnp.sum(bias_lanes, axis=1)
    returned = lax.all_to_all(lat, "lat", split_axis=0, concat_axis=0, tiled=True)
    latent_grads = pick_returned(returned, own_t)

    encoder_parts = []
    for p in range(parts):
        rows = gathered(inputs, p, decoder_parts + encoder_parts)
        encoder_parts.append(
            lax.dot_general(rows, pre_grads, (((0,), (1,)), ((), ())), preferred_element_type=jnp.float32).astype(
                jnp.bfloat16
            )
        )
    return (decoder_grad, jnp.concatenate(encoder_parts, axis=0), bias_grad, latent_grads)


def per_device(grad_recon, *others):
    row_bytes = lax.axis_size("lat") * grad_recon.size * grad_recon.dtype.itemsize
    way = by_ring if 2 * row_bytes <= RING_BYTES and lax.axis_size("lat") % 4 == 0 else by_gather
    return way(grad_recon, *others)


def solution(mesh):
    rows = P(("groups", "lat"), None)
    entries = P(("groups", "lat"), None, None)
    return jax.shard_map(
        per_device,
        mesh=mesh,
        in_specs=(rows, rows, P("lat", None), rows, rows, entries, entries),
        out_specs=(rows, P(None, ("groups", "lat")), P(("groups", "lat")), rows),
        check_vma=False,
    )
```

```python
import functools

import jax
import jax.numpy as jnp
import numpy as np
from jax import lax
from jax.experimental import pallas as pl
from jax.experimental.pallas import tpu as pltpu
from jax.sharding import PartitionSpec as P

BLOCK = 128
PART_BYTES = 9 << 20
HELD_BYTES = 1 << 25
RING_BYTES = 1 << 26
VMEM_BYTES = 24 << 20


def ring_tables(peer_count):
    chips = peer_count // 2
    ring = [chip for chip in range(chips) if chip % 2 == 0] + [chip for chip in reversed(range(chips)) if chip % 2]
    place = {chip: spot for spot, chip in enumerate(ring)}
    sources = np.zeros((peer_count, chips, 2), np.int32)
    for device in range(peer_count):
        chip, core = divmod(device, 2)
        sign = 1 - 2 * core
        for hop in range(chips):
            behind, ahead = ring[(place[chip] - sign * hop) % chips], ring[(place[chip] + sign * hop) % chips]
            sources[device, hop] = (2 * behind + core, 2 * ahead + 1 - core)
    onward = [(2 * ring[i], 2 * ring[(i + 1) % chips]) for i in range(chips)]
    onward += [(2 * ring[i] + 1, 2 * ring[(i - 1) % chips] + 1) for i in range(chips)]
    swap = [(i, i ^ 1) for i in range(peer_count)]
    return sources, onward, swap


def grad_kernel(per_block, order_ref, meta_ref, decoder_ref, mine_ref, theirs_ref, *refs):
    total_ref, lat_ref, bias_ref, pre_ref, acts_ref = refs[-5:]
    first = len(refs) == 5
    if first:
        lat_ref[...] = jnp.zeros_like(lat_ref)
        bias_ref[...] = jnp.zeros_like(bias_ref)
    else:
        lat_ref[...] = refs[1][...]
        bias_ref[...] = refs[2][...]
    latents, width = decoder_ref.shape
    tokens = mine_ref.shape[0]
    span = column_span(width)
    products = jnp.zeros((latents, 2 * tokens), jnp.float32)
    for at in range(0, width, span):
        rows = jnp.concatenate([mine_ref[:, at : at + span], theirs_ref[:, at : at + span]], axis=0)
        products += lax.dot_general(
            decoder_ref[:, at : at + span], rows, (((1,), (1,)), ((), ())), preferred_element_type=jnp.float32
        )
    row = lax.broadcasted_iota(jnp.int32, (8, tokens), 0)
    for tile in range(2):
        meta = meta_ref[order_ref[tile]].astype(jnp.float32)
        columns = [jnp.broadcast_to(meta[k : k + 1], (8, tokens)).astype(jnp.int32) for k in range(per_block)]
        values = [jnp.broadcast_to(meta[per_block + k : per_block + k + 1], (8, tokens)) for k in range(per_block)]
        sums = [jnp.zeros((8, tokens), jnp.float32) for _ in range(per_block)]
        at = slice(tile * tokens, (tile + 1) * tokens)
        for block in range(0, latents, 16):
            kept_both, dense_both = [], []
            for base in (block, block + 8):
                here = products[base : base + 8, at]
                kept = jnp.zeros((8, tokens), jnp.float32)
                dense = jnp.zeros((8, tokens), jnp.float32)
                for k in range(per_block):
                    hit = columns[k] == row + base
                    picked = jnp.where(hit, here, 0.0)
                    sums[k] = sums[k] + picked
                    kept = kept + picked
                    dense = jnp.where(hit, values[k], dense)
                bias_ref[base : base + 8, :] += kept
                kept_both.append(kept)
                dense_both.append(dense)
            pre_ref[block : block + 16, at] = jnp.concatenate(kept_both, axis=0).astype(jnp.bfloat16)
            acts_ref[block : block + 16, at] = jnp.concatenate(dense_both, axis=0).astype(jnp.bfloat16)
        source = order_ref[tile]
        for k in range(per_block):
            lat_ref[source, k : k + 1, :] = jnp.sum(sums[k], axis=0, keepdims=True)
    for at in range(0, width, span):
        rows = jnp.concatenate([mine_ref[:, at : at + span], theirs_ref[:, at : at + span]], axis=0)
        term = jnp.dot(acts_ref[...], rows, preferred_element_type=jnp.float32)
        if not first:
            term += refs[0][:, at : at + span]
        total_ref[:, at : at + span] = term.astype(total_ref.dtype)


def input_kernel(pre_ref, mine_ref, theirs_ref, *refs):
    total_ref = refs[-1]
    width = mine_ref.shape[1]
    span = column_span(width)
    for at in range(0, width, span):
        rows = jnp.concatenate([mine_ref[:, at : at + span], theirs_ref[:, at : at + span]], axis=0)
        term = lax.dot_general(rows, pre_ref[...], (((0,), (1,)), ((), ())), preferred_element_type=jnp.float32)
        if len(refs) == 2:
            term += refs[0][at : at + span, :]
        total_ref[at : at + span, :] = term.astype(total_ref.dtype)


def column_span(width):
    return 512 if width % 512 == 0 else BLOCK


def after(value, *others):
    return lax.optimization_barrier((value, *others))[0]


def by_ring(grad_recon, inputs, decoder, owners, local_blocks, offsets, act_values):
    token_count, width = grad_recon.shape
    block_count = owners.shape[1]
    per_block = offsets.shape[2]
    latent_count = decoder.shape[0]
    peer_count = lax.axis_size("lat")
    chips = peer_count // 2
    me = lax.axis_index("lat")
    sources, onward, swap = ring_tables(peer_count)
    order = jnp.asarray(sources)[me]

    own_t = owners.T
    columns_t = (local_blocks.T[:, None, :] * BLOCK + offsets.transpose(1, 2, 0)).astype(jnp.float32)
    values_t = act_values.transpose(1, 2, 0).astype(jnp.float32)
    peers = jnp.arange(peer_count, dtype=jnp.int32)
    sent_columns = jnp.full((peer_count, per_block, token_count), -1.0, jnp.float32)
    sent_values = jnp.zeros((peer_count, per_block, token_count), jnp.float32)
    for i in range(block_count):
        named = own_t[i][None, None, :] == peers[:, None, None]
        sent_columns = jnp.where(named, columns_t[i][None], sent_columns)
        sent_values = jnp.where(named, values_t[i][None], sent_values)
    meta = jnp.concatenate([sent_columns, sent_values], axis=1).astype(jnp.bfloat16)
    meta = lax.all_to_all(meta, "lat", split_axis=0, concat_axis=0, tiled=True)

    whole = pl.BlockSpec(memory_space=pltpu.VMEM)
    scalars = pl.BlockSpec(memory_space=pltpu.SMEM)
    step_tokens = 2 * token_count
    light = pl.CostEstimate(flops=1, bytes_accessed=1, transcendentals=0)
    params = pltpu.CompilerParams(vmem_limit_bytes=VMEM_BYTES)

    def near(value):
        return pltpu.with_memory_space_constraint(value, pltpu.VMEM)

    def grad_step(hop, rows, totals):
        last = hop == chips - 1
        sums = (latent_count, width)
        return pl.pallas_call(
            functools.partial(grad_kernel, per_block),
            in_specs=[scalars] + [whole] * (4 + len(totals)),
            out_specs=[whole] * 4,
            out_shape=[
                jax.ShapeDtypeStruct(sums, jnp.bfloat16) if last else pltpu.VMEM(sums, jnp.float32),
                pltpu.VMEM((peer_count, per_block, token_count), jnp.float32),
                pltpu.VMEM((latent_count, token_count), jnp.float32),
                pltpu.VMEM((latent_count, step_tokens), jnp.bfloat16),
            ],
            scratch_shapes=[pltpu.VMEM((latent_count, step_tokens), jnp.bfloat16)],
            input_output_aliases={5 + i: i for i in range(1 if last else 0, len(totals))},
            compiler_params=params,
            cost_estimate=light,
            name="grad_step",
        )(order[hop], near(meta), near(decoder), near(rows[0]), near(rows[1]), *map(near, totals))

    def input_step(hop, rows, total):
        last = hop == chips - 1
        sums = (width, latent_count)
        totals = () if total is None else (total,)
        return pl.pallas_call(
            input_kernel,
            in_specs=[whole] * (3 + len(totals)),
            out_specs=whole,
            out_shape=jax.ShapeDtypeStruct(sums, jnp.bfloat16) if last else pltpu.VMEM(sums, jnp.float32),
            input_output_aliases={3: 0} if totals and not last else {},
            compiler_params=params,
            cost_estimate=light,
            name="input_step",
        )(near(pres[hop]), near(rows[0]), near(rows[1]), *map(near, totals))

    def send(rows, way, *first):
        return lax.ppermute(after(rows, *first) if first else rows, "lat", way)

    pres, totals, encoder_total = [], (), None

    def use_grads(rows):
        nonlocal totals
        *totals, pre = grad_step(len(pres), rows, totals)
        pres.append(pre)

    grad, inward = send(grad_recon, onward), send(inputs, onward)
    use_grads((grad_recon, send(grad_recon, swap)))
    encoder_total = input_step(0, (inputs, send(inputs, swap, meta)), None)
    grad_next = send(grad, onward, meta)
    for hop in range(1, chips):
        use_grads((grad, send(grad, swap)))
        pair = (inward, send(inward, swap, *((totals[2], encoder_total) if hop == chips - 1 else ())))
        if hop < chips - 1:
            inward = send(inward, onward, totals[2])
        encoder_total = input_step(hop, pair, encoder_total)
        grad = grad_next
        if hop < chips - 2:
            grad_next = send(grad, onward, encoder_total)
    decoder_grad, lat, bias = totals
    returned = lax.all_to_all(lat, "lat", split_axis=0, concat_axis=0, tiled=True)
    latent_grads = pick_returned(after(returned, encoder_total), own_t)
    return (decoder_grad, encoder_total, jnp.sum(bias, axis=1), latent_grads)


def pick_returned(returned, own_t):
    owner_id = jnp.arange(returned.shape[0], dtype=jnp.int32)[:, None, None, None]
    picked = jnp.where(own_t[None, :, None, :] == owner_id, returned[:, None, :, :], 0.0)
    return jnp.sum(picked, axis=0).reshape(-1, own_t.shape[1]).T


def build_kernel(block_count, per_block, me_ref, meta_ref, acts_ref, cols_ref):
    pairs = block_count * per_block
    meta = meta_ref[0].astype(jnp.float32)
    me = me_ref[0].astype(jnp.float32)
    tokens = meta.shape[1]
    values = jnp.zeros((per_block, tokens), jnp.float32)
    columns = jnp.full((per_block, tokens), -1.0, jnp.float32)
    for i in range(block_count):
        mine = meta[2 * pairs + i : 2 * pairs + i + 1] == me
        values = jnp.where(mine, meta[i * per_block : (i + 1) * per_block], values)
        columns = jnp.where(mine, meta[pairs + i * per_block : pairs + (i + 1) * per_block], columns)
    columns = columns.astype(jnp.int32)
    cols_ref[0] = columns
    row = lax.broadcasted_iota(jnp.int32, (acts_ref.shape[0], tokens), 0)
    dense = jnp.zeros(row.shape, jnp.float32)
    for k in range(per_block):
        dense = jnp.where(row == columns[k : k + 1], values[k : k + 1], dense)
    acts_ref[...] = dense.astype(jnp.bfloat16)


def mask_kernel(per_block, products_ref, cols_ref, pre_ref, lat_ref, bias_ref):
    products = products_ref[...]
    columns = cols_ref[0]
    row = lax.broadcasted_iota(jnp.int32, products.shape, 0)
    kept = jnp.zeros(products.shape, jnp.float32)
    for k in range(per_block):
        picked = jnp.where(row == columns[k : k + 1], products, 0.0)
        lat_ref[0, k : k + 1, :] = jnp.sum(picked, axis=0, keepdims=True)
        kept = kept + picked
    pre_ref[...] = kept.astype(jnp.bfloat16)

    @pl.when(pl.program_id(0) == 0)
    def _():
        bias_ref[...] = jnp.zeros_like(bias_ref)

    bias_ref[...] += kept


def column_parts(width, row_count):
    lanes = width // BLOCK
    for parts in range(2, lanes + 1):
        if lanes % parts == 0 and row_count * (width // parts) * 2 <= PART_BYTES:
            return parts
    return lanes


def by_gather(grad_recon, inputs, decoder, owners, local_blocks, offsets, act_values):
    token_count, width = grad_recon.shape
    block_count = owners.shape[1]
    per_block = offsets.shape[2]
    latent_count = decoder.shape[0]
    peer_count = lax.axis_size("lat")
    pairs = block_count * per_block
    row_count = peer_count * token_count
    me = lax.axis_index("lat").astype(jnp.int32).reshape(1)

    own_t = owners.T
    columns_t = (local_blocks.T[:, None, :] * BLOCK + offsets.transpose(1, 2, 0)).reshape(pairs, token_count)
    acts_t = act_values.transpose(1, 2, 0).reshape(pairs, token_count)
    filler = jnp.zeros((-block_count % 16, token_count), jnp.bfloat16)
    meta = jnp.concatenate([acts_t, columns_t.astype(jnp.bfloat16), own_t.astype(jnp.bfloat16), filler], axis=0)
    meta_all = lax.all_gather(meta, "lat", axis=0)

    parts = column_parts(width, row_count)
    span = width // parts
    depth = max(1, HELD_BYTES // (row_count * span * 2))

    def gathered(rows, p, done):
        piece = rows[:, p * span : (p + 1) * span]
        if len(done) >= depth:
            piece, _ = lax.optimization_barrier((piece, done[-depth]))
        return lax.all_gather(piece, "lat", axis=0, tiled=True)

    tile = pl.BlockSpec((latent_count, token_count), lambda s: (0, s))
    picks = pl.BlockSpec((1, per_block, token_count), lambda s: (s, 0, 0))
    acts_dense, cols = pl.pallas_call(
        functools.partial(build_kernel, block_count, per_block),
        grid=(peer_count,),
        in_specs=[
            pl.BlockSpec(memory_space=pltpu.SMEM),
            pl.BlockSpec((1, meta.shape[0], token_count), lambda s: (s, 0, 0)),
        ],
        out_specs=[tile, picks],
        out_shape=[
            jax.ShapeDtypeStruct((latent_count, row_count), jnp.bfloat16),
            jax.ShapeDtypeStruct((peer_count, per_block, token_count), jnp.int32),
        ],
        name="build",
    )(me, meta_all)

    products = None
    decoder_parts = []
    for p in range(parts):
        rows = gathered(grad_recon, p, decoder_parts)
        part = lax.dot_general(
            acts_dense, rows, (((1,), (0,)), ((), ())), preferred_element_type=jnp.float32
        ).astype(jnp.bfloat16)
        term = lax.dot_general(
            decoder[:, p * span : (p + 1) * span], rows, (((1,), (1,)), ((), ())), preferred_element_type=jnp.float32
        )
        products = term if products is None else products + term
        if depth < 2 * parts:
            part, products = lax.optimization_barrier((part, products))
        decoder_parts.append(part)
    decoder_grad = jnp.concatenate(decoder_parts, axis=1)

    pre_grads, lat, bias_lanes = pl.pallas_call(
        functools.partial(mask_kernel, per_block),
        grid=(peer_count,),
        in_specs=[tile, picks],
        out_specs=[tile, picks, pl.BlockSpec((latent_count, token_count), lambda s: (0, 0))],
        out_shape=[
            jax.ShapeDtypeStruct((latent_count, row_count), jnp.bfloat16),
            jax.ShapeDtypeStruct((peer_count, per_block, token_count), jnp.float32),
            jax.ShapeDtypeStruct((latent_count, token_count), jnp.float32),
        ],
        name="mask",
    )(products, cols)
    bias_grad = jnp.sum(bias_lanes, axis=1)
    returned = lax.all_to_all(lat, "lat", split_axis=0, concat_axis=0, tiled=True)
    latent_grads = pick_returned(returned, own_t)

    encoder_parts = []
    for p in range(parts):
        rows = gathered(inputs, p, decoder_parts + encoder_parts)
        encoder_parts.append(
            lax.dot_general(rows, pre_grads, (((0,), (1,)), ((), ())), preferred_element_type=jnp.float32).astype(
                jnp.bfloat16
            )
        )
    return (decoder_grad, jnp.concatenate(encoder_parts, axis=0), bias_grad, latent_grads)


def per_device(grad_recon, *others):
    row_bytes = lax.axis_size("lat") * grad_recon.size * grad_recon.dtype.itemsize
    way = by_ring if 2 * row_bytes <= RING_BYTES and lax.axis_size("lat") % 4 == 0 else by_gather
    return way(grad_recon, *others)


def solution(mesh):
    rows = P(("groups", "lat"), None)
    entries = P(("groups", "lat"), None, None)
    return jax.shard_map(
        per_device,
        mesh=mesh,
        in_specs=(rows, rows, P("lat", None), rows, rows, entries, entries),
        out_specs=(rows, P(None, ("groups", "lat")), P(("groups", "lat")), rows),
        check_vma=False,
    )
```

```python
import functools

import jax
import jax.numpy as jnp
import numpy as np
from jax import lax
from jax.experimental import pallas as pl
from jax.experimental.pallas import tpu as pltpu
from jax.sharding import PartitionSpec as P

BLOCK = 128
PART_BYTES = 9 << 20
HELD_BYTES = 1 << 25
RING_BYTES = 1 << 26
VMEM_BYTES = 24 << 20
LAG = 4


def ring_tables(peer_count):
    chips = peer_count // 2
    ring = [chip for chip in range(chips) if chip % 2 == 0] + [chip for chip in reversed(range(chips)) if chip % 2]
    place = {chip: spot for spot, chip in enumerate(ring)}
    sources = np.zeros((peer_count, chips, 2), np.int32)
    for device in range(peer_count):
        chip, core = divmod(device, 2)
        sign = 1 - 2 * core
        for hop in range(chips):
            behind, ahead = ring[(place[chip] - sign * hop) % chips], ring[(place[chip] + sign * hop) % chips]
            sources[device, hop] = (2 * behind + core, 2 * ahead + 1 - core)
    onward = [(2 * ring[i], 2 * ring[(i + 1) % chips]) for i in range(chips)]
    onward += [(2 * ring[i] + 1, 2 * ring[(i - 1) % chips] + 1) for i in range(chips)]
    swap = [(i, i ^ 1) for i in range(peer_count)]
    backward = [(b, a) for a, b in onward]
    return sources, onward, backward, swap


def meta_kernel(owners_ref, blocks_ref, offsets_ref, values_ref, meta_ref):
    count, per_block, tokens = offsets_ref.shape
    columns = [
        (jnp.broadcast_to(blocks_ref[i : i + 1, :], (per_block, tokens)) * BLOCK + offsets_ref[i]).astype(jnp.float32)
        for i in range(count)
    ]
    values = [values_ref[i].astype(jnp.float32) for i in range(count)]
    named = [jnp.broadcast_to(owners_ref[i : i + 1, :], (per_block, tokens)) for i in range(count)]
    for owner in range(meta_ref.shape[0]):
        told_columns = jnp.full((per_block, tokens), -1.0, jnp.float32)
        told_values = jnp.zeros((per_block, tokens), jnp.float32)
        for i in range(count):
            mine = named[i] == owner
            told_columns = jnp.where(mine, columns[i], told_columns)
            told_values = jnp.where(mine, values[i], told_values)
        meta_ref[owner, :per_block, :] = told_columns.astype(jnp.bfloat16)
        meta_ref[owner, per_block:, :] = told_values.astype(jnp.bfloat16)


def grad_kernel(per_block, order_ref, meta_ref, decoder_ref, mine_ref, theirs_ref, *refs):
    total_ref, bias_ref, lat_ref, pre_ref, acts_ref, bias_sum = refs[-6:]
    first, last = len(refs) == 6, bias_ref.shape[0] == 1
    bias_sum[...] = jnp.zeros_like(bias_sum) if first else refs[1][...]
    lat_ref[...] = jnp.zeros_like(lat_ref) if first else refs[2][...]
    latents, width = decoder_ref.shape
    tokens = mine_ref.shape[0]
    span = column_span(width)
    products = jnp.zeros((latents, 2 * tokens), jnp.float32)
    for at in range(0, width, span):
        rows = jnp.concatenate([mine_ref[:, at : at + span], theirs_ref[:, at : at + span]], axis=0)
        products += lax.dot_general(
            decoder_ref[:, at : at + span], rows, (((1,), (1,)), ((), ())), preferred_element_type=jnp.float32
        )
    row = lax.broadcasted_iota(jnp.int32, (8, tokens), 0)
    for tile in range(2):
        meta = meta_ref[order_ref[tile]].astype(jnp.float32)
        columns = [jnp.broadcast_to(meta[k : k + 1], (8, tokens)).astype(jnp.int32) for k in range(per_block)]
        values = [jnp.broadcast_to(meta[per_block + k : per_block + k + 1], (8, tokens)) for k in range(per_block)]
        sums = [jnp.zeros((8, tokens), jnp.float32) for _ in range(per_block)]
        at = slice(tile * tokens, (tile + 1) * tokens)
        for block in range(0, latents, 16):
            kept_both, dense_both = [], []
            for base in (block, block + 8):
                here = products[base : base + 8, at]
                kept = jnp.zeros((8, tokens), jnp.float32)
                dense = jnp.zeros((8, tokens), jnp.float32)
                for k in range(per_block):
                    hit = columns[k] == row + base
                    picked = jnp.where(hit, here, 0.0)
                    sums[k] = sums[k] + picked
                    kept = kept + picked
                    dense = jnp.where(hit, values[k], dense)
                bias_sum[base : base + 8, :] += kept
                kept_both.append(kept)
                dense_both.append(dense)
            pre_ref[block : block + 16, at] = jnp.concatenate(kept_both, axis=0).astype(jnp.bfloat16)
            acts_ref[block : block + 16, at] = jnp.concatenate(dense_both, axis=0).astype(jnp.bfloat16)
        source = order_ref[tile]
        for k in range(per_block):
            lat_ref[source, k : k + 1, :] = jnp.sum(sums[k], axis=0, keepdims=True)
    for at in range(0, width, span):
        rows = jnp.concatenate([mine_ref[:, at : at + span], theirs_ref[:, at : at + span]], axis=0)
        term = jnp.dot(acts_ref[...], rows, preferred_element_type=jnp.float32)
        if not first:
            term += refs[0][:, at : at + span]
        total_ref[:, at : at + span] = term.astype(total_ref.dtype)
    bias_ref[...] = jnp.sum(bias_sum[...].T, axis=0, keepdims=True) if last else bias_sum[...]


def input_kernel(pre_ref, mine_ref, theirs_ref, *refs):
    total_ref = refs[-1]
    width = mine_ref.shape[1]
    span = column_span(width)
    for at in range(0, width, span):
        rows = jnp.concatenate([mine_ref[:, at : at + span], theirs_ref[:, at : at + span]], axis=0)
        term = lax.dot_general(rows, pre_ref[...], (((0,), (1,)), ((), ())), preferred_element_type=jnp.float32)
        if len(refs) == 2:
            term += refs[0][at : at + span, :]
        total_ref[at : at + span, :] = term.astype(total_ref.dtype)


def column_span(width):
    return 512 if width % 512 == 0 else BLOCK


def after(value, *others):
    return lax.optimization_barrier((value, *others))[0]


def by_ring(grad_recon, inputs, decoder, owners, local_blocks, offsets, act_values):
    token_count, width = grad_recon.shape
    block_count = owners.shape[1]
    per_block = offsets.shape[2]
    latent_count = decoder.shape[0]
    peer_count = lax.axis_size("lat")
    chips = peer_count // 2
    me = lax.axis_index("lat")
    sources, onward, backward, swap = ring_tables(peer_count)
    order = jnp.asarray(sources)[me]
    own_t = owners.T
    whole = pl.BlockSpec(memory_space=pltpu.VMEM)
    scalars = pl.BlockSpec(memory_space=pltpu.SMEM)
    step_tokens = 2 * token_count
    light = pl.CostEstimate(flops=1, bytes_accessed=1, transcendentals=0)
    params = pltpu.CompilerParams(vmem_limit_bytes=VMEM_BYTES)

    meta = pl.pallas_call(
        meta_kernel,
        in_specs=[whole] * 4,
        out_specs=whole,
        out_shape=jax.ShapeDtypeStruct((peer_count, 2 * per_block, token_count), jnp.bfloat16),
        compiler_params=params,
        cost_estimate=light,
        name="meta",
    )(own_t, local_blocks.T, offsets.transpose(1, 2, 0), act_values.transpose(1, 2, 0))
    meta = lax.all_to_all(meta, "lat", split_axis=0, concat_axis=0, tiled=True)

    def near(value):
        return pltpu.with_memory_space_constraint(value, pltpu.VMEM)

    def grad_step(hop, rows, totals, last):
        sums, lanes = (latent_count, width), (latent_count, token_count)
        return pl.pallas_call(
            functools.partial(grad_kernel, per_block),
            in_specs=[scalars] + [whole] * (4 + len(totals)),
            out_specs=[whole] * 4,
            out_shape=[
                jax.ShapeDtypeStruct(sums, jnp.bfloat16) if last else pltpu.VMEM(sums, jnp.float32),
                jax.ShapeDtypeStruct((1, latent_count), jnp.float32) if last else pltpu.VMEM(lanes, jnp.float32),
                jax.ShapeDtypeStruct((peer_count, per_block, token_count), jnp.float32),
                pltpu.VMEM((latent_count, step_tokens), jnp.bfloat16),
            ],
            scratch_shapes=[
                pltpu.VMEM((latent_count, step_tokens), jnp.bfloat16),
                pltpu.VMEM(lanes, jnp.float32),
            ],
            input_output_aliases={} if last or not totals else {5: 0, 6: 1},
            compiler_params=params,
            cost_estimate=light,
            name="grad_step",
        )(order[hop], near(meta), near(decoder), near(rows[0]), near(rows[1]), *map(near, totals))

    def input_step(pre, rows, total, last):
        sums = (width, latent_count)
        totals = () if total is None else (total,)
        return pl.pallas_call(
            input_kernel,
            in_specs=[whole] * (3 + len(totals)),
            out_specs=whole,
            out_shape=jax.ShapeDtypeStruct(sums, jnp.bfloat16) if last else pltpu.VMEM(sums, jnp.float32),
            input_output_aliases={3: 0} if totals and not last else {},
            compiler_params=params,
            cost_estimate=light,
            name="input_step",
        )(near(pre), near(rows[0]), near(rows[1]), *map(near, totals))

    def send(rows, way, *first):
        return lax.ppermute(after(rows, *first) if first else rows, "lat", way)

    half = chips // 2
    later = [("inputs", 1)]
    for hop in range(1, half):
        later += [("inputs", hop + 1), ("inputs", -hop)]
    turns = []
    for hop in range(1, half + 1):
        turns += [("grads", hop)] + ([("grads", -hop)] if hop < half else []) + [later.pop(0)]
    turns += later
    pres, totals, encoder_grad = {}, (), None

    def use(kind, hop, rows, last=False):
        nonlocal totals, encoder_grad
        if kind == "grads":
            *totals, pres[hop] = grad_step(hop, rows, totals, last)
            return totals[1]
        encoder_grad = input_step(pres[hop], rows, encoder_grad, last)
        return encoder_grad

    held = {(kind, way): rows for kind, rows in (("grads", grad_recon), ("inputs", inputs)) for way in (True, False)}
    own_grads, own_inputs = send(grad_recon, swap), send(inputs, swap, meta)
    marks = []
    last_grads = max(turn for turn, (kind, _) in enumerate(turns) if kind == "grads")
    returned = None

    def arrive(turn):
        nonlocal returned
        kind, hop = turns[turn]
        last = turn in (last_grads, len(turns) - 1)
        ready = (meta,) if turn < 2 else (marks[turn - 2],)
        if turn == len(turns) - 1:
            ready += (returned,)
        marks.append(use(kind, hop % chips, (arrived[turn], send(arrived[turn], swap, *ready)), last))
        if turn == last_grads:
            returned = lax.all_to_all(totals[2], "lat", split_axis=0, concat_axis=0, tiled=True)

    use("grads", 0, (grad_recon, own_grads))
    use("inputs", 0, (inputs, own_inputs))
    arrived = []
    for turn, (kind, hop) in enumerate(turns):
        if turn >= LAG:
            arrive(turn - LAG)
        ready = () if turn < 3 else (meta,) if turn < LAG else (marks[turn - LAG],)
        rows = send(held[kind, hop > 0], onward if hop > 0 else backward, *ready)
        held[kind, hop > 0] = rows
        arrived.append(rows)
    for turn in range(len(turns) - LAG, len(turns)):
        arrive(turn)
    latent_grads = pick_returned(after(returned, encoder_grad), own_t)
    return (totals[0], encoder_grad, totals[1].reshape(latent_count), latent_grads)


def pick_returned(returned, own_t):
    owner_id = jnp.arange(returned.shape[0], dtype=jnp.int32)[:, None, None, None]
    picked = jnp.where(own_t[None, :, None, :] == owner_id, returned[:, None, :, :], 0.0)
    return jnp.sum(picked, axis=0).reshape(-1, own_t.shape[1]).T


def build_kernel(block_count, per_block, me_ref, meta_ref, acts_ref, cols_ref):
    pairs = block_count * per_block
    meta = meta_ref[0].astype(jnp.float32)
    me = me_ref[0].astype(jnp.float32)
    tokens = meta.shape[1]
    values = jnp.zeros((per_block, tokens), jnp.float32)
    columns = jnp.full((per_block, tokens), -1.0, jnp.float32)
    for i in range(block_count):
        mine = meta[2 * pairs + i : 2 * pairs + i + 1] == me
        values = jnp.where(mine, meta[i * per_block : (i + 1) * per_block], values)
        columns = jnp.where(mine, meta[pairs + i * per_block : pairs + (i + 1) * per_block], columns)
    columns = columns.astype(jnp.int32)
    cols_ref[0] = columns
    row = lax.broadcasted_iota(jnp.int32, (acts_ref.shape[0], tokens), 0)
    dense = jnp.zeros(row.shape, jnp.float32)
    for k in range(per_block):
        dense = jnp.where(row == columns[k : k + 1], values[k : k + 1], dense)
    acts_ref[...] = dense.astype(jnp.bfloat16)


def mask_kernel(per_block, products_ref, cols_ref, pre_ref, lat_ref, bias_ref):
    products = products_ref[...]
    columns = cols_ref[0]
    row = lax.broadcasted_iota(jnp.int32, products.shape, 0)
    kept = jnp.zeros(products.shape, jnp.float32)
    for k in range(per_block):
        picked = jnp.where(row == columns[k : k + 1], products, 0.0)
        lat_ref[0, k : k + 1, :] = jnp.sum(picked, axis=0, keepdims=True)
        kept = kept + picked
    pre_ref[...] = kept.astype(jnp.bfloat16)

    @pl.when(pl.program_id(0) == 0)
    def _():
        bias_ref[...] = jnp.zeros_like(bias_ref)

    bias_ref[...] += kept


def column_parts(width, row_count):
    lanes = width // BLOCK
    for parts in range(2, lanes + 1):
        if lanes % parts == 0 and row_count * (width // parts) * 2 <= PART_BYTES:
            return parts
    return lanes


def by_gather(grad_recon, inputs, decoder, owners, local_blocks, offsets, act_values):
    token_count, width = grad_recon.shape
    block_count = owners.shape[1]
    per_block = offsets.shape[2]
    latent_count = decoder.shape[0]
    peer_count = lax.axis_size("lat")
    pairs = block_count * per_block
    row_count = peer_count * token_count
    me = lax.axis_index("lat").astype(jnp.int32).reshape(1)

    own_t = owners.T
    columns_t = (local_blocks.T[:, None, :] * BLOCK + offsets.transpose(1, 2, 0)).reshape(pairs, token_count)
    acts_t = act_values.transpose(1, 2, 0).reshape(pairs, token_count)
    filler = jnp.zeros((-block_count % 16, token_count), jnp.bfloat16)
    meta = jnp.concatenate([acts_t, columns_t.astype(jnp.bfloat16), own_t.astype(jnp.bfloat16), filler], axis=0)
    meta_all = lax.all_gather(meta, "lat", axis=0)

    parts = column_parts(width, row_count)
    span = width // parts
    depth = max(1, HELD_BYTES // (row_count * span * 2))

    def gathered(rows, p, done):
        piece = rows[:, p * span : (p + 1) * span]
        if len(done) >= depth:
            piece, _ = lax.optimization_barrier((piece, done[-depth]))
        return lax.all_gather(piece, "lat", axis=0, tiled=True)

    tile = pl.BlockSpec((latent_count, token_count), lambda s: (0, s))
    picks = pl.BlockSpec((1, per_block, token_count), lambda s: (s, 0, 0))
    acts_dense, cols = pl.pallas_call(
        functools.partial(build_kernel, block_count, per_block),
        grid=(peer_count,),
        in_specs=[
            pl.BlockSpec(memory_space=pltpu.SMEM),
            pl.BlockSpec((1, meta.shape[0], token_count), lambda s: (s, 0, 0)),
        ],
        out_specs=[tile, picks],
        out_shape=[
            jax.ShapeDtypeStruct((latent_count, row_count), jnp.bfloat16),
            jax.ShapeDtypeStruct((peer_count, per_block, token_count), jnp.int32),
        ],
        name="build",
    )(me, meta_all)

    products = None
    decoder_parts = []
    for p in range(parts):
        rows = gathered(grad_recon, p, decoder_parts)
        part = lax.dot_general(
            acts_dense, rows, (((1,), (0,)), ((), ())), preferred_element_type=jnp.float32
        ).astype(jnp.bfloat16)
        term = lax.dot_general(
            decoder[:, p * span : (p + 1) * span], rows, (((1,), (1,)), ((), ())), preferred_element_type=jnp.float32
        )
        products = term if products is None else products + term
        if depth < 2 * parts:
            part, products = lax.optimization_barrier((part, products))
        decoder_parts.append(part)
    decoder_grad = jnp.concatenate(decoder_parts, axis=1)

    pre_grads, lat, bias_lanes = pl.pallas_call(
        functools.partial(mask_kernel, per_block),
        grid=(peer_count,),
        in_specs=[tile, picks],
        out_specs=[tile, picks, pl.BlockSpec((latent_count, token_count), lambda s: (0, 0))],
        out_shape=[
            jax.ShapeDtypeStruct((latent_count, row_count), jnp.bfloat16),
            jax.ShapeDtypeStruct((peer_count, per_block, token_count), jnp.float32),
            jax.ShapeDtypeStruct((latent_count, token_count), jnp.float32),
        ],
        name="mask",
    )(products, cols)
    bias_grad = jnp.sum(bias_lanes, axis=1)
    returned = lax.all_to_all(lat, "lat", split_axis=0, concat_axis=0, tiled=True)
    latent_grads = pick_returned(returned, own_t)

    encoder_parts = []
    for p in range(parts):
        rows = gathered(inputs, p, decoder_parts + encoder_parts)
        encoder_parts.append(
            lax.dot_general(rows, pre_grads, (((0,), (1,)), ((), ())), preferred_element_type=jnp.float32).astype(
                jnp.bfloat16
            )
        )
    return (decoder_grad, jnp.concatenate(encoder_parts, axis=0), bias_grad, latent_grads)


def per_device(grad_recon, *others):
    row_bytes = lax.axis_size("lat") * grad_recon.size * grad_recon.dtype.itemsize
    way = by_ring if 2 * row_bytes <= RING_BYTES and lax.axis_size("lat") % 4 == 0 else by_gather
    return way(grad_recon, *others)


def solution(mesh):
    rows = P(("groups", "lat"), None)
    entries = P(("groups", "lat"), None, None)
    return jax.shard_map(
        per_device,
        mesh=mesh,
        in_specs=(rows, rows, P("lat", None), rows, rows, entries, entries),
        out_specs=(rows, P(None, ("groups", "lat")), P(("groups", "lat")), rows),
        check_vma=False,
    )
```

```python
import functools

import jax
import jax.numpy as jnp
import numpy as np
from jax import lax
from jax.experimental import pallas as pl
from jax.experimental.pallas import tpu as pltpu
from jax.sharding import PartitionSpec as P

BLOCK = 128
PART_BYTES = 9 << 20
HELD_BYTES = 1 << 25
RING_BYTES = 1 << 26
VMEM_BYTES = 24 << 20


def ring_tables(peer_count):
    chips = peer_count // 2
    ring = [chip for chip in range(chips) if chip % 2 == 0] + [chip for chip in reversed(range(chips)) if chip % 2]
    place = {chip: spot for spot, chip in enumerate(ring)}
    sources = np.zeros((peer_count, chips, 2), np.int32)
    for device in range(peer_count):
        chip, core = divmod(device, 2)
        sign = 1 - 2 * core
        for hop in range(chips):
            behind, ahead = ring[(place[chip] - sign * hop) % chips], ring[(place[chip] + sign * hop) % chips]
            sources[device, hop] = (2 * behind + core, 2 * ahead + 1 - core)
    onward = [(2 * ring[i], 2 * ring[(i + 1) % chips]) for i in range(chips)]
    onward += [(2 * ring[i] + 1, 2 * ring[(i - 1) % chips] + 1) for i in range(chips)]
    swap = [(i, i ^ 1) for i in range(peer_count)]
    backward = [(b, a) for a, b in onward]
    target = dict(onward)
    second = [(a, target[b]) for a, b in onward]
    across = [(b, a ^ 1) for a, b in second]
    return sources, onward, backward, swap, second, across


def meta_kernel(owners_ref, blocks_ref, offsets_ref, values_ref, meta_ref):
    count, per_block, tokens = offsets_ref.shape
    columns = [
        (jnp.broadcast_to(blocks_ref[i : i + 1, :], (per_block, tokens)) * BLOCK + offsets_ref[i]).astype(jnp.float32)
        for i in range(count)
    ]
    values = [values_ref[i].astype(jnp.float32) for i in range(count)]
    named = [jnp.broadcast_to(owners_ref[i : i + 1, :], (per_block, tokens)) for i in range(count)]
    for owner in range(meta_ref.shape[0]):
        told_columns = jnp.full((per_block, tokens), -1.0, jnp.float32)
        told_values = jnp.zeros((per_block, tokens), jnp.float32)
        for i in range(count):
            mine = named[i] == owner
            told_columns = jnp.where(mine, columns[i], told_columns)
            told_values = jnp.where(mine, values[i], told_values)
        meta_ref[owner, :per_block, :] = told_columns.astype(jnp.bfloat16)
        meta_ref[owner, per_block:, :] = told_values.astype(jnp.bfloat16)


def grad_kernel(per_block, order_ref, meta_ref, decoder_ref, mine_ref, theirs_ref, *refs):
    total_ref, bias_ref, lat_ref, pre_ref, acts_ref, bias_sum = refs[-6:]
    first, last = len(refs) == 6, bias_ref.shape[0] == 1
    bias_sum[...] = jnp.zeros_like(bias_sum) if first else refs[1][...]
    if not last:
        lat_ref[...] = jnp.zeros_like(lat_ref) if first else refs[2][...]
    latents, width = decoder_ref.shape
    tokens = mine_ref.shape[0]
    span = column_span(width)
    products = jnp.zeros((latents, 2 * tokens), jnp.float32)
    for at in range(0, width, span):
        rows = jnp.concatenate([mine_ref[:, at : at + span], theirs_ref[:, at : at + span]], axis=0)
        products += lax.dot_general(
            decoder_ref[:, at : at + span], rows, (((1,), (1,)), ((), ())), preferred_element_type=jnp.float32
        )
    row = lax.broadcasted_iota(jnp.int32, (8, tokens), 0)
    for tile in range(2):
        meta = meta_ref[order_ref[tile]].astype(jnp.float32)
        columns = [jnp.broadcast_to(meta[k : k + 1], (8, tokens)).astype(jnp.int32) for k in range(per_block)]
        values = [jnp.broadcast_to(meta[per_block + k : per_block + k + 1], (8, tokens)) for k in range(per_block)]
        sums = [jnp.zeros((8, tokens), jnp.float32) for _ in range(per_block)]
        at = slice(tile * tokens, (tile + 1) * tokens)
        for block in range(0, latents, 16):
            kept_both, dense_both = [], []
            for base in (block, block + 8):
                here = products[base : base + 8, at]
                kept = jnp.zeros((8, tokens), jnp.float32)
                dense = jnp.zeros((8, tokens), jnp.float32)
                for k in range(per_block):
                    hit = columns[k] == row + base
                    picked = jnp.where(hit, here, 0.0)
                    sums[k] = sums[k] + picked
                    kept = kept + picked
                    dense = jnp.where(hit, values[k], dense)
                bias_sum[base : base + 8, :] += kept
                kept_both.append(kept)
                dense_both.append(dense)
            pre_ref[block : block + 16, at] = jnp.concatenate(kept_both, axis=0).astype(jnp.bfloat16)
            acts_ref[block : block + 16, at] = jnp.concatenate(dense_both, axis=0).astype(jnp.bfloat16)
        source = tile if last else order_ref[tile]
        for k in range(per_block):
            lat_ref[source, k : k + 1, :] = jnp.sum(sums[k], axis=0, keepdims=True)
    for at in range(0, width, span):
        rows = jnp.concatenate([mine_ref[:, at : at + span], theirs_ref[:, at : at + span]], axis=0)
        term = jnp.dot(acts_ref[...], rows, preferred_element_type=jnp.float32)
        if not first:
            term += refs[0][:, at : at + span]
        total_ref[:, at : at + span] = term.astype(total_ref.dtype)
    bias_ref[...] = jnp.sum(bias_sum[...].T, axis=0, keepdims=True) if last else bias_sum[...]


def input_kernel(pre_ref, mine_ref, theirs_ref, *refs):
    total_ref = refs[-1]
    width = mine_ref.shape[1]
    span = column_span(width)
    for at in range(0, width, span):
        rows = jnp.concatenate([mine_ref[:, at : at + span], theirs_ref[:, at : at + span]], axis=0)
        term = lax.dot_general(rows, pre_ref[...], (((0,), (1,)), ((), ())), preferred_element_type=jnp.float32)
        if len(refs) == 2:
            term += refs[0][at : at + span, :]
        total_ref[at : at + span, :] = term.astype(total_ref.dtype)


def column_span(width):
    return 512 if width % 512 == 0 else BLOCK


def after(value, *others):
    return lax.optimization_barrier((value, *others))[0]


def by_ring(grad_recon, inputs, decoder, owners, local_blocks, offsets, act_values):
    token_count, width = grad_recon.shape
    block_count = owners.shape[1]
    per_block = offsets.shape[2]
    latent_count = decoder.shape[0]
    peer_count = lax.axis_size("lat")
    chips = peer_count // 2
    me = lax.axis_index("lat")
    sources, onward, backward, swap, second, across = ring_tables(peer_count)
    order = jnp.asarray(sources)[me]
    own_t = owners.T
    whole = pl.BlockSpec(memory_space=pltpu.VMEM)
    scalars = pl.BlockSpec(memory_space=pltpu.SMEM)
    step_tokens = 2 * token_count
    light = pl.CostEstimate(flops=1, bytes_accessed=1, transcendentals=0)
    params = pltpu.CompilerParams(vmem_limit_bytes=VMEM_BYTES)

    meta = pl.pallas_call(
        meta_kernel,
        in_specs=[whole] * 4,
        out_specs=whole,
        out_shape=jax.ShapeDtypeStruct((peer_count, 2 * per_block, token_count), jnp.bfloat16),
        compiler_params=params,
        cost_estimate=light,
        name="meta",
    )(own_t, local_blocks.T, offsets.transpose(1, 2, 0), act_values.transpose(1, 2, 0))
    meta = lax.all_to_all(meta, "lat", split_axis=0, concat_axis=0, tiled=True)

    def near(value):
        return pltpu.with_memory_space_constraint(value, pltpu.VMEM)

    def grad_step(hop, rows, totals, last):
        sums, lanes = (latent_count, width), (latent_count, token_count)
        lat = (2 if last else peer_count, per_block, token_count)
        return pl.pallas_call(
            functools.partial(grad_kernel, per_block),
            in_specs=[scalars] + [whole] * (4 + len(totals)),
            out_specs=[whole] * 4,
            out_shape=[
                jax.ShapeDtypeStruct(sums, jnp.bfloat16) if last else pltpu.VMEM(sums, jnp.float32),
                jax.ShapeDtypeStruct((1, latent_count), jnp.float32) if last else pltpu.VMEM(lanes, jnp.float32),
                jax.ShapeDtypeStruct(lat, jnp.float32),
                pltpu.VMEM((latent_count, step_tokens), jnp.bfloat16),
            ],
            scratch_shapes=[
                pltpu.VMEM((latent_count, step_tokens), jnp.bfloat16),
                pltpu.VMEM(lanes, jnp.float32),
            ],
            input_output_aliases={} if last or not totals else {5: 0, 6: 1},
            compiler_params=params,
            cost_estimate=light,
            name="grad_step",
        )(order[hop], near(meta), near(decoder), near(rows[0]), near(rows[1]), *map(near, totals))

    def input_step(pre, rows, total, last):
        sums = (width, latent_count)
        totals = () if total is None else (total,)
        return pl.pallas_call(
            input_kernel,
            in_specs=[whole] * (3 + len(totals)),
            out_specs=whole,
            out_shape=jax.ShapeDtypeStruct(sums, jnp.bfloat16) if last else pltpu.VMEM(sums, jnp.float32),
            input_output_aliases={3: 0} if totals and not last else {},
            compiler_params=params,
            cost_estimate=light,
            name="input_step",
        )(near(pre), near(rows[0]), near(rows[1]), *map(near, totals))

    def send(rows, way, *first):
        return lax.ppermute(after(rows, *first) if first else rows, "lat", way)

    final, back = chips - 2, chips - 1
    pres, totals, encoder_grad = {}, (), None

    def use_grads(hop, rows, last=False):
        nonlocal totals
        *totals, pres[hop] = grad_step(hop, rows, totals, last)

    def use_inputs(hop, rows, last=False):
        nonlocal encoder_grad
        encoder_grad = input_step(pres[hop], rows, encoder_grad, last)

    grad, grad_back = send(grad_recon, onward), send(grad_recon, backward)
    inward, input_back = send(inputs, onward), send(inputs, backward)
    own_theirs = send(grad_recon, swap)
    meta = after(meta, grad, grad_back, inward)
    grad_next = send(grad, onward)
    use_grads(0, (grad_recon, own_theirs))
    input_next = send(inward, onward, totals[1])
    use_grads(1, (grad, send(grad, swap)))
    use_grads(back, (grad_back, send(grad_back, swap)))
    use_inputs(0, (inputs, send(inputs, swap)))
    use_inputs(1, (inward, send(inward, swap)))
    use_inputs(back, (input_back, send(input_back, swap)))
    grad, inward = grad_next, input_next
    grad_next = send(grad, onward, totals[1])
    for hop in range(2, final):
        use_grads(hop, (grad, send(grad, swap)))
        input_next = send(inward, onward, totals[1])
        use_inputs(hop, (inward, send(inward, swap)))
        grad, inward = grad_next, input_next
        if hop < final - 1:
            grad_next = send(grad, onward, encoder_grad)
    returned = lax.all_to_all(totals[2], "lat", split_axis=0, concat_axis=0, tiled=True)
    totals = totals[:2]
    use_grads(final, (grad, send(grad, swap)), True)
    use_inputs(final, (inward, send(inward, swap, returned)), True)
    lat = totals[2]
    sent_back = lax.ppermute(lat[0], "lat", second), lax.ppermute(lat[1], "lat", across)
    nearest = jnp.asarray(sources)[me, 2, 0]
    latent_grads = pick_returned(returned, own_t, (nearest, nearest ^ 1), sent_back)
    return (totals[0], encoder_grad, totals[1].reshape(latent_count), latent_grads)


def pick_returned(returned, own_t, more_owners=(), more=()):
    owner_id = jnp.arange(returned.shape[0], dtype=jnp.int32)[:, None, None, None]
    picked = jnp.sum(jnp.where(own_t[None, :, None, :] == owner_id, returned[:, None, :, :], 0.0), axis=0)
    for owner, sent_back in zip(more_owners, more):
        picked += jnp.where(own_t[:, None, :] == owner, sent_back[None], 0.0)
    return picked.reshape(-1, own_t.shape[1]).T


def build_kernel(block_count, per_block, me_ref, meta_ref, acts_ref, cols_ref):
    pairs = block_count * per_block
    meta = meta_ref[0].astype(jnp.float32)
    me = me_ref[0].astype(jnp.float32)
    tokens = meta.shape[1]
    values = jnp.zeros((per_block, tokens), jnp.float32)
    columns = jnp.full((per_block, tokens), -1.0, jnp.float32)
    for i in range(block_count):
        mine = meta[2 * pairs + i : 2 * pairs + i + 1] == me
        values = jnp.where(mine, meta[i * per_block : (i + 1) * per_block], values)
        columns = jnp.where(mine, meta[pairs + i * per_block : pairs + (i + 1) * per_block], columns)
    columns = columns.astype(jnp.int32)
    cols_ref[0] = columns
    row = lax.broadcasted_iota(jnp.int32, (acts_ref.shape[0], tokens), 0)
    dense = jnp.zeros(row.shape, jnp.float32)
    for k in range(per_block):
        dense = jnp.where(row == columns[k : k + 1], values[k : k + 1], dense)
    acts_ref[...] = dense.astype(jnp.bfloat16)


def mask_kernel(per_block, products_ref, cols_ref, pre_ref, lat_ref, bias_ref):
    products = products_ref[...]
    columns = cols_ref[0]
    row = lax.broadcasted_iota(jnp.int32, products.shape, 0)
    kept = jnp.zeros(products.shape, jnp.float32)
    for k in range(per_block):
        picked = jnp.where(row == columns[k : k + 1], products, 0.0)
        lat_ref[0, k : k + 1, :] = jnp.sum(picked, axis=0, keepdims=True)
        kept = kept + picked
    pre_ref[...] = kept.astype(jnp.bfloat16)

    @pl.when(pl.program_id(0) == 0)
    def _():
        bias_ref[...] = jnp.zeros_like(bias_ref)

    bias_ref[...] += kept


def column_parts(width, row_count):
    lanes = width // BLOCK
    for parts in range(2, lanes + 1):
        if lanes % parts == 0 and row_count * (width // parts) * 2 <= PART_BYTES:
            return parts
    return lanes


def by_gather(grad_recon, inputs, decoder, owners, local_blocks, offsets, act_values):
    token_count, width = grad_recon.shape
    block_count = owners.shape[1]
    per_block = offsets.shape[2]
    latent_count = decoder.shape[0]
    peer_count = lax.axis_size("lat")
    pairs = block_count * per_block
    row_count = peer_count * token_count
    me = lax.axis_index("lat").astype(jnp.int32).reshape(1)

    own_t = owners.T
    columns_t = (local_blocks.T[:, None, :] * BLOCK + offsets.transpose(1, 2, 0)).reshape(pairs, token_count)
    acts_t = act_values.transpose(1, 2, 0).reshape(pairs, token_count)
    filler = jnp.zeros((-block_count % 16, token_count), jnp.bfloat16)
    meta = jnp.concatenate([acts_t, columns_t.astype(jnp.bfloat16), own_t.astype(jnp.bfloat16), filler], axis=0)
    meta_all = lax.all_gather(meta, "lat", axis=0)

    parts = column_parts(width, row_count)
    span = width // parts
    depth = max(1, HELD_BYTES // (row_count * span * 2))

    def gathered(rows, p, done):
        piece = rows[:, p * span : (p + 1) * span]
        if len(done) >= depth:
            piece, _ = lax.optimization_barrier((piece, done[-depth]))
        return lax.all_gather(piece, "lat", axis=0, tiled=True)

    tile = pl.BlockSpec((latent_count, token_count), lambda s: (0, s))
    picks = pl.BlockSpec((1, per_block, token_count), lambda s: (s, 0, 0))
    acts_dense, cols = pl.pallas_call(
        functools.partial(build_kernel, block_count, per_block),
        grid=(peer_count,),
        in_specs=[
            pl.BlockSpec(memory_space=pltpu.SMEM),
            pl.BlockSpec((1, meta.shape[0], token_count), lambda s: (s, 0, 0)),
        ],
        out_specs=[tile, picks],
        out_shape=[
            jax.ShapeDtypeStruct((latent_count, row_count), jnp.bfloat16),
            jax.ShapeDtypeStruct((peer_count, per_block, token_count), jnp.int32),
        ],
        name="build",
    )(me, meta_all)

    products = None
    decoder_parts = []
    for p in range(parts):
        rows = gathered(grad_recon, p, decoder_parts)
        part = lax.dot_general(
            acts_dense, rows, (((1,), (0,)), ((), ())), preferred_element_type=jnp.float32
        ).astype(jnp.bfloat16)
        term = lax.dot_general(
            decoder[:, p * span : (p + 1) * span], rows, (((1,), (1,)), ((), ())), preferred_element_type=jnp.float32
        )
        products = term if products is None else products + term
        if depth < 2 * parts:
            part, products = lax.optimization_barrier((part, products))
        decoder_parts.append(part)
    decoder_grad = jnp.concatenate(decoder_parts, axis=1)

    pre_grads, lat, bias_lanes = pl.pallas_call(
        functools.partial(mask_kernel, per_block),
        grid=(peer_count,),
        in_specs=[tile, picks],
        out_specs=[tile, picks, pl.BlockSpec((latent_count, token_count), lambda s: (0, 0))],
        out_shape=[
            jax.ShapeDtypeStruct((latent_count, row_count), jnp.bfloat16),
            jax.ShapeDtypeStruct((peer_count, per_block, token_count), jnp.float32),
            jax.ShapeDtypeStruct((latent_count, token_count), jnp.float32),
        ],
        name="mask",
    )(products, cols)
    bias_grad = jnp.sum(bias_lanes, axis=1)
    returned = lax.all_to_all(lat, "lat", split_axis=0, concat_axis=0, tiled=True)
    latent_grads = pick_returned(returned, own_t)

    encoder_parts = []
    for p in range(parts):
        rows = gathered(inputs, p, decoder_parts + encoder_parts)
        encoder_parts.append(
            lax.dot_general(rows, pre_grads, (((0,), (1,)), ((), ())), preferred_element_type=jnp.float32).astype(
                jnp.bfloat16
            )
        )
    return (decoder_grad, jnp.concatenate(encoder_parts, axis=0), bias_grad, latent_grads)


def per_device(grad_recon, *others):
    row_bytes = lax.axis_size("lat") * grad_recon.size * grad_recon.dtype.itemsize
    way = by_ring if 2 * row_bytes <= RING_BYTES and lax.axis_size("lat") % 4 == 0 else by_gather
    return way(grad_recon, *others)


def solution(mesh):
    rows = P(("groups", "lat"), None)
    entries = P(("groups", "lat"), None, None)
    return jax.shard_map(
        per_device,
        mesh=mesh,
        in_specs=(rows, rows, P("lat", None), rows, rows, entries, entries),
        out_specs=(rows, P(None, ("groups", "lat")), P(("groups", "lat")), rows),
        check_vma=False,
    )
```

```python
import functools

import jax
import jax.numpy as jnp
import numpy as np
from jax import lax
from jax.experimental import pallas as pl
from jax.experimental.pallas import tpu as pltpu
from jax.sharding import PartitionSpec as P

BLOCK = 128
PART_BYTES = 9 << 20
HELD_BYTES = 1 << 25
RING_BYTES = 1 << 26
VMEM_BYTES = 24 << 20
LAG = 4


def ring_tables(peer_count):
    chips = peer_count // 2
    ring = [chip for chip in range(chips) if chip % 2 == 0] + [chip for chip in reversed(range(chips)) if chip % 2]
    place = {chip: spot for spot, chip in enumerate(ring)}
    sources = np.zeros((peer_count, chips, 2), np.int32)
    for device in range(peer_count):
        chip, core = divmod(device, 2)
        sign = 1 - 2 * core
        for hop in range(chips):
            behind, ahead = ring[(place[chip] - sign * hop) % chips], ring[(place[chip] + sign * hop) % chips]
            sources[device, hop] = (2 * behind + core, 2 * ahead + 1 - core)
    onward = [(2 * ring[i], 2 * ring[(i + 1) % chips]) for i in range(chips)]
    onward += [(2 * ring[i] + 1, 2 * ring[(i - 1) % chips] + 1) for i in range(chips)]
    swap = [(i, i ^ 1) for i in range(peer_count)]
    backward = [(b, a) for a, b in onward]
    return sources, onward, backward, swap


def extend_kernel(rows_ref, owners_ref, blocks_ref, offsets_ref, values_ref, out_ref):
    width = rows_ref.shape[1]
    count, per_block, tokens = offsets_ref.shape
    pairs = count * per_block
    out_ref[:, :width] = rows_ref[...]
    out_ref[:, width:] = jnp.zeros((out_ref.shape[0], out_ref.shape[1] - width), jnp.bfloat16)
    for i in range(count):
        at = slice(i * per_block, (i + 1) * per_block)
        columns = jnp.broadcast_to(blocks_ref[i : i + 1, :], (per_block, tokens)) * BLOCK + offsets_ref[i]
        out_ref[at, width : width + tokens] = columns.astype(jnp.float32).astype(jnp.bfloat16)
        out_ref[pairs + at.start : pairs + at.stop, width : width + tokens] = values_ref[i]
    named = jnp.concatenate([owners_ref[...], jnp.zeros((16 - count, tokens), jnp.int32)], axis=0)
    out_ref[:16, width + tokens :] = named.astype(jnp.float32).astype(jnp.bfloat16)


def grad_kernel(count, per_block, order_ref, decoder_ref, mine_ref, theirs_ref, *refs):
    total_ref, bias_ref, lat_ref, pre_ref, acts_ref, bias_sum = refs[-6:]
    first, last = len(refs) == 6, bias_ref.shape[0] == 1
    bias_sum[...] = jnp.zeros_like(bias_sum) if first else refs[1][...]
    lat_ref[...] = jnp.zeros_like(lat_ref) if first else refs[2][...]
    latents, width = decoder_ref.shape
    tokens = mine_ref.shape[0]
    span = column_span(width)
    products = jnp.zeros((latents, 2 * tokens), jnp.float32)
    for at in range(0, width, span):
        rows = jnp.concatenate([mine_ref[:, at : at + span], theirs_ref[:, at : at + span]], axis=0)
        products += lax.dot_general(
            decoder_ref[:, at : at + span], rows, (((1,), (1,)), ((), ())), preferred_element_type=jnp.float32
        )
    row = lax.broadcasted_iota(jnp.int32, (8, tokens), 0)
    for tile in range(2):
        entries = (mine_ref, theirs_ref)[tile][:, width : width + tokens].astype(jnp.float32)
        named = (mine_ref, theirs_ref)[tile][:16, width + tokens :].astype(jnp.float32).astype(jnp.int32)
        told_columns = jnp.full((per_block, tokens), -1.0, jnp.float32)
        told_values = jnp.zeros((per_block, tokens), jnp.float32)
        for i in range(count):
            own = jnp.broadcast_to(named[i : i + 1], (per_block, tokens)) == order_ref[2]
            told_columns = jnp.where(own, entries[i * per_block : (i + 1) * per_block], told_columns)
            told_values = jnp.where(own, entries[(count + i) * per_block : (count + i + 1) * per_block], told_values)
        columns = [jnp.broadcast_to(told_columns[k : k + 1], (8, tokens)).astype(jnp.int32) for k in range(per_block)]
        values = [jnp.broadcast_to(told_values[k : k + 1], (8, tokens)) for k in range(per_block)]
        sums = [jnp.zeros((8, tokens), jnp.float32) for _ in range(per_block)]
        at = slice(tile * tokens, (tile + 1) * tokens)
        for block in range(0, latents, 16):
            kept_both, dense_both = [], []
            for base in (block, block + 8):
                here = products[base : base + 8, at]
                kept = jnp.zeros((8, tokens), jnp.float32)
                dense = jnp.zeros((8, tokens), jnp.float32)
                for k in range(per_block):
                    hit = columns[k] == row + base
                    picked = jnp.where(hit, here, 0.0)
                    sums[k] = sums[k] + picked
                    kept = kept + picked
                    dense = jnp.where(hit, values[k], dense)
                bias_sum[base : base + 8, :] += kept
                kept_both.append(kept)
                dense_both.append(dense)
            pre_ref[block : block + 16, at] = jnp.concatenate(kept_both, axis=0).astype(jnp.bfloat16)
            acts_ref[block : block + 16, at] = jnp.concatenate(dense_both, axis=0).astype(jnp.bfloat16)
        source = order_ref[tile]
        for k in range(per_block):
            lat_ref[source, k : k + 1, :] = jnp.sum(sums[k], axis=0, keepdims=True)
    for at in range(0, width, span):
        rows = jnp.concatenate([mine_ref[:, at : at + span], theirs_ref[:, at : at + span]], axis=0)
        term = jnp.dot(acts_ref[...], rows, preferred_element_type=jnp.float32)
        if not first:
            term += refs[0][:, at : at + span]
        total_ref[:, at : at + span] = term.astype(total_ref.dtype)
    bias_ref[...] = jnp.sum(bias_sum[...].T, axis=0, keepdims=True) if last else bias_sum[...]


def input_kernel(pre_ref, mine_ref, theirs_ref, *refs):
    total_ref = refs[-1]
    width = mine_ref.shape[1]
    span = column_span(width)
    for at in range(0, width, span):
        rows = jnp.concatenate([mine_ref[:, at : at + span], theirs_ref[:, at : at + span]], axis=0)
        term = lax.dot_general(rows, pre_ref[...], (((0,), (1,)), ((), ())), preferred_element_type=jnp.float32)
        if len(refs) == 2:
            term += refs[0][at : at + span, :]
        total_ref[at : at + span, :] = term.astype(total_ref.dtype)


def column_span(width):
    return 512 if width % 512 == 0 else BLOCK


def after(value, *others):
    return lax.optimization_barrier((value, *others))[0]


def by_ring(grad_recon, inputs, decoder, owners, local_blocks, offsets, act_values):
    token_count, width = grad_recon.shape
    block_count = owners.shape[1]
    per_block = offsets.shape[2]
    latent_count = decoder.shape[0]
    peer_count = lax.axis_size("lat")
    chips = peer_count // 2
    me = lax.axis_index("lat")
    sources, onward, backward, swap = ring_tables(peer_count)
    order = jnp.concatenate([jnp.asarray(sources)[me], jnp.full((chips, 1), me, jnp.int32)], axis=1)
    own_t = owners.T
    whole = pl.BlockSpec(memory_space=pltpu.VMEM)
    scalars = pl.BlockSpec(memory_space=pltpu.SMEM)
    step_tokens = 2 * token_count
    light = pl.CostEstimate(flops=1, bytes_accessed=1, transcendentals=0)
    params = pltpu.CompilerParams(vmem_limit_bytes=VMEM_BYTES)

    extended = pl.pallas_call(
        extend_kernel,
        in_specs=[whole] * 5,
        out_specs=whole,
        out_shape=jax.ShapeDtypeStruct((token_count, width + 2 * token_count), jnp.bfloat16),
        compiler_params=params,
        cost_estimate=light,
        name="extend",
    )(grad_recon, own_t, local_blocks.T, offsets.transpose(1, 2, 0), act_values.transpose(1, 2, 0))

    def near(value):
        return pltpu.with_memory_space_constraint(value, pltpu.VMEM)

    def grad_step(hop, rows, totals, last):
        sums, lanes = (latent_count, width), (latent_count, token_count)
        return pl.pallas_call(
            functools.partial(grad_kernel, block_count, per_block),
            in_specs=[scalars] + [whole] * (3 + len(totals)),
            out_specs=[whole] * 4,
            out_shape=[
                jax.ShapeDtypeStruct(sums, jnp.bfloat16) if last else pltpu.VMEM(sums, jnp.float32),
                jax.ShapeDtypeStruct((1, latent_count), jnp.float32) if last else pltpu.VMEM(lanes, jnp.float32),
                jax.ShapeDtypeStruct((peer_count, per_block, token_count), jnp.float32),
                pltpu.VMEM((latent_count, step_tokens), jnp.bfloat16),
            ],
            scratch_shapes=[
                pltpu.VMEM((latent_count, step_tokens), jnp.bfloat16),
                pltpu.VMEM(lanes, jnp.float32),
            ],
            input_output_aliases={} if last or not totals else {4: 0, 5: 1},
            compiler_params=params,
            cost_estimate=light,
            name="grad_step",
        )(order[hop], near(decoder), near(rows[0]), near(rows[1]), *map(near, totals))

    def input_step(pre, rows, total, last):
        sums = (width, latent_count)
        totals = () if total is None else (total,)
        return pl.pallas_call(
            input_kernel,
            in_specs=[whole] * (3 + len(totals)),
            out_specs=whole,
            out_shape=jax.ShapeDtypeStruct(sums, jnp.bfloat16) if last else pltpu.VMEM(sums, jnp.float32),
            input_output_aliases={3: 0} if totals and not last else {},
            compiler_params=params,
            cost_estimate=light,
            name="input_step",
        )(near(pre), near(rows[0]), near(rows[1]), *map(near, totals))

    def send(rows, way, *first):
        return lax.ppermute(after(rows, *first) if first else rows, "lat", way)

    turns = [("grads", 1), ("grads", -1)]
    input_hops = [1, -1, *range(2, chips - 3), -2, chips - 3]
    for hop in range(2, chips - 1):
        turns += [("grads", hop), ("inputs", input_hops.pop(0))]
    turns += [("inputs", hop) for hop in input_hops]
    pres, totals, encoder_grad = {}, (), None

    def use(kind, hop, rows, last=False):
        nonlocal totals, encoder_grad
        if kind == "grads":
            *totals, pres[hop] = grad_step(hop, rows, totals, last)
            return totals[1]
        encoder_grad = input_step(pres[hop], rows, encoder_grad, last)
        return encoder_grad

    held = {(kind, way): rows for kind, rows in (("grads", extended), ("inputs", inputs)) for way in (True, False)}
    own_grads, own_inputs = send(extended, swap), send(inputs, swap)
    marks = []
    last_grads = max(turn for turn, (kind, _) in enumerate(turns) if kind == "grads")
    returned = None

    def arrive(turn):
        nonlocal returned
        kind, hop = turns[turn]
        last = turn in (last_grads, len(turns) - 1)
        ready = () if turn < 2 else (marks[turn - 2],)
        if turn == len(turns) - 1:
            ready += (returned,)
        marks.append(use(kind, hop % chips, (arrived[turn], send(arrived[turn], swap, *ready)), last))
        if turn == last_grads:
            returned = lax.all_to_all(totals[2], "lat", split_axis=0, concat_axis=0, tiled=True)

    use("grads", 0, (extended, own_grads))
    use("inputs", 0, (inputs, own_inputs))
    arrived = []
    for turn, (kind, hop) in enumerate(turns):
        while len(marks) < (turn - 2 if turn == len(turns) - 1 else turn - LAG + 1):
            arrive(len(marks))
        ready = (marks[-1],) if marks else ()
        rows = send(held[kind, hop > 0], onward if hop > 0 else backward, *ready)
        held[kind, hop > 0] = rows
        arrived.append(rows)
    while len(marks) < len(turns):
        arrive(len(marks))
    latent_grads = pick_returned(after(returned, encoder_grad), own_t)
    return (totals[0], encoder_grad, totals[1].reshape(latent_count), latent_grads)


def pick_returned(returned, own_t):
    owner_id = jnp.arange(returned.shape[0], dtype=jnp.int32)[:, None, None, None]
    picked = jnp.where(own_t[None, :, None, :] == owner_id, returned[:, None, :, :], 0.0)
    return jnp.sum(picked, axis=0).reshape(-1, own_t.shape[1]).T


def build_kernel(block_count, per_block, me_ref, meta_ref, acts_ref, cols_ref):
    pairs = block_count * per_block
    meta = meta_ref[0].astype(jnp.float32)
    me = me_ref[0].astype(jnp.float32)
    tokens = meta.shape[1]
    values = jnp.zeros((per_block, tokens), jnp.float32)
    columns = jnp.full((per_block, tokens), -1.0, jnp.float32)
    for i in range(block_count):
        mine = meta[2 * pairs + i : 2 * pairs + i + 1] == me
        values = jnp.where(mine, meta[i * per_block : (i + 1) * per_block], values)
        columns = jnp.where(mine, meta[pairs + i * per_block : pairs + (i + 1) * per_block], columns)
    columns = columns.astype(jnp.int32)
    cols_ref[0] = columns
    row = lax.broadcasted_iota(jnp.int32, (acts_ref.shape[0], tokens), 0)
    dense = jnp.zeros(row.shape, jnp.float32)
    for k in range(per_block):
        dense = jnp.where(row == columns[k : k + 1], values[k : k + 1], dense)
    acts_ref[...] = dense.astype(jnp.bfloat16)


def mask_kernel(per_block, products_ref, cols_ref, pre_ref, lat_ref, bias_ref):
    products = products_ref[...]
    columns = cols_ref[0]
    row = lax.broadcasted_iota(jnp.int32, products.shape, 0)
    kept = jnp.zeros(products.shape, jnp.float32)
    for k in range(per_block):
        picked = jnp.where(row == columns[k : k + 1], products, 0.0)
        lat_ref[0, k : k + 1, :] = jnp.sum(picked, axis=0, keepdims=True)
        kept = kept + picked
    pre_ref[...] = kept.astype(jnp.bfloat16)

    @pl.when(pl.program_id(0) == 0)
    def _():
        bias_ref[...] = jnp.zeros_like(bias_ref)

    bias_ref[...] += kept


def column_parts(width, row_count):
    lanes = width // BLOCK
    for parts in range(2, lanes + 1):
        if lanes % parts == 0 and row_count * (width // parts) * 2 <= PART_BYTES:
            return parts
    return lanes


def by_gather(grad_recon, inputs, decoder, owners, local_blocks, offsets, act_values):
    token_count, width = grad_recon.shape
    block_count = owners.shape[1]
    per_block = offsets.shape[2]
    latent_count = decoder.shape[0]
    peer_count = lax.axis_size("lat")
    pairs = block_count * per_block
    row_count = peer_count * token_count
    me = lax.axis_index("lat").astype(jnp.int32).reshape(1)

    own_t = owners.T
    columns_t = (local_blocks.T[:, None, :] * BLOCK + offsets.transpose(1, 2, 0)).reshape(pairs, token_count)
    acts_t = act_values.transpose(1, 2, 0).reshape(pairs, token_count)
    filler = jnp.zeros((-block_count % 16, token_count), jnp.bfloat16)
    meta = jnp.concatenate([acts_t, columns_t.astype(jnp.bfloat16), own_t.astype(jnp.bfloat16), filler], axis=0)
    meta_all = lax.all_gather(meta, "lat", axis=0)

    parts = column_parts(width, row_count)
    span = width // parts
    depth = max(1, HELD_BYTES // (row_count * span * 2))

    def gathered(rows, p, done):
        piece = rows[:, p * span : (p + 1) * span]
        if len(done) >= depth:
            piece, _ = lax.optimization_barrier((piece, done[-depth]))
        return lax.all_gather(piece, "lat", axis=0, tiled=True)

    tile = pl.BlockSpec((latent_count, token_count), lambda s: (0, s))
    picks = pl.BlockSpec((1, per_block, token_count), lambda s: (s, 0, 0))
    acts_dense, cols = pl.pallas_call(
        functools.partial(build_kernel, block_count, per_block),
        grid=(peer_count,),
        in_specs=[
            pl.BlockSpec(memory_space=pltpu.SMEM),
            pl.BlockSpec((1, meta.shape[0], token_count), lambda s: (s, 0, 0)),
        ],
        out_specs=[tile, picks],
        out_shape=[
            jax.ShapeDtypeStruct((latent_count, row_count), jnp.bfloat16),
            jax.ShapeDtypeStruct((peer_count, per_block, token_count), jnp.int32),
        ],
        name="build",
    )(me, meta_all)

    products = None
    decoder_parts = []
    for p in range(parts):
        rows = gathered(grad_recon, p, decoder_parts)
        part = lax.dot_general(
            acts_dense, rows, (((1,), (0,)), ((), ())), preferred_element_type=jnp.float32
        ).astype(jnp.bfloat16)
        term = lax.dot_general(
            decoder[:, p * span : (p + 1) * span], rows, (((1,), (1,)), ((), ())), preferred_element_type=jnp.float32
        )
        products = term if products is None else products + term
        if depth < 2 * parts:
            part, products = lax.optimization_barrier((part, products))
        decoder_parts.append(part)
    decoder_grad = jnp.concatenate(decoder_parts, axis=1)

    pre_grads, lat, bias_lanes = pl.pallas_call(
        functools.partial(mask_kernel, per_block),
        grid=(peer_count,),
        in_specs=[tile, picks],
        out_specs=[tile, picks, pl.BlockSpec((latent_count, token_count), lambda s: (0, 0))],
        out_shape=[
            jax.ShapeDtypeStruct((latent_count, row_count), jnp.bfloat16),
            jax.ShapeDtypeStruct((peer_count, per_block, token_count), jnp.float32),
            jax.ShapeDtypeStruct((latent_count, token_count), jnp.float32),
        ],
        name="mask",
    )(products, cols)
    bias_grad = jnp.sum(bias_lanes, axis=1)
    returned = lax.all_to_all(lat, "lat", split_axis=0, concat_axis=0, tiled=True)
    latent_grads = pick_returned(returned, own_t)

    encoder_parts = []
    for p in range(parts):
        rows = gathered(inputs, p, decoder_parts + encoder_parts)
        encoder_parts.append(
            lax.dot_general(rows, pre_grads, (((0,), (1,)), ((), ())), preferred_element_type=jnp.float32).astype(
                jnp.bfloat16
            )
        )
    return (decoder_grad, jnp.concatenate(encoder_parts, axis=0), bias_grad, latent_grads)


def per_device(grad_recon, inputs, decoder, owners, local_blocks, offsets, act_values):
    peer_count = lax.axis_size("lat")
    token_count = grad_recon.shape[0]
    entries = offsets.shape[1] * offsets.shape[2]
    small = 2 * peer_count * grad_recon.size * grad_recon.dtype.itemsize <= RING_BYTES
    fits = token_count == BLOCK and 2 * entries <= token_count and offsets.shape[2] == 16 and offsets.shape[1] <= 16
    way = by_ring if small and fits and peer_count % 4 == 0 and peer_count >= 16 else by_gather
    return way(grad_recon, inputs, decoder, owners, local_blocks, offsets, act_values)


def solution(mesh):
    rows = P(("groups", "lat"), None)
    entries = P(("groups", "lat"), None, None)
    return jax.shard_map(
        per_device,
        mesh=mesh,
        in_specs=(rows, rows, P("lat", None), rows, rows, entries, entries),
        out_specs=(rows, P(None, ("groups", "lat")), P(("groups", "lat")), rows),
        check_vma=False,
    )
```

```python
import functools

import jax
import jax.numpy as jnp
import numpy as np
from jax import lax
from jax.experimental import pallas as pl
from jax.experimental.pallas import tpu as pltpu
from jax.sharding import PartitionSpec as P

BLOCK = 128
PART_BYTES = 9 << 20
HELD_BYTES = 1 << 25
RING_BYTES = 1 << 26
VMEM_BYTES = 24 << 20
LAG = 4


def ring_tables(peer_count):
    chips = peer_count // 2
    half = chips // 2
    ring = [chip for chip in range(chips) if chip % 2 == 0] + [chip for chip in reversed(range(chips)) if chip % 2]
    place = {chip: spot for spot, chip in enumerate(ring)}
    sources = np.zeros((peer_count, chips, 2), np.int32)
    ways = np.zeros((peer_count, peer_count + 2), np.int32)
    for device in range(peer_count):
        chip, core = divmod(device, 2)
        sign = 1 - 2 * core
        for hop in range(chips):
            behind, ahead = ring[(place[chip] - sign * hop) % chips], ring[(place[chip] + sign * hop) % chips]
            sources[device, hop] = (2 * behind + core, 2 * ahead + 1 - core)
            ways[device, 2 * ahead : 2 * ahead + 2] = 0 if hop == 0 else 1 if hop <= half else 2
            if hop in (half, half + 1):
                ways[device, peer_count + hop - half] = ahead
    onward = [(2 * ring[i], 2 * ring[(i + 1) % chips]) for i in range(chips)]
    onward += [(2 * ring[i] + 1, 2 * ring[(i - 1) % chips] + 1) for i in range(chips)]
    backward = [(b, a) for a, b in onward]
    swap = [(i, i ^ 1) for i in range(peer_count)]
    return sources, ways, onward, backward, swap


def one_hot(spots):
    count = spots.shape[1]
    row = lax.broadcasted_iota(jnp.int32, (count, count), 0)
    return jnp.where(row == jnp.broadcast_to(spots, (count, count)), 1.0, 0.0).astype(jnp.bfloat16)


def spread_kernel(ways_ref, *refs):
    sources, refs = refs[:6], refs[6:]
    meta_ref, orders_ref, *chains = refs[:6]
    held, sems = refs[6:12], refs[12]
    copies = [pltpu.make_async_copy(source, kept, sems.at[i]) for i, (source, kept) in enumerate(zip(sources, held))]
    for copy in copies:
        copy.start()
    owners_ref, blocks_ref, offsets_ref, values_ref = held[:4]
    peers = meta_ref.shape[0]
    count, per_block, tokens = offsets_ref.shape
    token = lax.broadcasted_iota(jnp.int32, (8, tokens), 1)
    up_to = jnp.where(
        lax.broadcasted_iota(jnp.int32, (tokens, tokens), 0) <= lax.broadcasted_iota(jnp.int32, (tokens, tokens), 1), 1.0, 0.0
    ).astype(jnp.bfloat16)
    copies[0].wait()
    owners = owners_ref[...]
    orders_ref[0] = one_hot(token[:1])
    for way in range(2):
        named = jnp.max(jnp.where((owners >> 1) == ways_ref[peers + way], 1.0, 0.0), axis=0, keepdims=True)
        named = jnp.broadcast_to(named, (8, tokens))
        before = jnp.dot(named.astype(jnp.bfloat16), up_to, preferred_element_type=jnp.float32).astype(jnp.int32)
        total = jnp.max(before, axis=1, keepdims=True)
        spots = jnp.where(named > 0, before - 1, total + token - before)
        orders_ref[way + 1] = one_hot(spots[:1])
    for copy in copies[1:4]:
        copy.wait()
    columns = [
        (jnp.broadcast_to(blocks_ref[i : i + 1, :], (per_block, tokens)) * BLOCK + offsets_ref[i]).astype(jnp.float32)
        for i in range(count)
    ]
    values = [values_ref[i].astype(jnp.float32) for i in range(count)]
    named = [jnp.broadcast_to(owners_ref[i : i + 1, :], (per_block, tokens)) for i in range(count)]
    for owner in range(peers):
        told_columns = jnp.full((per_block, tokens), -1.0, jnp.float32)
        told_values = jnp.zeros((per_block, tokens), jnp.float32)
        for i in range(count):
            mine = named[i] == owner
            told_columns = jnp.where(mine, columns[i], told_columns)
            told_values = jnp.where(mine, values[i], told_values)
        told = jnp.concatenate([told_columns, told_values], axis=0).astype(jnp.bfloat16)
        told = lax.dot_general(
            told, orders_ref[ways_ref[owner]], (((1,), (1,)), ((), ())), preferred_element_type=jnp.float32
        )
        meta_ref[owner] = told.astype(jnp.bfloat16)
    for i, rows_ref in enumerate(held[4:]):
        copies[4 + i].wait()
        width = rows_ref.shape[1]
        span = column_span(width)
        for at in range(0, width, span):
            for way in range(2):
                moved = jnp.dot(orders_ref[way + 1], rows_ref[:, at : at + span], preferred_element_type=jnp.float32)
                chains[2 * i + way][:, at : at + span] = moved.astype(jnp.bfloat16)


def pick_kernel(ways_ref, owners_ref, orders_ref, returned_ref, out_ref):
    peers, per_block, tokens = returned_ref.shape
    count = owners_ref.shape[0]
    out_ref[...] = jnp.zeros_like(out_ref)
    for owner in range(peers):
        rest, pieces = returned_ref[owner], []
        for _ in range(3):
            pieces.append(rest.astype(jnp.bfloat16))
            rest = rest - pieces[-1].astype(jnp.float32)
        back = jnp.dot(
            jnp.concatenate(pieces, axis=0), orders_ref[ways_ref[owner]], preferred_element_type=jnp.float32
        )
        back = back[:per_block] + back[per_block : 2 * per_block] + back[2 * per_block :]
        for i in range(count):
            mine = jnp.broadcast_to(owners_ref[i : i + 1, :], (per_block, tokens)) == owner
            at = slice(i * per_block, (i + 1) * per_block)
            out_ref[at, :] = jnp.where(mine, back, out_ref[at, :])


def both_rows(mine_ref, theirs_ref, at, tokens):
    parts = []
    for rows_ref in (mine_ref, theirs_ref):
        parts.append(rows_ref[:, at])
        if rows_ref.shape[0] < tokens:
            parts.append(jnp.zeros((tokens - rows_ref.shape[0], parts[-1].shape[1]), jnp.bfloat16))
    return jnp.concatenate(parts, axis=0)


def grad_kernel(per_block, order_ref, meta_ref, decoder_ref, mine_ref, theirs_ref, *refs):
    total_ref, bias_ref, lat_ref, pre_ref, acts_ref, bias_sum = refs[-6:]
    first, last = len(refs) == 6, bias_ref.shape[0] == 1
    bias_sum[...] = jnp.zeros_like(bias_sum) if first else refs[1][...]
    lat_ref[...] = jnp.zeros_like(lat_ref) if first else refs[2][...]
    latents, width = decoder_ref.shape
    tokens = meta_ref.shape[2]
    span = column_span(width)
    products = jnp.zeros((latents, 2 * tokens), jnp.float32)
    for at in range(0, width, span):
        rows = both_rows(mine_ref, theirs_ref, slice(at, at + span), tokens)
        products += lax.dot_general(
            decoder_ref[:, at : at + span], rows, (((1,), (1,)), ((), ())), preferred_element_type=jnp.float32
        )
    row = lax.broadcasted_iota(jnp.int32, (8, tokens), 0)
    for tile in range(2):
        meta = meta_ref[order_ref[tile]].astype(jnp.float32)
        columns = [jnp.broadcast_to(meta[k : k + 1], (8, tokens)).astype(jnp.int32) for k in range(per_block)]
        values = [jnp.broadcast_to(meta[per_block + k : per_block + k + 1], (8, tokens)) for k in range(per_block)]
        sums = [jnp.zeros((8, tokens), jnp.float32) for _ in range(per_block)]
        at = slice(tile * tokens, (tile + 1) * tokens)
        for block in range(0, latents, 16):
            kept_both, dense_both = [], []
            for base in (block, block + 8):
                here = products[base : base + 8, at]
                kept = jnp.zeros((8, tokens), jnp.float32)
                dense = jnp.zeros((8, tokens), jnp.float32)
                for k in range(per_block):
                    hit = columns[k] == row + base
                    picked = jnp.where(hit, here, 0.0)
                    sums[k] = sums[k] + picked
                    kept = kept + picked
                    dense = jnp.where(hit, values[k], dense)
                bias_sum[base : base + 8, :] += kept
                kept_both.append(kept)
                dense_both.append(dense)
            pre_ref[block : block + 16, at] = jnp.concatenate(kept_both, axis=0).astype(jnp.bfloat16)
            acts_ref[block : block + 16, at] = jnp.concatenate(dense_both, axis=0).astype(jnp.bfloat16)
        source = order_ref[tile]
        for k in range(per_block):
            lat_ref[source, k : k + 1, :] = jnp.sum(sums[k], axis=0, keepdims=True)
    for at in range(0, width, span):
        rows = both_rows(mine_ref, theirs_ref, slice(at, at + span), tokens)
        term = jnp.dot(acts_ref[...], rows, preferred_element_type=jnp.float32)
        if not first:
            term += refs[0][:, at : at + span]
        total_ref[:, at : at + span] = term.astype(total_ref.dtype)
    bias_ref[...] = jnp.sum(bias_sum[...].T, axis=0, keepdims=True) if last else bias_sum[...]


def input_kernel(pre_ref, mine_ref, theirs_ref, *refs):
    total_ref = refs[-1]
    width = mine_ref.shape[1]
    span = column_span(width)
    for at in range(0, width, span):
        rows = both_rows(mine_ref, theirs_ref, slice(at, at + span), pre_ref.shape[1] // 2)
        term = lax.dot_general(rows, pre_ref[...], (((0,), (1,)), ((), ())), preferred_element_type=jnp.float32)
        if len(refs) == 2:
            term += refs[0][at : at + span, :]
        total_ref[at : at + span, :] = term.astype(total_ref.dtype)


def column_span(width):
    return 512 if width % 512 == 0 else BLOCK


def after(value, *others):
    return lax.optimization_barrier((value, *others))[0]


def by_ring(grad_recon, inputs, decoder, owners, local_blocks, offsets, act_values):
    token_count, width = grad_recon.shape
    block_count = owners.shape[1]
    per_block = offsets.shape[2]
    latent_count = decoder.shape[0]
    peer_count = lax.axis_size("lat")
    chips = peer_count // 2
    me = lax.axis_index("lat")
    sources, ways, onward, backward, swap = ring_tables(peer_count)
    order, ways = jnp.asarray(sources)[me], jnp.asarray(ways)[me]
    capacity = (3 * token_count * block_count + 2 * peer_count - 1) // (2 * peer_count)
    needed = min(token_count, -(-2 * capacity // 16) * 16)
    own_t = owners.T
    whole = pl.BlockSpec(memory_space=pltpu.VMEM)
    scalars = pl.BlockSpec(memory_space=pltpu.SMEM)
    step_tokens = 2 * token_count
    light = pl.CostEstimate(flops=1, bytes_accessed=1, transcendentals=0)
    params = pltpu.CompilerParams(vmem_limit_bytes=VMEM_BYTES)

    arrays = (own_t, local_blocks.T, offsets.transpose(1, 2, 0), act_values.transpose(1, 2, 0), grad_recon, inputs)
    rows_shape = (token_count, width)
    meta, orders, *chains = pl.pallas_call(
        spread_kernel,
        in_specs=[scalars] + [pl.BlockSpec(memory_space=pltpu.HBM)] * len(arrays),
        out_specs=[whole] * 6,
        out_shape=[
            jax.ShapeDtypeStruct((peer_count, 2 * per_block, token_count), jnp.bfloat16),
            jax.ShapeDtypeStruct((3, token_count, token_count), jnp.bfloat16),
            *[pltpu.VMEM(rows_shape, jnp.bfloat16)] * 4,
        ],
        scratch_shapes=[pltpu.VMEM(array.shape, array.dtype) for array in arrays] + [pltpu.SemaphoreType.DMA((6,))],
        compiler_params=params,
        cost_estimate=light,
        name="spread",
    )(ways, *[pltpu.with_memory_space_constraint(array, pltpu.HBM) for array in arrays])
    meta = lax.all_to_all(meta, "lat", split_axis=0, concat_axis=0, tiled=True)

    def near(value):
        return pltpu.with_memory_space_constraint(value, pltpu.VMEM)

    def grad_step(hop, rows, totals, last):
        sums, lanes = (latent_count, width), (latent_count, token_count)
        return pl.pallas_call(
            functools.partial(grad_kernel, per_block),
            in_specs=[scalars] + [whole] * (4 + len(totals)),
            out_specs=[whole] * 4,
            out_shape=[
                jax.ShapeDtypeStruct(sums, jnp.bfloat16) if last else pltpu.VMEM(sums, jnp.float32),
                jax.ShapeDtypeStruct((1, latent_count), jnp.float32) if last else pltpu.VMEM(lanes, jnp.float32),
                jax.ShapeDtypeStruct((peer_count, per_block, token_count), jnp.float32),
                pltpu.VMEM((latent_count, step_tokens), jnp.bfloat16),
            ],
            scratch_shapes=[
                pltpu.VMEM((latent_count, step_tokens), jnp.bfloat16),
                pltpu.VMEM(lanes, jnp.float32),
            ],
            input_output_aliases={} if last or not totals else {5: 0, 6: 1},
            compiler_params=params,
            cost_estimate=light,
            name="grad_step",
        )(order[hop], near(meta), near(decoder), near(rows[0]), near(rows[1]), *map(near, totals))

    def input_step(pre, rows, total, last):
        sums = (width, latent_count)
        totals = () if total is None else (total,)
        return pl.pallas_call(
            input_kernel,
            in_specs=[whole] * (3 + len(totals)),
            out_specs=whole,
            out_shape=jax.ShapeDtypeStruct(sums, jnp.bfloat16) if last else pltpu.VMEM(sums, jnp.float32),
            input_output_aliases={3: 0} if totals and not last else {},
            compiler_params=params,
            cost_estimate=light,
            name="input_step",
        )(near(pre), near(rows[0]), near(rows[1]), *map(near, totals))

    def send(rows, way, *first):
        return lax.ppermute(after(rows, *first) if first else rows, "lat", way)

    half = chips // 2
    later = [("inputs", 1)]
    for hop in range(1, half):
        later += [("inputs", hop + 1), ("inputs", -hop)]
    turns = []
    for hop in range(1, half + 1):
        turns += [("grads", hop)] + ([("grads", -hop)] if hop < half else []) + [later.pop(0)]
    turns += later
    pres, totals, encoder_grad = {}, (), None

    def use(kind, hop, rows, last=False):
        nonlocal totals, encoder_grad
        if kind == "grads":
            *totals, pres[hop] = grad_step(hop, rows, totals, last)
            return totals[1]
        encoder_grad = input_step(pres[hop], rows, encoder_grad, last)
        return encoder_grad

    held = dict(zip([("grads", True), ("grads", False), ("inputs", True), ("inputs", False)], chains))
    own_grads, own_inputs = send(grad_recon, swap), send(inputs, swap, meta)
    marks = []
    last_grads = max(turn for turn, (kind, _) in enumerate(turns) if kind == "grads")
    latent_grads = None

    def arrive(turn):
        nonlocal latent_grads
        kind, hop = turns[turn]
        last = turn in (last_grads, len(turns) - 1)
        ready = (meta,) if turn < 2 else (marks[turn - 2],)
        if turn == len(turns) - 1:
            ready += (latent_grads,)
        marks.append(use(kind, hop % chips, (arrived[turn], send(arrived[turn], swap, *ready)), last))
        if turn == last_grads:
            returned = lax.all_to_all(totals[2], "lat", split_axis=0, concat_axis=0, tiled=True)
            latent_grads = pl.pallas_call(
                pick_kernel,
                in_specs=[scalars] + [whole] * 3,
                out_specs=whole,
                out_shape=jax.ShapeDtypeStruct((block_count * per_block, token_count), jnp.float32),
                compiler_params=params,
                cost_estimate=light,
                name="pick",
            )(ways, own_t, orders, returned)

    use("grads", 0, (grad_recon, own_grads))
    use("inputs", 0, (inputs, own_inputs))
    arrived = []
    for turn, (kind, hop) in enumerate(turns):
        if turn >= LAG:
            arrive(turn - LAG)
        ready = () if turn < 3 else (meta,) if turn < LAG else (marks[turn - LAG],)
        rows = held[kind, hop > 0]
        if hop in (half, 1 - half):
            rows = rows[:needed]
        rows = send(rows, onward if hop > 0 else backward, *ready)
        held[kind, hop > 0] = rows
        arrived.append(rows)
    for turn in range(len(turns) - LAG, len(turns)):
        arrive(turn)
    return (totals[0], encoder_grad, totals[1].reshape(latent_count), latent_grads.T)


def pick_returned(returned, own_t):
    owner_id = jnp.arange(returned.shape[0], dtype=jnp.int32)[:, None, None, None]
    picked = jnp.where(own_t[None, :, None, :] == owner_id, returned[:, None, :, :], 0.0)
    return jnp.sum(picked, axis=0).reshape(-1, own_t.shape[1]).T


def build_kernel(block_count, per_block, me_ref, meta_ref, acts_ref, cols_ref):
    pairs = block_count * per_block
    meta = meta_ref[0].astype(jnp.float32)
    me = me_ref[0].astype(jnp.float32)
    tokens = meta.shape[1]
    values = jnp.zeros((per_block, tokens), jnp.float32)
    columns = jnp.full((per_block, tokens), -1.0, jnp.float32)
    for i in range(block_count):
        mine = meta[2 * pairs + i : 2 * pairs + i + 1] == me
        values = jnp.where(mine, meta[i * per_block : (i + 1) * per_block], values)
        columns = jnp.where(mine, meta[pairs + i * per_block : pairs + (i + 1) * per_block], columns)
    columns = columns.astype(jnp.int32)
    cols_ref[0] = columns
    row = lax.broadcasted_iota(jnp.int32, (acts_ref.shape[0], tokens), 0)
    dense = jnp.zeros(row.shape, jnp.float32)
    for k in range(per_block):
        dense = jnp.where(row == columns[k : k + 1], values[k : k + 1], dense)
    acts_ref[...] = dense.astype(jnp.bfloat16)


def mask_kernel(per_block, products_ref, cols_ref, pre_ref, lat_ref, bias_ref):
    products = products_ref[...]
    columns = cols_ref[0]
    row = lax.broadcasted_iota(jnp.int32, products.shape, 0)
    kept = jnp.zeros(products.shape, jnp.float32)
    for k in range(per_block):
        picked = jnp.where(row == columns[k : k + 1], products, 0.0)
        lat_ref[0, k : k + 1, :] = jnp.sum(picked, axis=0, keepdims=True)
        kept = kept + picked
    pre_ref[...] = kept.astype(jnp.bfloat16)

    @pl.when(pl.program_id(0) == 0)
    def _():
        bias_ref[...] = jnp.zeros_like(bias_ref)

    bias_ref[...] += kept


def column_parts(width, row_count):
    lanes = width // BLOCK
    for parts in range(2, lanes + 1):
        if lanes % parts == 0 and row_count * (width // parts) * 2 <= PART_BYTES:
            return parts
    return lanes


def by_gather(grad_recon, inputs, decoder, owners, local_blocks, offsets, act_values):
    token_count, width = grad_recon.shape
    block_count = owners.shape[1]
    per_block = offsets.shape[2]
    latent_count = decoder.shape[0]
    peer_count = lax.axis_size("lat")
    pairs = block_count * per_block
    row_count = peer_count * token_count
    me = lax.axis_index("lat").astype(jnp.int32).reshape(1)

    own_t = owners.T
    columns_t = (local_blocks.T[:, None, :] * BLOCK + offsets.transpose(1, 2, 0)).reshape(pairs, token_count)
    acts_t = act_values.transpose(1, 2, 0).reshape(pairs, token_count)
    filler = jnp.zeros((-block_count % 16, token_count), jnp.bfloat16)
    meta = jnp.concatenate([acts_t, columns_t.astype(jnp.bfloat16), own_t.astype(jnp.bfloat16), filler], axis=0)
    meta_all = lax.all_gather(meta, "lat", axis=0)

    parts = column_parts(width, row_count)
    span = width // parts
    depth = max(1, HELD_BYTES // (row_count * span * 2))

    def gathered(rows, p, done):
        piece = rows[:, p * span : (p + 1) * span]
        if len(done) >= depth:
            piece, _ = lax.optimization_barrier((piece, done[-depth]))
        return lax.all_gather(piece, "lat", axis=0, tiled=True)

    tile = pl.BlockSpec((latent_count, token_count), lambda s: (0, s))
    picks = pl.BlockSpec((1, per_block, token_count), lambda s: (s, 0, 0))
    acts_dense, cols = pl.pallas_call(
        functools.partial(build_kernel, block_count, per_block),
        grid=(peer_count,),
        in_specs=[
            pl.BlockSpec(memory_space=pltpu.SMEM),
            pl.BlockSpec((1, meta.shape[0], token_count), lambda s: (s, 0, 0)),
        ],
        out_specs=[tile, picks],
        out_shape=[
            jax.ShapeDtypeStruct((latent_count, row_count), jnp.bfloat16),
            jax.ShapeDtypeStruct((peer_count, per_block, token_count), jnp.int32),
        ],
        name="build",
    )(me, meta_all)

    products = None
    decoder_parts = []
    for p in range(parts):
        rows = gathered(grad_recon, p, decoder_parts)
        part = lax.dot_general(
            acts_dense, rows, (((1,), (0,)), ((), ())), preferred_element_type=jnp.float32
        ).astype(jnp.bfloat16)
        term = lax.dot_general(
            decoder[:, p * span : (p + 1) * span], rows, (((1,), (1,)), ((), ())), preferred_element_type=jnp.float32
        )
        products = term if products is None else products + term
        if depth < 2 * parts:
            part, products = lax.optimization_barrier((part, products))
        decoder_parts.append(part)
    decoder_grad = jnp.concatenate(decoder_parts, axis=1)

    pre_grads, lat, bias_lanes = pl.pallas_call(
        functools.partial(mask_kernel, per_block),
        grid=(peer_count,),
        in_specs=[tile, picks],
        out_specs=[tile, picks, pl.BlockSpec((latent_count, token_count), lambda s: (0, 0))],
        out_shape=[
            jax.ShapeDtypeStruct((latent_count, row_count), jnp.bfloat16),
            jax.ShapeDtypeStruct((peer_count, per_block, token_count), jnp.float32),
            jax.ShapeDtypeStruct((latent_count, token_count), jnp.float32),
        ],
        name="mask",
    )(products, cols)
    bias_grad = jnp.sum(bias_lanes, axis=1)
    returned = lax.all_to_all(lat, "lat", split_axis=0, concat_axis=0, tiled=True)
    latent_grads = pick_returned(returned, own_t)

    encoder_parts = []
    for p in range(parts):
        rows = gathered(inputs, p, decoder_parts + encoder_parts)
        encoder_parts.append(
            lax.dot_general(rows, pre_grads, (((0,), (1,)), ((), ())), preferred_element_type=jnp.float32).astype(
                jnp.bfloat16
            )
        )
    return (decoder_grad, jnp.concatenate(encoder_parts, axis=0), bias_grad, latent_grads)


def per_device(grad_recon, inputs, decoder, owners, local_blocks, offsets, act_values):
    peer_count = lax.axis_size("lat")
    small = 2 * peer_count * grad_recon.size * grad_recon.dtype.itemsize <= RING_BYTES
    fits = grad_recon.shape[0] == BLOCK and offsets.shape[2] == 16 and decoder.shape[0] <= 256
    way = by_ring if small and fits and peer_count % 4 == 0 and peer_count >= 8 else by_gather
    return way(grad_recon, inputs, decoder, owners, local_blocks, offsets, act_values)


def solution(mesh):
    rows = P(("groups", "lat"), None)
    entries = P(("groups", "lat"), None, None)
    return jax.shard_map(
        per_device,
        mesh=mesh,
        in_specs=(rows, rows, P("lat", None), rows, rows, entries, entries),
        out_specs=(rows, P(None, ("groups", "lat")), P(("groups", "lat")), rows),
        check_vma=False,
    )
```

```python
import functools

import jax
import jax.numpy as jnp
import numpy as np
from jax import lax
from jax.experimental import pallas as pl
from jax.experimental.pallas import tpu as pltpu
from jax.sharding import PartitionSpec as P

BLOCK = 128
PART_BYTES = 9 << 20
HELD_BYTES = 1 << 25
RING_BYTES = 1 << 26
VMEM_BYTES = 24 << 20
LAG = 5
EARLY = 1


def ring_tables(peer_count):
    chips = peer_count // 2
    ring = [chip for chip in range(chips) if chip % 2 == 0] + [chip for chip in reversed(range(chips)) if chip % 2]
    place = {chip: spot for spot, chip in enumerate(ring)}
    sources = np.zeros((peer_count, chips, 2), np.int32)
    for device in range(peer_count):
        chip, core = divmod(device, 2)
        sign = 1 - 2 * core
        for hop in range(chips):
            behind, ahead = ring[(place[chip] - sign * hop) % chips], ring[(place[chip] + sign * hop) % chips]
            sources[device, hop] = (2 * behind + core, 2 * ahead + 1 - core)
    onward = [(2 * ring[i], 2 * ring[(i + 1) % chips]) for i in range(chips)]
    onward += [(2 * ring[i] + 1, 2 * ring[(i - 1) % chips] + 1) for i in range(chips)]
    swap = [(i, i ^ 1) for i in range(peer_count)]
    backward = [(b, a) for a, b in onward]
    return sources, onward, backward, swap


def meta_kernel(owners_ref, blocks_ref, offsets_ref, values_ref, meta_ref):
    count, per_block, tokens = offsets_ref.shape
    columns = [
        (jnp.broadcast_to(blocks_ref[i : i + 1, :], (per_block, tokens)) * BLOCK + offsets_ref[i]).astype(jnp.float32)
        for i in range(count)
    ]
    values = [values_ref[i].astype(jnp.float32) for i in range(count)]
    named = [jnp.broadcast_to(owners_ref[i : i + 1, :], (per_block, tokens)) for i in range(count)]
    for owner in range(meta_ref.shape[0]):
        told_columns = jnp.full((per_block, tokens), -1.0, jnp.float32)
        told_values = jnp.zeros((per_block, tokens), jnp.float32)
        for i in range(count):
            mine = named[i] == owner
            told_columns = jnp.where(mine, columns[i], told_columns)
            told_values = jnp.where(mine, values[i], told_values)
        meta_ref[owner, :per_block, :] = told_columns.astype(jnp.bfloat16)
        meta_ref[owner, per_block:, :] = told_values.astype(jnp.bfloat16)


def grad_kernel(per_block, order_ref, meta_ref, decoder_ref, mine_ref, theirs_ref, *refs):
    total_ref, bias_ref, lat_ref, pre_ref, acts_ref, bias_sum = refs[-6:]
    first, last = len(refs) == 6, bias_ref.shape[0] == 1
    bias_sum[...] = jnp.zeros_like(bias_sum) if first else refs[1][...]
    lat_ref[...] = jnp.zeros_like(lat_ref) if first else refs[2][...]
    latents, width = decoder_ref.shape
    tokens = mine_ref.shape[0]
    span = column_span(width)
    products = jnp.zeros((latents, 2 * tokens), jnp.float32)
    for at in range(0, width, span):
        rows = jnp.concatenate([mine_ref[:, at : at + span], theirs_ref[:, at : at + span]], axis=0)
        products += lax.dot_general(
            decoder_ref[:, at : at + span], rows, (((1,), (1,)), ((), ())), preferred_element_type=jnp.float32
        )
    row = lax.broadcasted_iota(jnp.int32, (8, tokens), 0)
    for tile in range(2):
        meta = meta_ref[order_ref[tile]].astype(jnp.float32)
        columns = [jnp.broadcast_to(meta[k : k + 1], (8, tokens)).astype(jnp.int32) for k in range(per_block)]
        values = [jnp.broadcast_to(meta[per_block + k : per_block + k + 1], (8, tokens)) for k in range(per_block)]
        sums = [jnp.zeros((8, tokens), jnp.float32) for _ in range(per_block)]
        at = slice(tile * tokens, (tile + 1) * tokens)
        for block in range(0, latents, 16):
            kept_both, dense_both = [], []
            for base in (block, block + 8):
                here = products[base : base + 8, at]
                kept = jnp.zeros((8, tokens), jnp.float32)
                dense = jnp.zeros((8, tokens), jnp.float32)
                for k in range(per_block):
                    hit = columns[k] == row + base
                    picked = jnp.where(hit, here, 0.0)
                    sums[k] = sums[k] + picked
                    kept = kept + picked
                    dense = jnp.where(hit, values[k], dense)
                bias_sum[base : base + 8, :] += kept
                kept_both.append(kept)
                dense_both.append(dense)
            pre_ref[block : block + 16, at] = jnp.concatenate(kept_both, axis=0).astype(jnp.bfloat16)
            acts_ref[block : block + 16, at] = jnp.concatenate(dense_both, axis=0).astype(jnp.bfloat16)
        source = order_ref[tile]
        for k in range(per_block):
            lat_ref[source, k : k + 1, :] = jnp.sum(sums[k], axis=0, keepdims=True)
    for at in range(0, width, span):
        rows = jnp.concatenate([mine_ref[:, at : at + span], theirs_ref[:, at : at + span]], axis=0)
        term = jnp.dot(acts_ref[...], rows, preferred_element_type=jnp.float32)
        if not first:
            term += refs[0][:, at : at + span]
        total_ref[:, at : at + span] = term.astype(total_ref.dtype)
    bias_ref[...] = jnp.sum(bias_sum[...].T, axis=0, keepdims=True) if last else bias_sum[...]


def input_kernel(pre_ref, mine_ref, theirs_ref, *refs):
    total_ref = refs[-1]
    width = mine_ref.shape[1]
    span = column_span(width)
    for at in range(0, width, span):
        rows = jnp.concatenate([mine_ref[:, at : at + span], theirs_ref[:, at : at + span]], axis=0)
        term = lax.dot_general(rows, pre_ref[...], (((0,), (1,)), ((), ())), preferred_element_type=jnp.float32)
        if len(refs) == 2:
            term += refs[0][at : at + span, :]
        total_ref[at : at + span, :] = term.astype(total_ref.dtype)


def column_span(width):
    return 512 if width % 512 == 0 else BLOCK


def after(value, *others):
    return lax.optimization_barrier((value, *others))[0]


def by_ring(grad_recon, inputs, decoder, owners, local_blocks, offsets, act_values):
    token_count, width = grad_recon.shape
    block_count = owners.shape[1]
    per_block = offsets.shape[2]
    latent_count = decoder.shape[0]
    peer_count = lax.axis_size("lat")
    chips = peer_count // 2
    me = lax.axis_index("lat")
    sources, onward, backward, swap = ring_tables(peer_count)
    order = jnp.asarray(sources)[me]
    own_t = owners.T
    whole = pl.BlockSpec(memory_space=pltpu.VMEM)
    scalars = pl.BlockSpec(memory_space=pltpu.SMEM)
    step_tokens = 2 * token_count
    light = pl.CostEstimate(flops=1, bytes_accessed=1, transcendentals=0)
    params = pltpu.CompilerParams(vmem_limit_bytes=VMEM_BYTES)

    meta = pl.pallas_call(
        meta_kernel,
        in_specs=[whole] * 4,
        out_specs=whole,
        out_shape=jax.ShapeDtypeStruct((peer_count, 2 * per_block, token_count), jnp.bfloat16),
        compiler_params=params,
        cost_estimate=light,
        name="meta",
    )(own_t, local_blocks.T, offsets.transpose(1, 2, 0), act_values.transpose(1, 2, 0))
    meta = lax.all_to_all(meta, "lat", split_axis=0, concat_axis=0, tiled=True)

    def near(value):
        return pltpu.with_memory_space_constraint(value, pltpu.VMEM)

    def grad_step(hop, rows, totals, last):
        sums, lanes = (latent_count, width), (latent_count, token_count)
        return pl.pallas_call(
            functools.partial(grad_kernel, per_block),
            in_specs=[scalars] + [whole] * (4 + len(totals)),
            out_specs=[whole] * 4,
            out_shape=[
                jax.ShapeDtypeStruct(sums, jnp.bfloat16) if last else pltpu.VMEM(sums, jnp.float32),
                jax.ShapeDtypeStruct((1, latent_count), jnp.float32) if last else pltpu.VMEM(lanes, jnp.float32),
                jax.ShapeDtypeStruct((peer_count, per_block, token_count), jnp.float32),
                pltpu.VMEM((latent_count, step_tokens), jnp.bfloat16),
            ],
            scratch_shapes=[
                pltpu.VMEM((latent_count, step_tokens), jnp.bfloat16),
                pltpu.VMEM(lanes, jnp.float32),
            ],
            input_output_aliases={} if last or not totals else {5: 0, 6: 1},
            compiler_params=params,
            cost_estimate=light,
            name="grad_step",
        )(order[hop], near(meta), near(decoder), near(rows[0]), near(rows[1]), *map(near, totals))

    def input_step(pre, rows, total, last):
        sums = (width, latent_count)
        totals = () if total is None else (total,)
        return pl.pallas_call(
            input_kernel,
            in_specs=[whole] * (3 + len(totals)),
            out_specs=whole,
            out_shape=jax.ShapeDtypeStruct(sums, jnp.bfloat16) if last else pltpu.VMEM(sums, jnp.float32),
            input_output_aliases={3: 0} if totals and not last else {},
            compiler_params=params,
            cost_estimate=light,
            name="input_step",
        )(near(pre), near(rows[0]), near(rows[1]), *map(near, totals))

    def send(rows, way, *first):
        return lax.ppermute(after(rows, *first) if first else rows, "lat", way)

    half = chips // 2
    later = [("inputs", 1)]
    for hop in range(1, half):
        later += [("inputs", hop + 1), ("inputs", -hop)]
    turns = []
    for hop in range(1, half + 1):
        turns += [("grads", hop)] + ([("grads", -hop)] if hop < half else []) + [later.pop(0)]
    turns += later
    pres, totals, encoder_grad = {}, (), None

    def use(kind, hop, rows, last=False):
        nonlocal totals, encoder_grad
        if kind == "grads":
            *totals, pres[hop] = grad_step(hop, rows, totals, last)
            return totals[1]
        encoder_grad = input_step(pres[hop], rows, encoder_grad, last)
        return encoder_grad

    held = {(kind, way): rows for kind, rows in (("grads", grad_recon), ("inputs", inputs)) for way in (True, False)}
    own_grads, own_inputs = send(grad_recon, swap), send(inputs, swap, meta)
    marks = []
    last_grads = max(turn for turn, (kind, _) in enumerate(turns) if kind == "grads")
    returned = None

    def arrive(turn):
        nonlocal returned
        kind, hop = turns[turn]
        last = turn in (last_grads, len(turns) - 1)
        ready = (meta,) if turn < 3 else (marks[turn - 3],)
        if turn == len(turns) - 1:
            ready += (returned,)
        marks.append(use(kind, hop % chips, (arrived[turn], send(arrived[turn], swap, *ready)), last))
        if turn == last_grads:
            returned = lax.all_to_all(totals[2], "lat", split_axis=0, concat_axis=0, tiled=True)

    use("grads", 0, (grad_recon, own_grads))
    use("inputs", 0, (inputs, own_inputs))
    arrived = []
    for turn, (kind, hop) in enumerate(turns):
        while len(marks) < (last_grads + 1 if turn >= len(turns) - EARLY else turn - LAG + 1):
            arrive(len(marks))
        ready = () if turn < 3 else (meta,) if turn < max(LAG, 4) else (marks[-1],)
        rows = send(held[kind, hop > 0], onward if hop > 0 else backward, *ready)
        held[kind, hop > 0] = rows
        arrived.append(rows)
    while len(marks) < len(turns):
        arrive(len(marks))
    latent_grads = pick_returned(after(returned, encoder_grad), own_t)
    return (totals[0], encoder_grad, totals[1].reshape(latent_count), latent_grads)


def pick_returned(returned, own_t):
    owner_id = jnp.arange(returned.shape[0], dtype=jnp.int32)[:, None, None, None]
    picked = jnp.where(own_t[None, :, None, :] == owner_id, returned[:, None, :, :], 0.0)
    return jnp.sum(picked, axis=0).reshape(-1, own_t.shape[1]).T


def build_kernel(block_count, per_block, me_ref, meta_ref, acts_ref, cols_ref):
    pairs = block_count * per_block
    meta = meta_ref[0].astype(jnp.float32)
    me = me_ref[0].astype(jnp.float32)
    tokens = meta.shape[1]
    values = jnp.zeros((per_block, tokens), jnp.float32)
    columns = jnp.full((per_block, tokens), -1.0, jnp.float32)
    for i in range(block_count):
        mine = meta[2 * pairs + i : 2 * pairs + i + 1] == me
        values = jnp.where(mine, meta[i * per_block : (i + 1) * per_block], values)
        columns = jnp.where(mine, meta[pairs + i * per_block : pairs + (i + 1) * per_block], columns)
    columns = columns.astype(jnp.int32)
    cols_ref[0] = columns
    row = lax.broadcasted_iota(jnp.int32, (acts_ref.shape[0], tokens), 0)
    dense = jnp.zeros(row.shape, jnp.float32)
    for k in range(per_block):
        dense = jnp.where(row == columns[k : k + 1], values[k : k + 1], dense)
    acts_ref[...] = dense.astype(jnp.bfloat16)


def mask_kernel(per_block, products_ref, cols_ref, pre_ref, lat_ref, bias_ref):
    products = products_ref[...]
    columns = cols_ref[0]
    row = lax.broadcasted_iota(jnp.int32, products.shape, 0)
    kept = jnp.zeros(products.shape, jnp.float32)
    for k in range(per_block):
        picked = jnp.where(row == columns[k : k + 1], products, 0.0)
        lat_ref[0, k : k + 1, :] = jnp.sum(picked, axis=0, keepdims=True)
        kept = kept + picked
    pre_ref[...] = kept.astype(jnp.bfloat16)

    @pl.when(pl.program_id(0) == 0)
    def _():
        bias_ref[...] = jnp.zeros_like(bias_ref)

    bias_ref[...] += kept


def column_parts(width, row_count):
    lanes = width // BLOCK
    for parts in range(2, lanes + 1):
        if lanes % parts == 0 and row_count * (width // parts) * 2 <= PART_BYTES:
            return parts
    return lanes


def by_gather(grad_recon, inputs, decoder, owners, local_blocks, offsets, act_values):
    token_count, width = grad_recon.shape
    block_count = owners.shape[1]
    per_block = offsets.shape[2]
    latent_count = decoder.shape[0]
    peer_count = lax.axis_size("lat")
    pairs = block_count * per_block
    row_count = peer_count * token_count
    me = lax.axis_index("lat").astype(jnp.int32).reshape(1)

    own_t = owners.T
    columns_t = (local_blocks.T[:, None, :] * BLOCK + offsets.transpose(1, 2, 0)).reshape(pairs, token_count)
    acts_t = act_values.transpose(1, 2, 0).reshape(pairs, token_count)
    filler = jnp.zeros((-block_count % 16, token_count), jnp.bfloat16)
    meta = jnp.concatenate([acts_t, columns_t.astype(jnp.bfloat16), own_t.astype(jnp.bfloat16), filler], axis=0)
    meta_all = lax.all_gather(meta, "lat", axis=0)

    parts = column_parts(width, row_count)
    span = width // parts
    depth = max(1, HELD_BYTES // (row_count * span * 2))

    def gathered(rows, p, done):
        piece = rows[:, p * span : (p + 1) * span]
        if len(done) >= depth:
            piece, _ = lax.optimization_barrier((piece, done[-depth]))
        return lax.all_gather(piece, "lat", axis=0, tiled=True)

    tile = pl.BlockSpec((latent_count, token_count), lambda s: (0, s))
    picks = pl.BlockSpec((1, per_block, token_count), lambda s: (s, 0, 0))
    acts_dense, cols = pl.pallas_call(
        functools.partial(build_kernel, block_count, per_block),
        grid=(peer_count,),
        in_specs=[
            pl.BlockSpec(memory_space=pltpu.SMEM),
            pl.BlockSpec((1, meta.shape[0], token_count), lambda s: (s, 0, 0)),
        ],
        out_specs=[tile, picks],
        out_shape=[
            jax.ShapeDtypeStruct((latent_count, row_count), jnp.bfloat16),
            jax.ShapeDtypeStruct((peer_count, per_block, token_count), jnp.int32),
        ],
        name="build",
    )(me, meta_all)

    products = None
    decoder_parts = []
    for p in range(parts):
        rows = gathered(grad_recon, p, decoder_parts)
        part = lax.dot_general(
            acts_dense, rows, (((1,), (0,)), ((), ())), preferred_element_type=jnp.float32
        ).astype(jnp.bfloat16)
        term = lax.dot_general(
            decoder[:, p * span : (p + 1) * span], rows, (((1,), (1,)), ((), ())), preferred_element_type=jnp.float32
        )
        products = term if products is None else products + term
        if depth < 2 * parts:
            part, products = lax.optimization_barrier((part, products))
        decoder_parts.append(part)
    decoder_grad = jnp.concatenate(decoder_parts, axis=1)

    pre_grads, lat, bias_lanes = pl.pallas_call(
        functools.partial(mask_kernel, per_block),
        grid=(peer_count,),
        in_specs=[tile, picks],
        out_specs=[tile, picks, pl.BlockSpec((latent_count, token_count), lambda s: (0, 0))],
        out_shape=[
            jax.ShapeDtypeStruct((latent_count, row_count), jnp.bfloat16),
            jax.ShapeDtypeStruct((peer_count, per_block, token_count), jnp.float32),
            jax.ShapeDtypeStruct((latent_count, token_count), jnp.float32),
        ],
        name="mask",
    )(products, cols)
    bias_grad = jnp.sum(bias_lanes, axis=1)
    returned = lax.all_to_all(lat, "lat", split_axis=0, concat_axis=0, tiled=True)
    latent_grads = pick_returned(returned, own_t)

    encoder_parts = []
    for p in range(parts):
        rows = gathered(inputs, p, decoder_parts + encoder_parts)
        encoder_parts.append(
            lax.dot_general(rows, pre_grads, (((0,), (1,)), ((), ())), preferred_element_type=jnp.float32).astype(
                jnp.bfloat16
            )
        )
    return (decoder_grad, jnp.concatenate(encoder_parts, axis=0), bias_grad, latent_grads)


def per_device(grad_recon, *others):
    row_bytes = lax.axis_size("lat") * grad_recon.size * grad_recon.dtype.itemsize
    way = by_ring if 2 * row_bytes <= RING_BYTES and lax.axis_size("lat") % 4 == 0 else by_gather
    return way(grad_recon, *others)


def solution(mesh):
    rows = P(("groups", "lat"), None)
    entries = P(("groups", "lat"), None, None)
    return jax.shard_map(
        per_device,
        mesh=mesh,
        in_specs=(rows, rows, P("lat", None), rows, rows, entries, entries),
        out_specs=(rows, P(None, ("groups", "lat")), P(("groups", "lat")), rows),
        check_vma=False,
    )
```

```python
import functools

import jax
import jax.numpy as jnp
import numpy as np
from jax import lax
from jax.experimental import pallas as pl
from jax.experimental.pallas import tpu as pltpu
from jax.sharding import PartitionSpec as P

BLOCK = 128
PART_BYTES = 9 << 20
HELD_BYTES = 1 << 25
RING_BYTES = 1 << 26
VMEM_BYTES = 24 << 20
LAG = 4


def ring_tables(peer_count):
    chips = peer_count // 2
    ring = [chip for chip in range(chips) if chip % 2 == 0] + [chip for chip in reversed(range(chips)) if chip % 2]
    place = {chip: spot for spot, chip in enumerate(ring)}
    sources = np.zeros((peer_count, chips, 2), np.int32)
    for device in range(peer_count):
        chip, core = divmod(device, 2)
        sign = 1 - 2 * core
        for hop in range(chips):
            behind, ahead = ring[(place[chip] - sign * hop) % chips], ring[(place[chip] + sign * hop) % chips]
            sources[device, hop] = (2 * behind + core, 2 * ahead + 1 - core)
    onward = [(2 * ring[i], 2 * ring[(i + 1) % chips]) for i in range(chips)]
    onward += [(2 * ring[i] + 1, 2 * ring[(i - 1) % chips] + 1) for i in range(chips)]
    swap = [(i, i ^ 1) for i in range(peer_count)]
    backward = [(b, a) for a, b in onward]
    target = dict(onward)
    second = [(a, target[b]) for a, b in onward]
    across = [(b, a ^ 1) for a, b in second]
    return sources, onward, backward, swap, second, across


def meta_kernel(owners_ref, blocks_ref, offsets_ref, values_ref, meta_ref):
    count, per_block, tokens = offsets_ref.shape
    columns = [
        (jnp.broadcast_to(blocks_ref[i : i + 1, :], (per_block, tokens)) * BLOCK + offsets_ref[i]).astype(jnp.float32)
        for i in range(count)
    ]
    values = [values_ref[i].astype(jnp.float32) for i in range(count)]
    named = [jnp.broadcast_to(owners_ref[i : i + 1, :], (per_block, tokens)) for i in range(count)]
    for owner in range(meta_ref.shape[0]):
        told_columns = jnp.full((per_block, tokens), -1.0, jnp.float32)
        told_values = jnp.zeros((per_block, tokens), jnp.float32)
        for i in range(count):
            mine = named[i] == owner
            told_columns = jnp.where(mine, columns[i], told_columns)
            told_values = jnp.where(mine, values[i], told_values)
        meta_ref[owner, :per_block, :] = told_columns.astype(jnp.bfloat16)
        meta_ref[owner, per_block:, :] = told_values.astype(jnp.bfloat16)


def grad_kernel(per_block, order_ref, meta_ref, decoder_ref, mine_ref, theirs_ref, *refs):
    total_ref, bias_ref, lat_ref, pre_ref, acts_ref, bias_sum = refs[-6:]
    first, last = len(refs) == 6, bias_ref.shape[0] == 1
    bias_sum[...] = jnp.zeros_like(bias_sum) if first else refs[1][...]
    if not last:
        lat_ref[...] = jnp.zeros_like(lat_ref) if first else refs[2][...]
    latents, width = decoder_ref.shape
    tokens = mine_ref.shape[0]
    span = column_span(width)
    products = jnp.zeros((latents, 2 * tokens), jnp.float32)
    for at in range(0, width, span):
        rows = jnp.concatenate([mine_ref[:, at : at + span], theirs_ref[:, at : at + span]], axis=0)
        products += lax.dot_general(
            decoder_ref[:, at : at + span], rows, (((1,), (1,)), ((), ())), preferred_element_type=jnp.float32
        )
    row = lax.broadcasted_iota(jnp.int32, (8, tokens), 0)
    for tile in range(2):
        meta = meta_ref[order_ref[tile]].astype(jnp.float32)
        columns = [jnp.broadcast_to(meta[k : k + 1], (8, tokens)).astype(jnp.int32) for k in range(per_block)]
        values = [jnp.broadcast_to(meta[per_block + k : per_block + k + 1], (8, tokens)) for k in range(per_block)]
        sums = [jnp.zeros((8, tokens), jnp.float32) for _ in range(per_block)]
        at = slice(tile * tokens, (tile + 1) * tokens)
        for block in range(0, latents, 16):
            kept_both, dense_both = [], []
            for base in (block, block + 8):
                here = products[base : base + 8, at]
                kept = jnp.zeros((8, tokens), jnp.float32)
                dense = jnp.zeros((8, tokens), jnp.float32)
                for k in range(per_block):
                    hit = columns[k] == row + base
                    picked = jnp.where(hit, here, 0.0)
                    sums[k] = sums[k] + picked
                    kept = kept + picked
                    dense = jnp.where(hit, values[k], dense)
                bias_sum[base : base + 8, :] += kept
                kept_both.append(kept)
                dense_both.append(dense)
            pre_ref[block : block + 16, at] = jnp.concatenate(kept_both, axis=0).astype(jnp.bfloat16)
            acts_ref[block : block + 16, at] = jnp.concatenate(dense_both, axis=0).astype(jnp.bfloat16)
        source = tile if last else order_ref[tile]
        for k in range(per_block):
            lat_ref[source, k : k + 1, :] = jnp.sum(sums[k], axis=0, keepdims=True)
    for at in range(0, width, span):
        rows = jnp.concatenate([mine_ref[:, at : at + span], theirs_ref[:, at : at + span]], axis=0)
        term = jnp.dot(acts_ref[...], rows, preferred_element_type=jnp.float32)
        if not first:
            term += refs[0][:, at : at + span]
        total_ref[:, at : at + span] = term.astype(total_ref.dtype)
    bias_ref[...] = jnp.sum(bias_sum[...].T, axis=0, keepdims=True) if last else bias_sum[...]


def input_kernel(last, pre_ref, mine_ref, theirs_ref, *refs):
    copies = []
    if last:
        out_ref, total_ref, sems = refs[-3:]
        refs = refs[:-2]
    else:
        total_ref = refs[-1]
    width = mine_ref.shape[1]
    span = column_span(width)
    for at in range(0, width, span):
        rows = jnp.concatenate([mine_ref[:, at : at + span], theirs_ref[:, at : at + span]], axis=0)
        term = lax.dot_general(rows, pre_ref[...], (((0,), (1,)), ((), ())), preferred_element_type=jnp.float32)
        if len(refs) == 2:
            term += refs[0][at : at + span, :]
        total_ref[at : at + span, :] = term.astype(total_ref.dtype)
        if last:
            here = pl.ds(at, span)
            copies.append(pltpu.make_async_copy(total_ref.at[here], out_ref.at[here], sems.at[at // span]))
            copies[-1].start()
    for copy in copies:
        copy.wait()


def column_span(width):
    return 512 if width % 512 == 0 else BLOCK


def after(value, *others):
    return lax.optimization_barrier((value, *others))[0]


def by_ring(grad_recon, inputs, decoder, owners, local_blocks, offsets, act_values):
    token_count, width = grad_recon.shape
    block_count = owners.shape[1]
    per_block = offsets.shape[2]
    latent_count = decoder.shape[0]
    peer_count = lax.axis_size("lat")
    chips = peer_count // 2
    me = lax.axis_index("lat")
    sources, onward, backward, swap, second, across = ring_tables(peer_count)
    order = jnp.asarray(sources)[me]
    own_t = owners.T
    whole = pl.BlockSpec(memory_space=pltpu.VMEM)
    scalars = pl.BlockSpec(memory_space=pltpu.SMEM)
    step_tokens = 2 * token_count
    light = pl.CostEstimate(flops=1, bytes_accessed=1, transcendentals=0)
    params = pltpu.CompilerParams(vmem_limit_bytes=VMEM_BYTES)

    meta = pl.pallas_call(
        meta_kernel,
        in_specs=[whole] * 4,
        out_specs=whole,
        out_shape=jax.ShapeDtypeStruct((peer_count, 2 * per_block, token_count), jnp.bfloat16),
        compiler_params=params,
        cost_estimate=light,
        name="meta",
    )(own_t, local_blocks.T, offsets.transpose(1, 2, 0), act_values.transpose(1, 2, 0))
    meta = lax.all_to_all(meta, "lat", split_axis=0, concat_axis=0, tiled=True)

    def near(value):
        return pltpu.with_memory_space_constraint(value, pltpu.VMEM)

    def grad_step(hop, rows, totals, last):
        sums, lanes = (latent_count, width), (latent_count, token_count)
        lat = (2 if last else peer_count, per_block, token_count)
        return pl.pallas_call(
            functools.partial(grad_kernel, per_block),
            in_specs=[scalars] + [whole] * (4 + len(totals)),
            out_specs=[whole] * 4,
            out_shape=[
                jax.ShapeDtypeStruct(sums, jnp.bfloat16) if last else pltpu.VMEM(sums, jnp.float32),
                jax.ShapeDtypeStruct((1, latent_count), jnp.float32) if last else pltpu.VMEM(lanes, jnp.float32),
                jax.ShapeDtypeStruct(lat, jnp.float32),
                pltpu.VMEM((latent_count, step_tokens), jnp.bfloat16),
            ],
            scratch_shapes=[
                pltpu.VMEM((latent_count, step_tokens), jnp.bfloat16),
                pltpu.VMEM(lanes, jnp.float32),
            ],
            input_output_aliases={} if last or not totals else {5: 0, 6: 1},
            compiler_params=params,
            cost_estimate=light,
            name="grad_step",
        )(order[hop], near(meta), near(decoder), near(rows[0]), near(rows[1]), *map(near, totals))

    def input_step(pre, rows, total, last):
        sums = (width, latent_count)
        totals = () if total is None else (total,)
        return pl.pallas_call(
            functools.partial(input_kernel, last),
            in_specs=[whole] * (3 + len(totals)),
            out_specs=pl.BlockSpec(memory_space=pl.ANY) if last else whole,
            out_shape=jax.ShapeDtypeStruct(sums, jnp.bfloat16) if last else pltpu.VMEM(sums, jnp.float32),
            scratch_shapes=[
                pltpu.VMEM(sums, jnp.bfloat16),
                pltpu.SemaphoreType.DMA((width // column_span(width),)),
            ]
            if last
            else [],
            input_output_aliases={3: 0} if totals and not last else {},
            compiler_params=params,
            cost_estimate=light,
            name="input_step",
        )(near(pre), near(rows[0]), near(rows[1]), *map(near, totals))

    def send(rows, way, *first):
        return lax.ppermute(after(rows, *first) if first else rows, "lat", way)

    turns = [("grads", 1), ("grads", -1), ("inputs", 1)]
    for hop in range(2, chips - 2):
        turns += [("grads", hop), ("inputs", hop)]
    turns += [("grads", chips - 2), ("inputs", -1), ("inputs", chips - 2)]
    pres, totals, encoder_grad = {}, (), None

    def use(kind, hop, rows, last=False):
        nonlocal totals, encoder_grad
        if kind == "grads":
            *totals, pres[hop] = grad_step(hop, rows, totals, last)
            return totals[1]
        encoder_grad = input_step(pres[hop], rows, encoder_grad, last)
        return encoder_grad

    held = {(kind, way): rows for kind, rows in (("grads", grad_recon), ("inputs", inputs)) for way in (True, False)}
    own_grads, own_inputs = send(grad_recon, swap), send(inputs, swap, meta)
    marks = []
    last_grads = max(turn for turn, (kind, _) in enumerate(turns) if kind == "grads")
    returned = None

    def arrive(turn):
        nonlocal returned, totals
        kind, hop = turns[turn]
        last = turn in (last_grads, len(turns) - 1)
        if turn == last_grads:
            returned = lax.all_to_all(totals[2], "lat", split_axis=0, concat_axis=0, tiled=True)
            totals = totals[:2]
        ready = (meta,) if turn < 2 else (marks[turn - 2],)
        if turn == len(turns) - 1:
            ready += (returned,)
        marks.append(use(kind, hop % chips, (arrived[turn], send(arrived[turn], swap, *ready)), last))

    use("grads", 0, (grad_recon, own_grads))
    use("inputs", 0, (inputs, own_inputs))
    arrived = []
    for turn, (kind, hop) in enumerate(turns):
        while len(marks) < turn - LAG + 1:
            arrive(len(marks))
        ready = () if turn < 3 else (meta,) if turn < LAG else (marks[-1],)
        rows = send(held[kind, hop > 0], onward if hop > 0 else backward, *ready)
        held[kind, hop > 0] = rows
        arrived.append(rows)
    while len(marks) < len(turns):
        arrive(len(marks))
    lat = totals[2]
    sent_back = lax.ppermute(lat[0], "lat", second), lax.ppermute(lat[1], "lat", across)
    nearest = jnp.asarray(sources)[me, 2, 0]
    latent_grads = pick_returned(after(returned, encoder_grad), own_t, (nearest, nearest ^ 1), sent_back)
    return (totals[0], encoder_grad, totals[1].reshape(latent_count), latent_grads)


def pick_returned(returned, own_t, more_owners=(), more=()):
    owner_id = jnp.arange(returned.shape[0], dtype=jnp.int32)[:, None, None, None]
    picked = jnp.sum(jnp.where(own_t[None, :, None, :] == owner_id, returned[:, None, :, :], 0.0), axis=0)
    for owner, sent_back in zip(more_owners, more):
        picked += jnp.where(own_t[:, None, :] == owner, sent_back[None], 0.0)
    return picked.reshape(-1, own_t.shape[1]).T


def build_kernel(block_count, per_block, me_ref, meta_ref, acts_ref, cols_ref):
    pairs = block_count * per_block
    meta = meta_ref[0].astype(jnp.float32)
    me = me_ref[0].astype(jnp.float32)
    tokens = meta.shape[1]
    values = jnp.zeros((per_block, tokens), jnp.float32)
    columns = jnp.full((per_block, tokens), -1.0, jnp.float32)
    for i in range(block_count):
        mine = meta[2 * pairs + i : 2 * pairs + i + 1] == me
        values = jnp.where(mine, meta[i * per_block : (i + 1) * per_block], values)
        columns = jnp.where(mine, meta[pairs + i * per_block : pairs + (i + 1) * per_block], columns)
    columns = columns.astype(jnp.int32)
    cols_ref[0] = columns
    row = lax.broadcasted_iota(jnp.int32, (acts_ref.shape[0], tokens), 0)
    dense = jnp.zeros(row.shape, jnp.float32)
    for k in range(per_block):
        dense = jnp.where(row == columns[k : k + 1], values[k : k + 1], dense)
    acts_ref[...] = dense.astype(jnp.bfloat16)


def mask_kernel(per_block, products_ref, cols_ref, pre_ref, lat_ref, bias_ref):
    products = products_ref[...]
    columns = cols_ref[0]
    row = lax.broadcasted_iota(jnp.int32, products.shape, 0)
    kept = jnp.zeros(products.shape, jnp.float32)
    for k in range(per_block):
        picked = jnp.where(row == columns[k : k + 1], products, 0.0)
        lat_ref[0, k : k + 1, :] = jnp.sum(picked, axis=0, keepdims=True)
        kept = kept + picked
    pre_ref[...] = kept.astype(jnp.bfloat16)

    @pl.when(pl.program_id(0) == 0)
    def _():
        bias_ref[...] = jnp.zeros_like(bias_ref)

    bias_ref[...] += kept


def column_parts(width, row_count):
    lanes = width // BLOCK
    for parts in range(2, lanes + 1):
        if lanes % parts == 0 and row_count * (width // parts) * 2 <= PART_BYTES:
            return parts
    return lanes


def by_gather(grad_recon, inputs, decoder, owners, local_blocks, offsets, act_values):
    token_count, width = grad_recon.shape
    block_count = owners.shape[1]
    per_block = offsets.shape[2]
    latent_count = decoder.shape[0]
    peer_count = lax.axis_size("lat")
    pairs = block_count * per_block
    row_count = peer_count * token_count
    me = lax.axis_index("lat").astype(jnp.int32).reshape(1)

    own_t = owners.T
    columns_t = (local_blocks.T[:, None, :] * BLOCK + offsets.transpose(1, 2, 0)).reshape(pairs, token_count)
    acts_t = act_values.transpose(1, 2, 0).reshape(pairs, token_count)
    filler = jnp.zeros((-block_count % 16, token_count), jnp.bfloat16)
    meta = jnp.concatenate([acts_t, columns_t.astype(jnp.bfloat16), own_t.astype(jnp.bfloat16), filler], axis=0)
    meta_all = lax.all_gather(meta, "lat", axis=0)

    parts = column_parts(width, row_count)
    span = width // parts
    depth = max(1, HELD_BYTES // (row_count * span * 2))

    def gathered(rows, p, done):
        piece = rows[:, p * span : (p + 1) * span]
        if len(done) >= depth:
            piece, _ = lax.optimization_barrier((piece, done[-depth]))
        return lax.all_gather(piece, "lat", axis=0, tiled=True)

    tile = pl.BlockSpec((latent_count, token_count), lambda s: (0, s))
    picks = pl.BlockSpec((1, per_block, token_count), lambda s: (s, 0, 0))
    acts_dense, cols = pl.pallas_call(
        functools.partial(build_kernel, block_count, per_block),
        grid=(peer_count,),
        in_specs=[
            pl.BlockSpec(memory_space=pltpu.SMEM),
            pl.BlockSpec((1, meta.shape[0], token_count), lambda s: (s, 0, 0)),
        ],
        out_specs=[tile, picks],
        out_shape=[
            jax.ShapeDtypeStruct((latent_count, row_count), jnp.bfloat16),
            jax.ShapeDtypeStruct((peer_count, per_block, token_count), jnp.int32),
        ],
        name="build",
    )(me, meta_all)

    products = None
    decoder_parts = []
    for p in range(parts):
        rows = gathered(grad_recon, p, decoder_parts)
        part = lax.dot_general(
            acts_dense, rows, (((1,), (0,)), ((), ())), preferred_element_type=jnp.float32
        ).astype(jnp.bfloat16)
        term = lax.dot_general(
            decoder[:, p * span : (p + 1) * span], rows, (((1,), (1,)), ((), ())), preferred_element_type=jnp.float32
        )
        products = term if products is None else products + term
        if depth < 2 * parts:
            part, products = lax.optimization_barrier((part, products))
        decoder_parts.append(part)
    decoder_grad = jnp.concatenate(decoder_parts, axis=1)

    pre_grads, lat, bias_lanes = pl.pallas_call(
        functools.partial(mask_kernel, per_block),
        grid=(peer_count,),
        in_specs=[tile, picks],
        out_specs=[tile, picks, pl.BlockSpec((latent_count, token_count), lambda s: (0, 0))],
        out_shape=[
            jax.ShapeDtypeStruct((latent_count, row_count), jnp.bfloat16),
            jax.ShapeDtypeStruct((peer_count, per_block, token_count), jnp.float32),
            jax.ShapeDtypeStruct((latent_count, token_count), jnp.float32),
        ],
        name="mask",
    )(products, cols)
    bias_grad = jnp.sum(bias_lanes, axis=1)
    returned = lax.all_to_all(lat, "lat", split_axis=0, concat_axis=0, tiled=True)
    latent_grads = pick_returned(returned, own_t)

    encoder_parts = []
    for p in range(parts):
        rows = gathered(inputs, p, decoder_parts + encoder_parts)
        encoder_parts.append(
            lax.dot_general(rows, pre_grads, (((0,), (1,)), ((), ())), preferred_element_type=jnp.float32).astype(
                jnp.bfloat16
            )
        )
    return (decoder_grad, jnp.concatenate(encoder_parts, axis=0), bias_grad, latent_grads)


def per_device(grad_recon, *others):
    row_bytes = lax.axis_size("lat") * grad_recon.size * grad_recon.dtype.itemsize
    way = by_ring if 2 * row_bytes <= RING_BYTES and lax.axis_size("lat") % 4 == 0 else by_gather
    return way(grad_recon, *others)


def solution(mesh):
    rows = P(("groups", "lat"), None)
    entries = P(("groups", "lat"), None, None)
    return jax.shard_map(
        per_device,
        mesh=mesh,
        in_specs=(rows, rows, P("lat", None), rows, rows, entries, entries),
        out_specs=(rows, P(None, ("groups", "lat")), P(("groups", "lat")), rows),
        check_vma=False,
    )
```

```python
import functools

import jax
import jax.numpy as jnp
import numpy as np
from jax import lax
from jax.experimental import pallas as pl
from jax.experimental.pallas import tpu as pltpu
from jax.sharding import PartitionSpec as P

BLOCK = 128
PART_BYTES = 9 << 20
HELD_BYTES = 1 << 25
RING_BYTES = 1 << 26
VMEM_BYTES = 24 << 20
LAG = 4


def ring_tables(peer_count):
    chips = peer_count // 2
    ring = [chip for chip in range(chips) if chip % 2 == 0] + [chip for chip in reversed(range(chips)) if chip % 2]
    place = {chip: spot for spot, chip in enumerate(ring)}
    sources = np.zeros((peer_count, chips, 2), np.int32)
    for device in range(peer_count):
        chip, core = divmod(device, 2)
        sign = 1 - 2 * core
        for hop in range(chips):
            behind, ahead = ring[(place[chip] - sign * hop) % chips], ring[(place[chip] + sign * hop) % chips]
            sources[device, hop] = (2 * behind + core, 2 * ahead + 1 - core)
    onward = [(2 * ring[i], 2 * ring[(i + 1) % chips]) for i in range(chips)]
    onward += [(2 * ring[i] + 1, 2 * ring[(i - 1) % chips] + 1) for i in range(chips)]
    swap = [(i, i ^ 1) for i in range(peer_count)]
    backward = [(b, a) for a, b in onward]
    return sources, onward, backward, swap


def meta_kernel(*refs):
    sources, meta_ref, held, sems = refs[:4], refs[4], refs[5:9], refs[9]
    copies = [pltpu.make_async_copy(source, kept, sems.at[i]) for i, (source, kept) in enumerate(zip(sources, held))]
    for copy in copies:
        copy.start()
    for copy in copies:
        copy.wait()
    owners_ref, blocks_ref, offsets_ref, values_ref = held
    count, per_block, tokens = offsets_ref.shape
    columns = [
        (jnp.broadcast_to(blocks_ref[i : i + 1, :], (per_block, tokens)) * BLOCK + offsets_ref[i]).astype(jnp.float32)
        for i in range(count)
    ]
    values = [values_ref[i].astype(jnp.float32) for i in range(count)]
    named = [jnp.broadcast_to(owners_ref[i : i + 1, :], (per_block, tokens)) for i in range(count)]
    for owner in range(meta_ref.shape[0]):
        told_columns = jnp.full((per_block, tokens), -1.0, jnp.float32)
        told_values = jnp.zeros((per_block, tokens), jnp.float32)
        for i in range(count):
            mine = named[i] == owner
            told_columns = jnp.where(mine, columns[i], told_columns)
            told_values = jnp.where(mine, values[i], told_values)
        meta_ref[owner, :per_block, :] = told_columns.astype(jnp.bfloat16)
        meta_ref[owner, per_block:, :] = told_values.astype(jnp.bfloat16)


def grad_kernel(per_block, order_ref, meta_ref, decoder_ref, mine_ref, theirs_ref, *refs):
    total_ref, bias_ref, lat_ref, pre_ref, acts_ref, bias_sum = refs[-6:]
    first, last = len(refs) == 6, bias_ref.shape[0] == 1
    bias_sum[...] = jnp.zeros_like(bias_sum) if first else refs[1][...]
    lat_ref[...] = jnp.zeros_like(lat_ref) if first else refs[2][...]
    latents, width = decoder_ref.shape
    tokens = mine_ref.shape[0]
    span = column_span(width)
    products = jnp.zeros((latents, 2 * tokens), jnp.float32)
    for at in range(0, width, span):
        rows = jnp.concatenate([mine_ref[:, at : at + span], theirs_ref[:, at : at + span]], axis=0)
        products += lax.dot_general(
            decoder_ref[:, at : at + span], rows, (((1,), (1,)), ((), ())), preferred_element_type=jnp.float32
        )
    row = lax.broadcasted_iota(jnp.int32, (8, tokens), 0)
    for tile in range(2):
        meta = meta_ref[order_ref[tile]].astype(jnp.float32)
        columns = [jnp.broadcast_to(meta[k : k + 1], (8, tokens)).astype(jnp.int32) for k in range(per_block)]
        values = [jnp.broadcast_to(meta[per_block + k : per_block + k + 1], (8, tokens)) for k in range(per_block)]
        sums = [jnp.zeros((8, tokens), jnp.float32) for _ in range(per_block)]
        at = slice(tile * tokens, (tile + 1) * tokens)
        for block in range(0, latents, 16):
            kept_both, dense_both = [], []
            for base in (block, block + 8):
                here = products[base : base + 8, at]
                kept = jnp.zeros((8, tokens), jnp.float32)
                dense = jnp.zeros((8, tokens), jnp.float32)
                for k in range(per_block):
                    hit = columns[k] == row + base
                    picked = jnp.where(hit, here, 0.0)
                    sums[k] = sums[k] + picked
                    kept = kept + picked
                    dense = jnp.where(hit, values[k], dense)
                bias_sum[base : base + 8, :] += kept
                kept_both.append(kept)
                dense_both.append(dense)
            pre_ref[block : block + 16, at] = jnp.concatenate(kept_both, axis=0).astype(jnp.bfloat16)
            acts_ref[block : block + 16, at] = jnp.concatenate(dense_both, axis=0).astype(jnp.bfloat16)
        source = order_ref[tile]
        for k in range(per_block):
            lat_ref[source, k : k + 1, :] = jnp.sum(sums[k], axis=0, keepdims=True)
    for at in range(0, width, span):
        rows = jnp.concatenate([mine_ref[:, at : at + span], theirs_ref[:, at : at + span]], axis=0)
        term = jnp.dot(acts_ref[...], rows, preferred_element_type=jnp.float32)
        if not first:
            term += refs[0][:, at : at + span]
        total_ref[:, at : at + span] = term.astype(total_ref.dtype)
    bias_ref[...] = jnp.sum(bias_sum[...].T, axis=0, keepdims=True) if last else bias_sum[...]


def input_kernel(pre_ref, mine_ref, theirs_ref, *refs):
    total_ref = refs[-1]
    width = mine_ref.shape[1]
    span = column_span(width)
    for at in range(0, width, span):
        rows = jnp.concatenate([mine_ref[:, at : at + span], theirs_ref[:, at : at + span]], axis=0)
        term = lax.dot_general(rows, pre_ref[...], (((0,), (1,)), ((), ())), preferred_element_type=jnp.float32)
        if len(refs) == 2:
            term += refs[0][at : at + span, :]
        total_ref[at : at + span, :] = term.astype(total_ref.dtype)


def last_input_kernel(pre_ref, mine_ref, theirs_ref, part_ref, total_ref, out_ref, held_ref, made_ref, in_sems, out_sems):
    width = mine_ref.shape[1]
    span = column_span(width)
    parts = [pl.ds(at, span) for at in range(0, width, span)]
    copies_in = [pltpu.make_async_copy(total_ref.at[p], held_ref.at[p], in_sems.at[i]) for i, p in enumerate(parts)]
    copies_out = [pltpu.make_async_copy(made_ref.at[p], out_ref.at[p], out_sems.at[i]) for i, p in enumerate(parts)]
    for copy in copies_in:
        copy.start()
    for i, at in enumerate(range(0, width, span)):
        rows = jnp.concatenate([mine_ref[:, at : at + span], theirs_ref[:, at : at + span]], axis=0)
        term = lax.dot_general(rows, pre_ref[...], (((0,), (1,)), ((), ())), preferred_element_type=jnp.float32)
        term += part_ref[at : at + span, :]
        copies_in[i].wait()
        made_ref[at : at + span, :] = (term + held_ref[at : at + span, :]).astype(made_ref.dtype)
        copies_out[i].start()
    for copy in copies_out:
        copy.wait()


def column_span(width):
    return 512 if width % 512 == 0 else BLOCK


def after(value, *others):
    return lax.optimization_barrier((value, *others))[0]


def by_ring(grad_recon, inputs, decoder, owners, local_blocks, offsets, act_values):
    token_count, width = grad_recon.shape
    block_count = owners.shape[1]
    per_block = offsets.shape[2]
    latent_count = decoder.shape[0]
    peer_count = lax.axis_size("lat")
    chips = peer_count // 2
    me = lax.axis_index("lat")
    sources, onward, backward, swap = ring_tables(peer_count)
    order = jnp.asarray(sources)[me]
    own_t = owners.T
    whole = pl.BlockSpec(memory_space=pltpu.VMEM)
    scalars = pl.BlockSpec(memory_space=pltpu.SMEM)
    step_tokens = 2 * token_count
    light = pl.CostEstimate(flops=1, bytes_accessed=1, transcendentals=0)
    params = pltpu.CompilerParams(vmem_limit_bytes=VMEM_BYTES)

    entries = (own_t, local_blocks.T, offsets.transpose(1, 2, 0), act_values.transpose(1, 2, 0))
    meta = pl.pallas_call(
        meta_kernel,
        in_specs=[pl.BlockSpec(memory_space=pltpu.HBM)] * 4,
        out_specs=whole,
        out_shape=jax.ShapeDtypeStruct((peer_count, 2 * per_block, token_count), jnp.bfloat16),
        scratch_shapes=[pltpu.VMEM(array.shape, array.dtype) for array in entries] + [pltpu.SemaphoreType.DMA((4,))],
        compiler_params=params,
        cost_estimate=light,
        name="meta",
    )(*[pltpu.with_memory_space_constraint(array, pltpu.HBM) for array in entries])
    meta = lax.all_to_all(meta, "lat", split_axis=0, concat_axis=0, tiled=True)

    def near(value):
        return pltpu.with_memory_space_constraint(value, pltpu.VMEM)

    def grad_step(hop, rows, totals, last):
        sums, lanes = (latent_count, width), (latent_count, token_count)
        return pl.pallas_call(
            functools.partial(grad_kernel, per_block),
            in_specs=[scalars] + [whole] * (4 + len(totals)),
            out_specs=[whole] * 4,
            out_shape=[
                jax.ShapeDtypeStruct(sums, jnp.bfloat16) if last else pltpu.VMEM(sums, jnp.float32),
                jax.ShapeDtypeStruct((1, latent_count), jnp.float32) if last else pltpu.VMEM(lanes, jnp.float32),
                jax.ShapeDtypeStruct((peer_count, per_block, token_count), jnp.float32),
                pltpu.VMEM((latent_count, step_tokens), jnp.bfloat16),
            ],
            scratch_shapes=[
                pltpu.VMEM((latent_count, step_tokens), jnp.bfloat16),
                pltpu.VMEM(lanes, jnp.float32),
            ],
            input_output_aliases={} if last or not totals else {5: 0, 6: 1},
            compiler_params=params,
            cost_estimate=light,
            name="grad_step",
        )(order[hop], near(meta), near(decoder), near(rows[0]), near(rows[1]), *map(near, totals))

    def input_step(pre, rows, total):
        sums = (width, latent_count)
        totals = () if total is None else (total,)
        return pl.pallas_call(
            input_kernel,
            in_specs=[whole] * (3 + len(totals)),
            out_specs=whole,
            out_shape=pltpu.VMEM(sums, jnp.float32),
            input_output_aliases={3: 0} if totals else {},
            compiler_params=params,
            cost_estimate=light,
            name="input_step",
        )(near(pre), near(rows[0]), near(rows[1]), *map(near, totals))

    def last_input_step(pre, rows, part, total):
        sums, far = (width, latent_count), pl.BlockSpec(memory_space=pltpu.HBM)
        count = width // column_span(width)
        return pl.pallas_call(
            last_input_kernel,
            in_specs=[whole] * 4 + [far],
            out_specs=far,
            out_shape=jax.ShapeDtypeStruct(sums, jnp.bfloat16),
            scratch_shapes=[
                pltpu.VMEM(sums, jnp.float32),
                pltpu.VMEM(sums, jnp.bfloat16),
                pltpu.SemaphoreType.DMA((count,)),
                pltpu.SemaphoreType.DMA((count,)),
            ],
            compiler_params=params,
            cost_estimate=light,
            name="last_input_step",
        )(near(pre), near(rows[0]), near(rows[1]), near(part), pltpu.with_memory_space_constraint(total, pltpu.HBM))

    def send(rows, way, *first):
        return lax.ppermute(after(rows, *first) if first else rows, "lat", way)

    half = chips // 2
    later = [("inputs", 1)]
    for hop in range(1, half):
        later += [("inputs", hop + 1), ("inputs", -hop)]
    turns = []
    for hop in range(1, half + 1):
        turns += [("grads", hop)] + ([("grads", -hop)] if hop < half else []) + [later.pop(0)]
    turns += later
    pres, totals, encoder_grad = {}, (), None

    encoder_part = None

    def use(kind, hop, rows, left=len(turns)):
        nonlocal totals, encoder_grad, encoder_part
        if kind == "grads":
            *totals, pres[hop] = grad_step(hop, rows, totals, left == 0)
            return totals[1]
        if left == 0:
            encoder_grad = last_input_step(pres[hop], rows, encoder_part, encoder_grad)
        elif left == 1:
            encoder_part = input_step(pres[hop], rows, None)
            return encoder_part
        else:
            encoder_grad = input_step(pres[hop], rows, encoder_grad)
        return encoder_grad

    held = {(kind, way): rows for kind, rows in (("grads", grad_recon), ("inputs", inputs)) for way in (True, False)}
    own_grads, own_inputs = send(grad_recon, swap), send(inputs, swap, meta)
    marks = []
    last_grads = max(turn for turn, (kind, _) in enumerate(turns) if kind == "grads")
    returned = None

    def arrive(turn):
        nonlocal returned
        kind, hop = turns[turn]
        left = 0 if turn == last_grads else len(turns) - 1 - turn
        ready = (meta,) if turn < 2 else (marks[turn - 2],)
        if turn == len(turns) - 1:
            ready += (returned,)
        marks.append(use(kind, hop % chips, (arrived[turn], send(arrived[turn], swap, *ready)), left))
        if turn == last_grads:
            returned = lax.all_to_all(totals[2], "lat", split_axis=0, concat_axis=0, tiled=True)

    use("grads", 0, (grad_recon, own_grads))
    use("inputs", 0, (inputs, own_inputs))
    arrived = []
    for turn, (kind, hop) in enumerate(turns):
        if turn >= LAG:
            arrive(turn - LAG)
        ready = () if turn < 3 else (meta,) if turn < LAG else (marks[turn - LAG],)
        rows = send(held[kind, hop > 0], onward if hop > 0 else backward, *ready)
        held[kind, hop > 0] = rows
        arrived.append(rows)
    for turn in range(len(turns) - LAG, len(turns)):
        arrive(turn)
    latent_grads = pick_returned(after(returned, encoder_grad), own_t)
    return (totals[0], encoder_grad, totals[1].reshape(latent_count), latent_grads)


def pick_returned(returned, own_t):
    owner_id = jnp.arange(returned.shape[0], dtype=jnp.int32)[:, None, None, None]
    picked = jnp.where(own_t[None, :, None, :] == owner_id, returned[:, None, :, :], 0.0)
    return jnp.sum(picked, axis=0).reshape(-1, own_t.shape[1]).T


def build_kernel(block_count, per_block, me_ref, meta_ref, acts_ref, cols_ref):
    pairs = block_count * per_block
    meta = meta_ref[0].astype(jnp.float32)
    me = me_ref[0].astype(jnp.float32)
    tokens = meta.shape[1]
    values = jnp.zeros((per_block, tokens), jnp.float32)
    columns = jnp.full((per_block, tokens), -1.0, jnp.float32)
    for i in range(block_count):
        mine = meta[2 * pairs + i : 2 * pairs + i + 1] == me
        values = jnp.where(mine, meta[i * per_block : (i + 1) * per_block], values)
        columns = jnp.where(mine, meta[pairs + i * per_block : pairs + (i + 1) * per_block], columns)
    columns = columns.astype(jnp.int32)
    cols_ref[0] = columns
    row = lax.broadcasted_iota(jnp.int32, (acts_ref.shape[0], tokens), 0)
    dense = jnp.zeros(row.shape, jnp.float32)
    for k in range(per_block):
        dense = jnp.where(row == columns[k : k + 1], values[k : k + 1], dense)
    acts_ref[...] = dense.astype(jnp.bfloat16)


def mask_kernel(per_block, products_ref, cols_ref, pre_ref, lat_ref, bias_ref):
    products = products_ref[...]
    columns = cols_ref[0]
    row = lax.broadcasted_iota(jnp.int32, products.shape, 0)
    kept = jnp.zeros(products.shape, jnp.float32)
    for k in range(per_block):
        picked = jnp.where(row == columns[k : k + 1], products, 0.0)
        lat_ref[0, k : k + 1, :] = jnp.sum(picked, axis=0, keepdims=True)
        kept = kept + picked
    pre_ref[...] = kept.astype(jnp.bfloat16)

    @pl.when(pl.program_id(0) == 0)
    def _():
        bias_ref[...] = jnp.zeros_like(bias_ref)

    bias_ref[...] += kept


def column_parts(width, row_count):
    lanes = width // BLOCK
    for parts in range(2, lanes + 1):
        if lanes % parts == 0 and row_count * (width // parts) * 2 <= PART_BYTES:
            return parts
    return lanes


def by_gather(grad_recon, inputs, decoder, owners, local_blocks, offsets, act_values):
    token_count, width = grad_recon.shape
    block_count = owners.shape[1]
    per_block = offsets.shape[2]
    latent_count = decoder.shape[0]
    peer_count = lax.axis_size("lat")
    pairs = block_count * per_block
    row_count = peer_count * token_count
    me = lax.axis_index("lat").astype(jnp.int32).reshape(1)

    own_t = owners.T
    columns_t = (local_blocks.T[:, None, :] * BLOCK + offsets.transpose(1, 2, 0)).reshape(pairs, token_count)
    acts_t = act_values.transpose(1, 2, 0).reshape(pairs, token_count)
    filler = jnp.zeros((-block_count % 16, token_count), jnp.bfloat16)
    meta = jnp.concatenate([acts_t, columns_t.astype(jnp.bfloat16), own_t.astype(jnp.bfloat16), filler], axis=0)
    meta_all = lax.all_gather(meta, "lat", axis=0)

    parts = column_parts(width, row_count)
    span = width // parts
    depth = max(1, HELD_BYTES // (row_count * span * 2))

    def gathered(rows, p, done):
        piece = rows[:, p * span : (p + 1) * span]
        if len(done) >= depth:
            piece, _ = lax.optimization_barrier((piece, done[-depth]))
        return lax.all_gather(piece, "lat", axis=0, tiled=True)

    tile = pl.BlockSpec((latent_count, token_count), lambda s: (0, s))
    picks = pl.BlockSpec((1, per_block, token_count), lambda s: (s, 0, 0))
    acts_dense, cols = pl.pallas_call(
        functools.partial(build_kernel, block_count, per_block),
        grid=(peer_count,),
        in_specs=[
            pl.BlockSpec(memory_space=pltpu.SMEM),
            pl.BlockSpec((1, meta.shape[0], token_count), lambda s: (s, 0, 0)),
        ],
        out_specs=[tile, picks],
        out_shape=[
            jax.ShapeDtypeStruct((latent_count, row_count), jnp.bfloat16),
            jax.ShapeDtypeStruct((peer_count, per_block, token_count), jnp.int32),
        ],
        name="build",
    )(me, meta_all)

    products = None
    decoder_parts = []
    for p in range(parts):
        rows = gathered(grad_recon, p, decoder_parts)
        part = lax.dot_general(
            acts_dense, rows, (((1,), (0,)), ((), ())), preferred_element_type=jnp.float32
        ).astype(jnp.bfloat16)
        term = lax.dot_general(
            decoder[:, p * span : (p + 1) * span], rows, (((1,), (1,)), ((), ())), preferred_element_type=jnp.float32
        )
        products = term if products is None else products + term
        if depth < 2 * parts:
            part, products = lax.optimization_barrier((part, products))
        decoder_parts.append(part)
    decoder_grad = jnp.concatenate(decoder_parts, axis=1)

    pre_grads, lat, bias_lanes = pl.pallas_call(
        functools.partial(mask_kernel, per_block),
        grid=(peer_count,),
        in_specs=[tile, picks],
        out_specs=[tile, picks, pl.BlockSpec((latent_count, token_count), lambda s: (0, 0))],
        out_shape=[
            jax.ShapeDtypeStruct((latent_count, row_count), jnp.bfloat16),
            jax.ShapeDtypeStruct((peer_count, per_block, token_count), jnp.float32),
            jax.ShapeDtypeStruct((latent_count, token_count), jnp.float32),
        ],
        name="mask",
    )(products, cols)
    bias_grad = jnp.sum(bias_lanes, axis=1)
    returned = lax.all_to_all(lat, "lat", split_axis=0, concat_axis=0, tiled=True)
    latent_grads = pick_returned(returned, own_t)

    encoder_parts = []
    for p in range(parts):
        rows = gathered(inputs, p, decoder_parts + encoder_parts)
        encoder_parts.append(
            lax.dot_general(rows, pre_grads, (((0,), (1,)), ((), ())), preferred_element_type=jnp.float32).astype(
                jnp.bfloat16
            )
        )
    return (decoder_grad, jnp.concatenate(encoder_parts, axis=0), bias_grad, latent_grads)


def per_device(grad_recon, *others):
    row_bytes = lax.axis_size("lat") * grad_recon.size * grad_recon.dtype.itemsize
    way = by_ring if 2 * row_bytes <= RING_BYTES and lax.axis_size("lat") % 4 == 0 else by_gather
    return way(grad_recon, *others)


def solution(mesh):
    rows = P(("groups", "lat"), None)
    entries = P(("groups", "lat"), None, None)
    return jax.shard_map(
        per_device,
        mesh=mesh,
        in_specs=(rows, rows, P("lat", None), rows, rows, entries, entries),
        out_specs=(rows, P(None, ("groups", "lat")), P(("groups", "lat")), rows),
        check_vma=False,
    )
```

```python
import functools

import jax
import jax.numpy as jnp
import numpy as np
from jax import lax
from jax.experimental import pallas as pl
from jax.experimental.pallas import tpu as pltpu
from jax.sharding import PartitionSpec as P

BLOCK = 128
PART_BYTES = 9 << 20
HELD_BYTES = 1 << 25
RING_BYTES = 1 << 26
VMEM_BYTES = 24 << 20
LAG = 4


def ring_tables(peer_count):
    chips = peer_count // 2
    ring = [chip for chip in range(chips) if chip % 2 == 0] + [chip for chip in reversed(range(chips)) if chip % 2]
    place = {chip: spot for spot, chip in enumerate(ring)}
    sources = np.zeros((peer_count, chips, 2), np.int32)
    for device in range(peer_count):
        chip, core = divmod(device, 2)
        sign = 1 - 2 * core
        for hop in range(chips):
            behind, ahead = ring[(place[chip] - sign * hop) % chips], ring[(place[chip] + sign * hop) % chips]
            sources[device, hop] = (2 * behind + core, 2 * ahead + 1 - core)
    onward = [(2 * ring[i], 2 * ring[(i + 1) % chips]) for i in range(chips)]
    onward += [(2 * ring[i] + 1, 2 * ring[(i - 1) % chips] + 1) for i in range(chips)]
    swap = [(i, i ^ 1) for i in range(peer_count)]
    backward = [(b, a) for a, b in onward]
    target = dict(onward)
    second = [(a, target[b]) for a, b in onward]
    across = [(b, a ^ 1) for a, b in second]
    return sources, onward, backward, swap, second, across


def meta_kernel(*refs):
    sources, meta_ref, held, sems = refs[:4], refs[4], refs[5:9], refs[9]
    copies = [pltpu.make_async_copy(source, kept, sems.at[i]) for i, (source, kept) in enumerate(zip(sources, held))]
    for copy in copies:
        copy.start()
    for copy in copies:
        copy.wait()
    owners_ref, blocks_ref, offsets_ref, values_ref = held
    count, per_block, tokens = offsets_ref.shape
    columns = [
        (jnp.broadcast_to(blocks_ref[i : i + 1, :], (per_block, tokens)) * BLOCK + offsets_ref[i]).astype(jnp.float32)
        for i in range(count)
    ]
    values = [values_ref[i].astype(jnp.float32) for i in range(count)]
    named = [jnp.broadcast_to(owners_ref[i : i + 1, :], (per_block, tokens)) for i in range(count)]
    for owner in range(meta_ref.shape[0]):
        told_columns = jnp.full((per_block, tokens), -1.0, jnp.float32)
        told_values = jnp.zeros((per_block, tokens), jnp.float32)
        for i in range(count):
            mine = named[i] == owner
            told_columns = jnp.where(mine, columns[i], told_columns)
            told_values = jnp.where(mine, values[i], told_values)
        meta_ref[owner, :per_block, :] = told_columns.astype(jnp.bfloat16)
        meta_ref[owner, per_block:, :] = told_values.astype(jnp.bfloat16)


def grad_kernel(per_block, order_ref, meta_ref, decoder_ref, mine_ref, theirs_ref, *refs):
    total_ref, bias_ref, lat_ref, pre_ref, acts_ref, bias_sum = refs[-6:]
    first, last = len(refs) == 6, bias_ref.shape[0] == 1
    bias_sum[...] = jnp.zeros_like(bias_sum) if first else refs[1][...]
    if not last:
        lat_ref[...] = jnp.zeros_like(lat_ref) if first else refs[2][...]
    latents, width = decoder_ref.shape
    tokens = mine_ref.shape[0]
    span = column_span(width)
    products = jnp.zeros((latents, 2 * tokens), jnp.float32)
    for at in range(0, width, span):
        rows = jnp.concatenate([mine_ref[:, at : at + span], theirs_ref[:, at : at + span]], axis=0)
        products += lax.dot_general(
            decoder_ref[:, at : at + span], rows, (((1,), (1,)), ((), ())), preferred_element_type=jnp.float32
        )
    row = lax.broadcasted_iota(jnp.int32, (8, tokens), 0)
    for tile in range(2):
        meta = meta_ref[order_ref[tile]].astype(jnp.float32)
        columns = [jnp.broadcast_to(meta[k : k + 1], (8, tokens)).astype(jnp.int32) for k in range(per_block)]
        values = [jnp.broadcast_to(meta[per_block + k : per_block + k + 1], (8, tokens)) for k in range(per_block)]
        sums = [jnp.zeros((8, tokens), jnp.float32) for _ in range(per_block)]
        at = slice(tile * tokens, (tile + 1) * tokens)
        for block in range(0, latents, 16):
            kept_both, dense_both = [], []
            for base in (block, block + 8):
                here = products[base : base + 8, at]
                kept = jnp.zeros((8, tokens), jnp.float32)
                dense = jnp.zeros((8, tokens), jnp.float32)
                for k in range(per_block):
                    hit = columns[k] == row + base
                    picked = jnp.where(hit, here, 0.0)
                    sums[k] = sums[k] + picked
                    kept = kept + picked
                    dense = jnp.where(hit, values[k], dense)
                bias_sum[base : base + 8, :] += kept
                kept_both.append(kept)
                dense_both.append(dense)
            pre_ref[block : block + 16, at] = jnp.concatenate(kept_both, axis=0).astype(jnp.bfloat16)
            acts_ref[block : block + 16, at] = jnp.concatenate(dense_both, axis=0).astype(jnp.bfloat16)
        source = tile if last else order_ref[tile]
        for k in range(per_block):
            lat_ref[source, k : k + 1, :] = jnp.sum(sums[k], axis=0, keepdims=True)
    for at in range(0, width, span):
        rows = jnp.concatenate([mine_ref[:, at : at + span], theirs_ref[:, at : at + span]], axis=0)
        term = jnp.dot(acts_ref[...], rows, preferred_element_type=jnp.float32)
        if not first:
            term += refs[0][:, at : at + span]
        total_ref[:, at : at + span] = term.astype(total_ref.dtype)
    bias_ref[...] = jnp.sum(bias_sum[...].T, axis=0, keepdims=True) if last else bias_sum[...]


def input_kernel(pre_ref, mine_ref, theirs_ref, *refs):
    total_ref = refs[-1]
    width = mine_ref.shape[1]
    span = column_span(width)
    for at in range(0, width, span):
        rows = jnp.concatenate([mine_ref[:, at : at + span], theirs_ref[:, at : at + span]], axis=0)
        term = lax.dot_general(rows, pre_ref[...], (((0,), (1,)), ((), ())), preferred_element_type=jnp.float32)
        if len(refs) == 2:
            term += refs[0][at : at + span, :]
        total_ref[at : at + span, :] = term.astype(total_ref.dtype)


def late_input_kernel(pre_ref, mine_ref, theirs_ref, total_ref, out_ref, held_ref, sems):
    width = mine_ref.shape[1]
    span = column_span(width)
    parts = [pl.ds(at, span) for at in range(0, width, span)]
    copies = [pltpu.make_async_copy(total_ref.at[p], held_ref.at[p], sems.at[i]) for i, p in enumerate(parts)]
    for copy in copies:
        copy.start()
    for i, at in enumerate(range(0, width, span)):
        rows = jnp.concatenate([mine_ref[:, at : at + span], theirs_ref[:, at : at + span]], axis=0)
        term = lax.dot_general(rows, pre_ref[...], (((0,), (1,)), ((), ())), preferred_element_type=jnp.float32)
        copies[i].wait()
        out_ref[at : at + span, :] = term + held_ref[at : at + span, :]


def last_input_kernel(pre_ref, mine_ref, theirs_ref, total_ref, out_ref, made_ref, sems):
    width = mine_ref.shape[1]
    span = column_span(width)
    copies = []
    for i, at in enumerate(range(0, width, span)):
        rows = jnp.concatenate([mine_ref[:, at : at + span], theirs_ref[:, at : at + span]], axis=0)
        term = lax.dot_general(rows, pre_ref[...], (((0,), (1,)), ((), ())), preferred_element_type=jnp.float32)
        made_ref[at : at + span, :] = (term + total_ref[at : at + span, :]).astype(made_ref.dtype)
        here = pl.ds(at, span)
        copies.append(pltpu.make_async_copy(made_ref.at[here], out_ref.at[here], sems.at[i]))
        copies[-1].start()
    for copy in copies:
        copy.wait()


def column_span(width):
    return 512 if width % 512 == 0 else BLOCK


def after(value, *others):
    return lax.optimization_barrier((value, *others))[0]


def by_ring(grad_recon, inputs, decoder, owners, local_blocks, offsets, act_values):
    token_count, width = grad_recon.shape
    block_count = owners.shape[1]
    per_block = offsets.shape[2]
    latent_count = decoder.shape[0]
    peer_count = lax.axis_size("lat")
    chips = peer_count // 2
    me = lax.axis_index("lat")
    sources, onward, backward, swap, second, across = ring_tables(peer_count)
    order = jnp.asarray(sources)[me]
    own_t = owners.T
    whole = pl.BlockSpec(memory_space=pltpu.VMEM)
    scalars = pl.BlockSpec(memory_space=pltpu.SMEM)
    step_tokens = 2 * token_count
    light = pl.CostEstimate(flops=1, bytes_accessed=1, transcendentals=0)
    params = pltpu.CompilerParams(vmem_limit_bytes=VMEM_BYTES)

    entries = (own_t, local_blocks.T, offsets.transpose(1, 2, 0), act_values.transpose(1, 2, 0))
    meta = pl.pallas_call(
        meta_kernel,
        in_specs=[pl.BlockSpec(memory_space=pltpu.HBM)] * 4,
        out_specs=whole,
        out_shape=jax.ShapeDtypeStruct((peer_count, 2 * per_block, token_count), jnp.bfloat16),
        scratch_shapes=[pltpu.VMEM(array.shape, array.dtype) for array in entries] + [pltpu.SemaphoreType.DMA((4,))],
        compiler_params=params,
        cost_estimate=light,
        name="meta",
    )(*[pltpu.with_memory_space_constraint(array, pltpu.HBM) for array in entries])
    meta = lax.all_to_all(meta, "lat", split_axis=0, concat_axis=0, tiled=True)

    def near(value):
        return pltpu.with_memory_space_constraint(value, pltpu.VMEM)

    def grad_step(hop, rows, totals, last):
        sums, lanes = (latent_count, width), (latent_count, token_count)
        lat = (2 if last else peer_count, per_block, token_count)
        return pl.pallas_call(
            functools.partial(grad_kernel, per_block),
            in_specs=[scalars] + [whole] * (4 + len(totals)),
            out_specs=[whole] * 4,
            out_shape=[
                jax.ShapeDtypeStruct(sums, jnp.bfloat16) if last else pltpu.VMEM(sums, jnp.float32),
                jax.ShapeDtypeStruct((1, latent_count), jnp.float32) if last else pltpu.VMEM(lanes, jnp.float32),
                jax.ShapeDtypeStruct(lat, jnp.float32),
                pltpu.VMEM((latent_count, step_tokens), jnp.bfloat16),
            ],
            scratch_shapes=[
                pltpu.VMEM((latent_count, step_tokens), jnp.bfloat16),
                pltpu.VMEM(lanes, jnp.float32),
            ],
            input_output_aliases={} if last or not totals else {5: 0, 6: 1},
            compiler_params=params,
            cost_estimate=light,
            name="grad_step",
        )(order[hop], near(meta), near(decoder), near(rows[0]), near(rows[1]), *map(near, totals))

    def input_step(pre, rows, total):
        sums = (width, latent_count)
        totals = () if total is None else (total,)
        return pl.pallas_call(
            input_kernel,
            in_specs=[whole] * (3 + len(totals)),
            out_specs=whole,
            out_shape=pltpu.VMEM(sums, jnp.float32),
            input_output_aliases={3: 0} if totals else {},
            compiler_params=params,
            cost_estimate=light,
            name="input_step",
        )(near(pre), near(rows[0]), near(rows[1]), *map(near, totals))

    def late_input_step(pre, rows, total, last):
        sums, far = (width, latent_count), pl.BlockSpec(memory_space=pltpu.HBM)
        total = near(total) if last else pltpu.with_memory_space_constraint(total, pltpu.HBM)
        return pl.pallas_call(
            last_input_kernel if last else late_input_kernel,
            in_specs=[whole] * 3 + [whole if last else far],
            out_specs=far if last else whole,
            out_shape=jax.ShapeDtypeStruct(sums, jnp.bfloat16) if last else pltpu.VMEM(sums, jnp.float32),
            scratch_shapes=[
                pltpu.VMEM(sums, jnp.bfloat16 if last else jnp.float32),
                pltpu.SemaphoreType.DMA((width // column_span(width),)),
            ],
            compiler_params=params,
            cost_estimate=light,
            name="late_input_step",
        )(near(pre), near(rows[0]), near(rows[1]), total)

    def send(rows, way, *first):
        return lax.ppermute(after(rows, *first) if first else rows, "lat", way)

    turns = [("grads", 1), ("grads", -1)]
    for hop in range(2, chips - 1):
        turns += [("grads", hop), ("inputs", hop - 1)]
    turns += [("inputs", -1), ("inputs", chips - 2)]
    pres, totals, encoder_grad = {}, (), None


    def use(kind, hop, rows, left=len(turns)):
        nonlocal totals, encoder_grad
        if kind == "grads":
            *totals, pres[hop] = grad_step(hop, rows, totals, left == 0)
            return totals[1]
        if left < 2:
            encoder_grad = late_input_step(pres[hop], rows, encoder_grad, left == 0)
        else:
            encoder_grad = input_step(pres[hop], rows, encoder_grad)
        return encoder_grad

    held = {(kind, way): rows for kind, rows in (("grads", grad_recon), ("inputs", inputs)) for way in (True, False)}
    own_grads, own_inputs = send(grad_recon, swap), send(inputs, swap, meta)
    marks = []
    last_grads = max(turn for turn, (kind, _) in enumerate(turns) if kind == "grads")
    returned = None

    def arrive(turn):
        nonlocal returned, totals
        kind, hop = turns[turn]
        left = 0 if turn == last_grads else len(turns) - 1 - turn
        ready = (meta,) if turn < 2 else (marks[turn - 2],)
        if turn == len(turns) - 1:
            ready += (returned,)
        if turn == last_grads:
            returned = lax.all_to_all(totals[2], "lat", split_axis=0, concat_axis=0, tiled=True)
            totals = totals[:2]
        marks.append(use(kind, hop % chips, (arrived[turn], send(arrived[turn], swap, *ready)), left))

    use("grads", 0, (grad_recon, own_grads))
    use("inputs", 0, (inputs, own_inputs))
    arrived = []
    for turn, (kind, hop) in enumerate(turns):
        if turn >= LAG:
            arrive(turn - LAG)
        ready = () if turn < 2 else (meta,) if turn < LAG else (marks[turn - LAG],)
        rows = send(held[kind, hop > 0], onward if hop > 0 else backward, *ready)
        held[kind, hop > 0] = rows
        arrived.append(rows)
    for turn in range(len(turns) - LAG, len(turns)):
        arrive(turn)
    lat = totals[2]
    sent_back = lax.ppermute(lat[0], "lat", second), lax.ppermute(lat[1], "lat", across)
    nearest = jnp.asarray(sources)[me, 2, 0]
    latent_grads = pick_returned(after(returned, encoder_grad), own_t, (nearest, nearest ^ 1), sent_back)
    return (totals[0], encoder_grad, totals[1].reshape(latent_count), latent_grads)


def pick_returned(returned, own_t, more_owners=(), more=()):
    owner_id = jnp.arange(returned.shape[0], dtype=jnp.int32)[:, None, None, None]
    picked = jnp.sum(jnp.where(own_t[None, :, None, :] == owner_id, returned[:, None, :, :], 0.0), axis=0)
    for owner, sent_back in zip(more_owners, more):
        picked += jnp.where(own_t[:, None, :] == owner, sent_back[None], 0.0)
    return picked.reshape(-1, own_t.shape[1]).T


def build_kernel(block_count, per_block, me_ref, meta_ref, acts_ref, cols_ref):
    pairs = block_count * per_block
    meta = meta_ref[0].astype(jnp.float32)
    me = me_ref[0].astype(jnp.float32)
    tokens = meta.shape[1]
    values = jnp.zeros((per_block, tokens), jnp.float32)
    columns = jnp.full((per_block, tokens), -1.0, jnp.float32)
    for i in range(block_count):
        mine = meta[2 * pairs + i : 2 * pairs + i + 1] == me
        values = jnp.where(mine, meta[i * per_block : (i + 1) * per_block], values)
        columns = jnp.where(mine, meta[pairs + i * per_block : pairs + (i + 1) * per_block], columns)
    columns = columns.astype(jnp.int32)
    cols_ref[0] = columns
    row = lax.broadcasted_iota(jnp.int32, (acts_ref.shape[0], tokens), 0)
    dense = jnp.zeros(row.shape, jnp.float32)
    for k in range(per_block):
        dense = jnp.where(row == columns[k : k + 1], values[k : k + 1], dense)
    acts_ref[...] = dense.astype(jnp.bfloat16)


def mask_kernel(per_block, products_ref, cols_ref, pre_ref, lat_ref, bias_ref):
    products = products_ref[...]
    columns = cols_ref[0]
    row = lax.broadcasted_iota(jnp.int32, products.shape, 0)
    kept = jnp.zeros(products.shape, jnp.float32)
    for k in range(per_block):
        picked = jnp.where(row == columns[k : k + 1], products, 0.0)
        lat_ref[0, k : k + 1, :] = jnp.sum(picked, axis=0, keepdims=True)
        kept = kept + picked
    pre_ref[...] = kept.astype(jnp.bfloat16)

    @pl.when(pl.program_id(0) == 0)
    def _():
        bias_ref[...] = jnp.zeros_like(bias_ref)

    bias_ref[...] += kept


def column_parts(width, row_count):
    lanes = width // BLOCK
    for parts in range(2, lanes + 1):
        if lanes % parts == 0 and row_count * (width // parts) * 2 <= PART_BYTES:
            return parts
    return lanes


def by_gather(grad_recon, inputs, decoder, owners, local_blocks, offsets, act_values):
    token_count, width = grad_recon.shape
    block_count = owners.shape[1]
    per_block = offsets.shape[2]
    latent_count = decoder.shape[0]
    peer_count = lax.axis_size("lat")
    pairs = block_count * per_block
    row_count = peer_count * token_count
    me = lax.axis_index("lat").astype(jnp.int32).reshape(1)

    own_t = owners.T
    columns_t = (local_blocks.T[:, None, :] * BLOCK + offsets.transpose(1, 2, 0)).reshape(pairs, token_count)
    acts_t = act_values.transpose(1, 2, 0).reshape(pairs, token_count)
    filler = jnp.zeros((-block_count % 16, token_count), jnp.bfloat16)
    meta = jnp.concatenate([acts_t, columns_t.astype(jnp.bfloat16), own_t.astype(jnp.bfloat16), filler], axis=0)
    meta_all = lax.all_gather(meta, "lat", axis=0)

    parts = column_parts(width, row_count)
    span = width // parts
    depth = max(1, HELD_BYTES // (row_count * span * 2))

    def gathered(rows, p, done):
        piece = rows[:, p * span : (p + 1) * span]
        if len(done) >= depth:
            piece, _ = lax.optimization_barrier((piece, done[-depth]))
        return lax.all_gather(piece, "lat", axis=0, tiled=True)

    tile = pl.BlockSpec((latent_count, token_count), lambda s: (0, s))
    picks = pl.BlockSpec((1, per_block, token_count), lambda s: (s, 0, 0))
    acts_dense, cols = pl.pallas_call(
        functools.partial(build_kernel, block_count, per_block),
        grid=(peer_count,),
        in_specs=[
            pl.BlockSpec(memory_space=pltpu.SMEM),
            pl.BlockSpec((1, meta.shape[0], token_count), lambda s: (s, 0, 0)),
        ],
        out_specs=[tile, picks],
        out_shape=[
            jax.ShapeDtypeStruct((latent_count, row_count), jnp.bfloat16),
            jax.ShapeDtypeStruct((peer_count, per_block, token_count), jnp.int32),
        ],
        name="build",
    )(me, meta_all)

    products = None
    decoder_parts = []
    for p in range(parts):
        rows = gathered(grad_recon, p, decoder_parts)
        part = lax.dot_general(
            acts_dense, rows, (((1,), (0,)), ((), ())), preferred_element_type=jnp.float32
        ).astype(jnp.bfloat16)
        term = lax.dot_general(
            decoder[:, p * span : (p + 1) * span], rows, (((1,), (1,)), ((), ())), preferred_element_type=jnp.float32
        )
        products = term if products is None else products + term
        if depth < 2 * parts:
            part, products = lax.optimization_barrier((part, products))
        decoder_parts.append(part)
    decoder_grad = jnp.concatenate(decoder_parts, axis=1)

    pre_grads, lat, bias_lanes = pl.pallas_call(
        functools.partial(mask_kernel, per_block),
        grid=(peer_count,),
        in_specs=[tile, picks],
        out_specs=[tile, picks, pl.BlockSpec((latent_count, token_count), lambda s: (0, 0))],
        out_shape=[
            jax.ShapeDtypeStruct((latent_count, row_count), jnp.bfloat16),
            jax.ShapeDtypeStruct((peer_count, per_block, token_count), jnp.float32),
            jax.ShapeDtypeStruct((latent_count, token_count), jnp.float32),
        ],
        name="mask",
    )(products, cols)
    bias_grad = jnp.sum(bias_lanes, axis=1)
    returned = lax.all_to_all(lat, "lat", split_axis=0, concat_axis=0, tiled=True)
    latent_grads = pick_returned(returned, own_t)

    encoder_parts = []
    for p in range(parts):
        rows = gathered(inputs, p, decoder_parts + encoder_parts)
        encoder_parts.append(
            lax.dot_general(rows, pre_grads, (((0,), (1,)), ((), ())), preferred_element_type=jnp.float32).astype(
                jnp.bfloat16
            )
        )
    return (decoder_grad, jnp.concatenate(encoder_parts, axis=0), bias_grad, latent_grads)


def per_device(grad_recon, *others):
    row_bytes = lax.axis_size("lat") * grad_recon.size * grad_recon.dtype.itemsize
    way = by_ring if 2 * row_bytes <= RING_BYTES and lax.axis_size("lat") % 4 == 0 else by_gather
    return way(grad_recon, *others)


def solution(mesh):
    rows = P(("groups", "lat"), None)
    entries = P(("groups", "lat"), None, None)
    return jax.shard_map(
        per_device,
        mesh=mesh,
        in_specs=(rows, rows, P("lat", None), rows, rows, entries, entries),
        out_specs=(rows, P(None, ("groups", "lat")), P(("groups", "lat")), rows),
        check_vma=False,
    )
```

```python
import functools

import jax
import jax.numpy as jnp
import numpy as np
from jax import lax
from jax.experimental import pallas as pl
from jax.experimental.pallas import tpu as pltpu
from jax.sharding import PartitionSpec as P

BLOCK = 128
PART_BYTES = 9 << 20
HELD_BYTES = 1 << 25
RING_BYTES = 1 << 26
VMEM_BYTES = 24 << 20
LAG = 4


def ring_tables(peer_count):
    chips = peer_count // 2
    ring = [chip for chip in range(chips) if chip % 2 == 0] + [chip for chip in reversed(range(chips)) if chip % 2]
    place = {chip: spot for spot, chip in enumerate(ring)}
    sources = np.zeros((peer_count, chips, 2), np.int32)
    for device in range(peer_count):
        chip, core = divmod(device, 2)
        sign = 1 - 2 * core
        for hop in range(chips):
            behind, ahead = ring[(place[chip] - sign * hop) % chips], ring[(place[chip] + sign * hop) % chips]
            sources[device, hop] = (2 * behind + core, 2 * ahead + 1 - core)
    onward = [(2 * ring[i], 2 * ring[(i + 1) % chips]) for i in range(chips)]
    onward += [(2 * ring[i] + 1, 2 * ring[(i - 1) % chips] + 1) for i in range(chips)]
    swap = [(i, i ^ 1) for i in range(peer_count)]
    backward = [(b, a) for a, b in onward]
    return sources, onward, backward, swap


def meta_kernel(*refs):
    sources, meta_ref, held, sems = refs[:4], refs[4], refs[5:9], refs[9]
    copies = [pltpu.make_async_copy(source, kept, sems.at[i]) for i, (source, kept) in enumerate(zip(sources, held))]
    for copy in copies:
        copy.start()
    for copy in copies:
        copy.wait()
    owners_ref, blocks_ref, offsets_ref, values_ref = held
    count, per_block, tokens = offsets_ref.shape
    columns = [
        (jnp.broadcast_to(blocks_ref[i : i + 1, :], (per_block, tokens)) * BLOCK + offsets_ref[i]).astype(jnp.float32)
        for i in range(count)
    ]
    values = [values_ref[i].astype(jnp.float32) for i in range(count)]
    named = [jnp.broadcast_to(owners_ref[i : i + 1, :], (per_block, tokens)) for i in range(count)]
    for owner in range(meta_ref.shape[0]):
        told_columns = jnp.full((per_block, tokens), -1.0, jnp.float32)
        told_values = jnp.zeros((per_block, tokens), jnp.float32)
        for i in range(count):
            mine = named[i] == owner
            told_columns = jnp.where(mine, columns[i], told_columns)
            told_values = jnp.where(mine, values[i], told_values)
        meta_ref[owner, :per_block, :] = told_columns.astype(jnp.bfloat16)
        meta_ref[owner, per_block:, :] = told_values.astype(jnp.bfloat16)


def grad_kernel(per_block, order_ref, meta_ref, decoder_ref, mine_ref, theirs_ref, *refs):
    total_ref, bias_ref, lat_ref, pre_ref, acts_ref, bias_sum = refs[-6:]
    first, last = len(refs) == 6, bias_ref.shape[0] == 1
    bias_sum[...] = jnp.zeros_like(bias_sum) if first else refs[1][...]
    lat_ref[...] = jnp.zeros_like(lat_ref) if first else refs[2][...]
    latents, width = decoder_ref.shape
    tokens = mine_ref.shape[0]
    span = column_span(width)
    products = jnp.zeros((latents, 2 * tokens), jnp.float32)
    for at in range(0, width, span):
        rows = jnp.concatenate([mine_ref[:, at : at + span], theirs_ref[:, at : at + span]], axis=0)
        products += lax.dot_general(
            decoder_ref[:, at : at + span], rows, (((1,), (1,)), ((), ())), preferred_element_type=jnp.float32
        )
    row = lax.broadcasted_iota(jnp.int32, (8, tokens), 0)
    for tile in range(2):
        meta = meta_ref[order_ref[tile]].astype(jnp.float32)
        columns = [jnp.broadcast_to(meta[k : k + 1], (8, tokens)).astype(jnp.int32) for k in range(per_block)]
        values = [jnp.broadcast_to(meta[per_block + k : per_block + k + 1], (8, tokens)) for k in range(per_block)]
        sums = [jnp.zeros((8, tokens), jnp.float32) for _ in range(per_block)]
        at = slice(tile * tokens, (tile + 1) * tokens)
        for block in range(0, latents, 16):
            kept_both, dense_both = [], []
            for base in (block, block + 8):
                here = products[base : base + 8, at]
                kept = jnp.zeros((8, tokens), jnp.float32)
                dense = jnp.zeros((8, tokens), jnp.float32)
                for k in range(per_block):
                    hit = columns[k] == row + base
                    picked = jnp.where(hit, here, 0.0)
                    sums[k] = sums[k] + picked
                    kept = kept + picked
                    dense = jnp.where(hit, values[k], dense)
                bias_sum[base : base + 8, :] += kept
                kept_both.append(kept)
                dense_both.append(dense)
            pre_ref[block : block + 16, at] = jnp.concatenate(kept_both, axis=0).astype(jnp.bfloat16)
            acts_ref[block : block + 16, at] = jnp.concatenate(dense_both, axis=0).astype(jnp.bfloat16)
        source = order_ref[tile]
        for k in range(per_block):
            lat_ref[source, k : k + 1, :] = jnp.sum(sums[k], axis=0, keepdims=True)
    for at in range(0, width, span):
        rows = jnp.concatenate([mine_ref[:, at : at + span], theirs_ref[:, at : at + span]], axis=0)
        term = jnp.dot(acts_ref[...], rows, preferred_element_type=jnp.float32)
        if not first:
            term += refs[0][:, at : at + span]
        total_ref[:, at : at + span] = term.astype(total_ref.dtype)
    bias_ref[...] = jnp.sum(bias_sum[...].T, axis=0, keepdims=True) if last else bias_sum[...]


def input_kernel(pre_ref, mine_ref, theirs_ref, *refs):
    total_ref = refs[-1]
    width = mine_ref.shape[1]
    span = column_span(width)
    for at in range(0, width, span):
        rows = jnp.concatenate([mine_ref[:, at : at + span], theirs_ref[:, at : at + span]], axis=0)
        term = lax.dot_general(rows, pre_ref[...], (((0,), (1,)), ((), ())), preferred_element_type=jnp.float32)
        if len(refs) == 2:
            term += refs[0][at : at + span, :]
        total_ref[at : at + span, :] = term.astype(total_ref.dtype)


def late_input_kernel(pre_ref, mine_ref, theirs_ref, total_ref, out_ref, held_ref, sems):
    width = mine_ref.shape[1]
    span = column_span(width)
    parts = [pl.ds(at, span) for at in range(0, width, span)]
    copies = [pltpu.make_async_copy(total_ref.at[p], held_ref.at[p], sems.at[i]) for i, p in enumerate(parts)]
    for copy in copies:
        copy.start()
    for i, at in enumerate(range(0, width, span)):
        rows = jnp.concatenate([mine_ref[:, at : at + span], theirs_ref[:, at : at + span]], axis=0)
        term = lax.dot_general(rows, pre_ref[...], (((0,), (1,)), ((), ())), preferred_element_type=jnp.float32)
        copies[i].wait()
        out_ref[at : at + span, :] = term + held_ref[at : at + span, :]


def last_input_kernel(pre_ref, mine_ref, theirs_ref, total_ref, out_ref, made_ref, sems):
    width = mine_ref.shape[1]
    span = column_span(width)
    copies = []
    for i, at in enumerate(range(0, width, span)):
        rows = jnp.concatenate([mine_ref[:, at : at + span], theirs_ref[:, at : at + span]], axis=0)
        term = lax.dot_general(rows, pre_ref[...], (((0,), (1,)), ((), ())), preferred_element_type=jnp.float32)
        made_ref[at : at + span, :] = (term + total_ref[at : at + span, :]).astype(made_ref.dtype)
        here = pl.ds(at, span)
        copies.append(pltpu.make_async_copy(made_ref.at[here], out_ref.at[here], sems.at[i]))
        copies[-1].start()
    for copy in copies:
        copy.wait()


def column_span(width):
    return 512 if width % 512 == 0 else BLOCK


def after(value, *others):
    return lax.optimization_barrier((value, *others))[0]


def by_ring(grad_recon, inputs, decoder, owners, local_blocks, offsets, act_values):
    token_count, width = grad_recon.shape
    block_count = owners.shape[1]
    per_block = offsets.shape[2]
    latent_count = decoder.shape[0]
    peer_count = lax.axis_size("lat")
    chips = peer_count // 2
    me = lax.axis_index("lat")
    sources, onward, backward, swap = ring_tables(peer_count)
    order = jnp.asarray(sources)[me]
    own_t = owners.T
    whole = pl.BlockSpec(memory_space=pltpu.VMEM)
    scalars = pl.BlockSpec(memory_space=pltpu.SMEM)
    step_tokens = 2 * token_count
    light = pl.CostEstimate(flops=1, bytes_accessed=1, transcendentals=0)
    params = pltpu.CompilerParams(vmem_limit_bytes=VMEM_BYTES)

    entries = (own_t, local_blocks.T, offsets.transpose(1, 2, 0), act_values.transpose(1, 2, 0))
    meta = pl.pallas_call(
        meta_kernel,
        in_specs=[pl.BlockSpec(memory_space=pltpu.HBM)] * 4,
        out_specs=whole,
        out_shape=jax.ShapeDtypeStruct((peer_count, 2 * per_block, token_count), jnp.bfloat16),
        scratch_shapes=[pltpu.VMEM(array.shape, array.dtype) for array in entries] + [pltpu.SemaphoreType.DMA((4,))],
        compiler_params=params,
        cost_estimate=light,
        name="meta",
    )(*[pltpu.with_memory_space_constraint(array, pltpu.HBM) for array in entries])
    meta = lax.all_to_all(meta, "lat", split_axis=0, concat_axis=0, tiled=True)

    def near(value):
        return pltpu.with_memory_space_constraint(value, pltpu.VMEM)

    def grad_step(hop, rows, totals, last):
        sums, lanes = (latent_count, width), (latent_count, token_count)
        return pl.pallas_call(
            functools.partial(grad_kernel, per_block),
            in_specs=[scalars] + [whole] * (4 + len(totals)),
            out_specs=[whole] * 4,
            out_shape=[
                jax.ShapeDtypeStruct(sums, jnp.bfloat16) if last else pltpu.VMEM(sums, jnp.float32),
                jax.ShapeDtypeStruct((1, latent_count), jnp.float32) if last else pltpu.VMEM(lanes, jnp.float32),
                jax.ShapeDtypeStruct((peer_count, per_block, token_count), jnp.float32),
                pltpu.VMEM((latent_count, step_tokens), jnp.bfloat16),
            ],
            scratch_shapes=[
                pltpu.VMEM((latent_count, step_tokens), jnp.bfloat16),
                pltpu.VMEM(lanes, jnp.float32),
            ],
            input_output_aliases={} if last or not totals else {5: 0, 6: 1},
            compiler_params=params,
            cost_estimate=light,
            name="grad_step",
        )(order[hop], near(meta), near(decoder), near(rows[0]), near(rows[1]), *map(near, totals))

    def input_step(pre, rows, total):
        sums = (width, latent_count)
        totals = () if total is None else (total,)
        return pl.pallas_call(
            input_kernel,
            in_specs=[whole] * (3 + len(totals)),
            out_specs=whole,
            out_shape=pltpu.VMEM(sums, jnp.float32),
            input_output_aliases={3: 0} if totals else {},
            compiler_params=params,
            cost_estimate=light,
            name="input_step",
        )(near(pre), near(rows[0]), near(rows[1]), *map(near, totals))

    def late_input_step(pre, rows, total, last):
        sums, far = (width, latent_count), pl.BlockSpec(memory_space=pltpu.HBM)
        total = near(total) if last else pltpu.with_memory_space_constraint(total, pltpu.HBM)
        return pl.pallas_call(
            last_input_kernel if last else late_input_kernel,
            in_specs=[whole] * 3 + [whole if last else far],
            out_specs=far if last else whole,
            out_shape=jax.ShapeDtypeStruct(sums, jnp.bfloat16) if last else pltpu.VMEM(sums, jnp.float32),
            scratch_shapes=[
                pltpu.VMEM(sums, jnp.bfloat16 if last else jnp.float32),
                pltpu.SemaphoreType.DMA((width // column_span(width),)),
            ],
            compiler_params=params,
            cost_estimate=light,
            name="late_input_step",
        )(near(pre), near(rows[0]), near(rows[1]), total)

    def send(rows, way, *first):
        return lax.ppermute(after(rows, *first) if first else rows, "lat", way)

    half = chips // 2
    later = [("inputs", 1)]
    for hop in range(1, half):
        later += [("inputs", hop + 1), ("inputs", -hop)]
    turns = []
    for hop in range(1, half + 1):
        turns += [("grads", hop)] + ([("grads", -hop)] if hop < half else []) + [later.pop(0)]
    turns += later
    pres, totals, encoder_grad = {}, (), None


    def use(kind, hop, rows, left=len(turns)):
        nonlocal totals, encoder_grad
        if kind == "grads":
            *totals, pres[hop] = grad_step(hop, rows, totals, left == 0)
            return totals[1]
        if left < 2:
            encoder_grad = late_input_step(pres[hop], rows, encoder_grad, left == 0)
        else:
            encoder_grad = input_step(pres[hop], rows, encoder_grad)
        return encoder_grad

    held = {(kind, way): rows for kind, rows in (("grads", grad_recon), ("inputs", inputs)) for way in (True, False)}
    own_grads, own_inputs = send(grad_recon, swap), send(inputs, swap, meta)
    marks = []
    last_grads = max(turn for turn, (kind, _) in enumerate(turns) if kind == "grads")
    returned = None

    def arrive(turn):
        nonlocal returned
        kind, hop = turns[turn]
        left = 0 if turn == last_grads else len(turns) - 1 - turn
        ready = (meta,) if turn < 2 else (marks[turn - 2],)
        if turn == len(turns) - 1:
            ready += (returned,)
        marks.append(use(kind, hop % chips, (arrived[turn], send(arrived[turn], swap, *ready)), left))
        if turn == last_grads:
            returned = lax.all_to_all(totals[2], "lat", split_axis=0, concat_axis=0, tiled=True)

    use("grads", 0, (grad_recon, own_grads))
    use("inputs", 0, (inputs, own_inputs))
    arrived = []
    for turn, (kind, hop) in enumerate(turns):
        if turn >= LAG:
            arrive(turn - LAG)
        ready = () if turn < 3 else (meta,) if turn < LAG else (marks[turn - LAG],)
        rows = send(held[kind, hop > 0], onward if hop > 0 else backward, *ready)
        held[kind, hop > 0] = rows
        arrived.append(rows)
    for turn in range(len(turns) - LAG, len(turns)):
        arrive(turn)
    latent_grads = pick_returned(after(returned, encoder_grad), own_t)
    return (totals[0], encoder_grad, totals[1].reshape(latent_count), latent_grads)


def pick_returned(returned, own_t):
    owner_id = jnp.arange(returned.shape[0], dtype=jnp.int32)[:, None, None, None]
    picked = jnp.where(own_t[None, :, None, :] == owner_id, returned[:, None, :, :], 0.0)
    return jnp.sum(picked, axis=0).reshape(-1, own_t.shape[1]).T


def build_kernel(block_count, per_block, me_ref, meta_ref, acts_ref, cols_ref):
    pairs = block_count * per_block
    meta = meta_ref[0].astype(jnp.float32)
    me = me_ref[0].astype(jnp.float32)
    tokens = meta.shape[1]
    values = jnp.zeros((per_block, tokens), jnp.float32)
    columns = jnp.full((per_block, tokens), -1.0, jnp.float32)
    for i in range(block_count):
        mine = meta[2 * pairs + i : 2 * pairs + i + 1] == me
        values = jnp.where(mine, meta[i * per_block : (i + 1) * per_block], values)
        columns = jnp.where(mine, meta[pairs + i * per_block : pairs + (i + 1) * per_block], columns)
    columns = columns.astype(jnp.int32)
    cols_ref[0] = columns
    row = lax.broadcasted_iota(jnp.int32, (acts_ref.shape[0], tokens), 0)
    dense = jnp.zeros(row.shape, jnp.float32)
    for k in range(per_block):
        dense = jnp.where(row == columns[k : k + 1], values[k : k + 1], dense)
    acts_ref[...] = dense.astype(jnp.bfloat16)


def mask_kernel(per_block, products_ref, cols_ref, pre_ref, lat_ref, bias_ref):
    products = products_ref[...]
    columns = cols_ref[0]
    row = lax.broadcasted_iota(jnp.int32, products.shape, 0)
    kept = jnp.zeros(products.shape, jnp.float32)
    for k in range(per_block):
        picked = jnp.where(row == columns[k : k + 1], products, 0.0)
        lat_ref[0, k : k + 1, :] = jnp.sum(picked, axis=0, keepdims=True)
        kept = kept + picked
    pre_ref[...] = kept.astype(jnp.bfloat16)

    @pl.when(pl.program_id(0) == 0)
    def _():
        bias_ref[...] = jnp.zeros_like(bias_ref)

    bias_ref[...] += kept


def column_parts(width, row_count):
    lanes = width // BLOCK
    for parts in range(2, lanes + 1):
        if lanes % parts == 0 and row_count * (width // parts) * 2 <= PART_BYTES:
            return parts
    return lanes


def by_gather(grad_recon, inputs, decoder, owners, local_blocks, offsets, act_values):
    token_count, width = grad_recon.shape
    block_count = owners.shape[1]
    per_block = offsets.shape[2]
    latent_count = decoder.shape[0]
    peer_count = lax.axis_size("lat")
    pairs = block_count * per_block
    row_count = peer_count * token_count
    me = lax.axis_index("lat").astype(jnp.int32).reshape(1)

    own_t = owners.T
    columns_t = (local_blocks.T[:, None, :] * BLOCK + offsets.transpose(1, 2, 0)).reshape(pairs, token_count)
    acts_t = act_values.transpose(1, 2, 0).reshape(pairs, token_count)
    filler = jnp.zeros((-block_count % 16, token_count), jnp.bfloat16)
    meta = jnp.concatenate([acts_t, columns_t.astype(jnp.bfloat16), own_t.astype(jnp.bfloat16), filler], axis=0)
    meta_all = lax.all_gather(meta, "lat", axis=0)

    parts = column_parts(width, row_count)
    span = width // parts
    depth = max(1, HELD_BYTES // (row_count * span * 2))

    def gathered(rows, p, done):
        piece = rows[:, p * span : (p + 1) * span]
        if len(done) >= depth:
            piece, _ = lax.optimization_barrier((piece, done[-depth]))
        return lax.all_gather(piece, "lat", axis=0, tiled=True)

    tile = pl.BlockSpec((latent_count, token_count), lambda s: (0, s))
    picks = pl.BlockSpec((1, per_block, token_count), lambda s: (s, 0, 0))
    acts_dense, cols = pl.pallas_call(
        functools.partial(build_kernel, block_count, per_block),
        grid=(peer_count,),
        in_specs=[
            pl.BlockSpec(memory_space=pltpu.SMEM),
            pl.BlockSpec((1, meta.shape[0], token_count), lambda s: (s, 0, 0)),
        ],
        out_specs=[tile, picks],
        out_shape=[
            jax.ShapeDtypeStruct((latent_count, row_count), jnp.bfloat16),
            jax.ShapeDtypeStruct((peer_count, per_block, token_count), jnp.int32),
        ],
        name="build",
    )(me, meta_all)

    products = None
    decoder_parts = []
    for p in range(parts):
        rows = gathered(grad_recon, p, decoder_parts)
        part = lax.dot_general(
            acts_dense, rows, (((1,), (0,)), ((), ())), preferred_element_type=jnp.float32
        ).astype(jnp.bfloat16)
        term = lax.dot_general(
            decoder[:, p * span : (p + 1) * span], rows, (((1,), (1,)), ((), ())), preferred_element_type=jnp.float32
        )
        products = term if products is None else products + term
        if depth < 2 * parts:
            part, products = lax.optimization_barrier((part, products))
        decoder_parts.append(part)
    decoder_grad = jnp.concatenate(decoder_parts, axis=1)

    pre_grads, lat, bias_lanes = pl.pallas_call(
        functools.partial(mask_kernel, per_block),
        grid=(peer_count,),
        in_specs=[tile, picks],
        out_specs=[tile, picks, pl.BlockSpec((latent_count, token_count), lambda s: (0, 0))],
        out_shape=[
            jax.ShapeDtypeStruct((latent_count, row_count), jnp.bfloat16),
            jax.ShapeDtypeStruct((peer_count, per_block, token_count), jnp.float32),
            jax.ShapeDtypeStruct((latent_count, token_count), jnp.float32),
        ],
        name="mask",
    )(products, cols)
    bias_grad = jnp.sum(bias_lanes, axis=1)
    returned = lax.all_to_all(lat, "lat", split_axis=0, concat_axis=0, tiled=True)
    latent_grads = pick_returned(returned, own_t)

    encoder_parts = []
    for p in range(parts):
        rows = gathered(inputs, p, decoder_parts + encoder_parts)
        encoder_parts.append(
            lax.dot_general(rows, pre_grads, (((0,), (1,)), ((), ())), preferred_element_type=jnp.float32).astype(
                jnp.bfloat16
            )
        )
    return (decoder_grad, jnp.concatenate(encoder_parts, axis=0), bias_grad, latent_grads)


def per_device(grad_recon, *others):
    row_bytes = lax.axis_size("lat") * grad_recon.size * grad_recon.dtype.itemsize
    way = by_ring if 2 * row_bytes <= RING_BYTES and lax.axis_size("lat") % 4 == 0 else by_gather
    return way(grad_recon, *others)


def solution(mesh):
    rows = P(("groups", "lat"), None)
    entries = P(("groups", "lat"), None, None)
    return jax.shard_map(
        per_device,
        mesh=mesh,
        in_specs=(rows, rows, P("lat", None), rows, rows, entries, entries),
        out_specs=(rows, P(None, ("groups", "lat")), P(("groups", "lat")), rows),
        check_vma=False,
    )
```
